32 devices in a mesh: dp: 8 (over y, x, core), tensor: 4 (over z).
Axes of the slice: x: 2, y: 2, z: 4, core: 2. Of those that a mesh axis runs over, the one named last changes fastest.
Arguments:
- frames_in: bfloat16 [8, 1024, 1536], P('dp', 'tensor'), may hold values from -6 to 6
- text_states: bfloat16 [8, 64, 1536], P('dp'), may hold values from -6 to 6
- ln_gain: bfloat16 [2, 3, 1536], P(None, None, 'dp'), may hold values from 0.5 to 1.5
- ln_bias: bfloat16 [2, 3, 1536], P(None, None, 'dp'), may hold values from -2 to 2
- w_self: bfloat16 [2, 1536, 3, 1536], P(None, 'dp', None, 'tensor'), may hold values from -0.15625 to 0.15625
- w_self_out: bfloat16 [2, 1536, 1536], P(None, 'tensor', 'dp'), may hold values from -0.625 to 0.625
- w_cross_q: bfloat16 [2, 1536, 1536], P(None, 'dp', 'tensor'), may hold values from -0.15625 to 0.15625
- w_cross_kv: bfloat16 [2, 1536, 2, 1536], P(None, 'dp', None, 'tensor'), may hold values from -0.15625 to 0.15625
- w_cross_out: bfloat16 [2, 1536, 1536], P(None, 'tensor', 'dp'), may hold values from -0.3125 to 0.3125
- w_up: bfloat16 [2, 1536, 6144], P(None, 'dp', 'tensor'), may hold values from -0.15625 to 0.15625
- w_down: bfloat16 [2, 6144, 1536], P(None, 'tensor', 'dp'), may hold values from -0.109375 to 0.109375
- cotangent: bfloat16 [8, 1024, 1536], P('dp', 'tensor'), may hold values from -8 to 8
Outputs:
- result: bfloat16 [8, 1024, 1536], P('dp', 'tensor')
- grad_frames: float32 [8, 1024, 1536], P('dp', 'tensor')
- grad_text: float32 [8, 64, 1536], P('dp')
- grad_ln_gain: float32 [2, 3, 1536], P(None, None, 'dp')
- grad_ln_bias: float32 [2, 3, 1536], P(None, None, 'dp')
- grad_w_self: float32 [2, 1536, 3, 1536], P(None, 'dp', None, 'tensor')
- grad_w_self_out: float32 [2, 1536, 1536], P(None, 'tensor', 'dp')
- grad_w_cross_q: float32 [2, 1536, 1536], P(None, 'dp', 'tensor')
- grad_w_cross_kv: float32 [2, 1536, 2, 1536], P(None, 'dp', None, 'tensor')
- grad_w_cross_out: float32 [2, 1536, 1536], P(None, 'tensor', 'dp')
- grad_w_up: float32 [2, 1536, 6144], P(None, 'dp', 'tensor')
- grad_w_down: float32 [2, 6144, 1536], P(None, 'tensor', 'dp')
The draws below stay inside these ranges and needn't reach their ends.
All inputs are finite; a program needn't handle non-finite values.
Results may differ from the reference program's by a relative error of at most 0.03.
Values may be sent and summed in bfloat16 or wider, within the bound.
A program may use at most 320 MiB of HBM per device.

```python
from functools import partial
import jax
import jax.numpy as jnp
from jax import lax

D = 1536
HEADS = 24
HEAD_DIM = 64
FF = 6144
FRAMES = 1024
ATT_BLOCK = 512
TEXT = 64
LAYERS = 2
CLIPS_ALL = 8


def spiked(values, own_key, source, target, blocks, factor):
    owner, partner = [(jnp.arange(values.shape[position]) // (values.shape[position] // blocks)).reshape([-1 if axis == position else 1 for axis in range(values.ndim)]) for position in (source, target)]
    chosen = jax.random.permutation(own_key, blocks)[partner]
    strong = (owner == chosen) | (owner == (partner + blocks // 2) % blocks)
    return jnp.where(strong, factor * values, values)


def steps_of(stream_key, dims, cuts, least, high):
    loudness, own = 1.0, jax.random.fold_in(stream_key, 6)
    for position, parts in cuts:
        heights = jnp.exp(jax.random.uniform(jax.random.fold_in(own, position), (parts,), jnp.float32, least / len(cuts), high / len(cuts)))
        loudness = loudness * jnp.repeat(heights, dims[position] // parts).reshape([-1 if axis == position else 1 for axis in range(len(dims))])
    return loudness


def scatter_about(stream_key, dims, scale, limit, cuts=(), dtype=jnp.bfloat16):
    factor_of = steps_of(stream_key, dims, cuts, -0.22, 0.18) if cuts else 1.0
    result = jax.random.normal(stream_key, dims, jnp.float32) * scale * factor_of
    return jnp.minimum(jnp.maximum(result, -limit), limit).astype(dtype)


def heavy_noise(rng, dims, width, bound, shards, heavy, dtype=jnp.bfloat16):
    array = width * jax.random.normal(rng, dims, jnp.float32)
    if shards:
        array = array * steps_of(rng, dims, shards, -0.22, 0.18)
    return jnp.clip(spiked(array, jax.random.fold_in(rng, 3), *heavy), -bound, bound).astype(dtype)


def setup_inputs(seed: int = 0) -> dict:
    streams_of = jax.random.split(jax.random.key(seed), 13)
    frames_in = scatter_about(streams_of[0], (CLIPS_ALL, FRAMES, D), 1.0, 6.0, ((0, 8), (1, 4)))
    text_states = scatter_about(streams_of[1], (CLIPS_ALL, TEXT, D), 1.0, 6.0, ((0, 8),))
    ln_gain = jnp.clip(1.0 + 0.1 * jax.random.normal(streams_of[2], (LAYERS, 3, D), jnp.float32), 0.5, 1.5).astype(jnp.bfloat16)
    ln_bias = scatter_about(streams_of[3], (LAYERS, 3, D), 0.3, 2.0, ((2, 8),))
    w_self = scatter_about(streams_of[4], (LAYERS, D, 3, D), D ** -0.5, 0.15625, ((1, 8), (3, 4)))
    w_self_out = scatter_about(streams_of[5], (LAYERS, D, D), (D // 16) ** -0.5, 0.625, ((1, 4), (2, 8)))
    w_cross_q = scatter_about(streams_of[6], (LAYERS, D, D), D ** -0.5, 0.15625, ((1, 8), (2, 4)))
    w_cross_kv = scatter_about(streams_of[7], (LAYERS, D, 2, D), D ** -0.5, 0.15625, ((1, 8), (3, 4)))
    w_cross_out = scatter_about(streams_of[8], (LAYERS, D, D), (D // 4) ** -0.5, 0.3125, ((1, 4), (2, 8)))
    w_up = scatter_about(streams_of[9], (LAYERS, D, FF), D ** -0.5, 0.15625, ((1, 8), (2, 4)))
    w_down = scatter_about(streams_of[10], (LAYERS, FF, D), (FF // 2) ** -0.5, 0.109375, ((1, 4), (2, 8)))
    cotangent = heavy_noise(streams_of[11], (CLIPS_ALL, FRAMES, D), 1.0, 8.0, ((0, 8), (1, 4)), (0, 2, 8, 2.0))
    return dict(frames_in=frames_in, text_states=text_states, ln_gain=ln_gain, ln_bias=ln_bias, w_self=w_self, w_self_out=w_self_out, w_cross_q=w_cross_q, w_cross_kv=w_cross_kv, w_cross_out=w_cross_out, w_up=w_up, w_down=w_down, cotangent=cotangent)


@jax.custom_vjp
def low(v):
    return lax.optimization_barrier(v.astype(jnp.bfloat16)).astype(jnp.float32)

@jax.custom_vjp
def low_back(v):
    return v

def low_keep(v):
    return (low(v), None)

def low_pass(kept, grad):
    return (grad,)

def back_keep(v):
    return (v, None)

def back_low(kept, grad):
    return (low(grad),)
low.defvjp(low_keep, low_pass)
low_back.defvjp(back_keep, back_low)
highest = lax.Precision.HIGHEST
norm_eps = 1e-05
masked_score = -1e+30

def layer_norm(stream, gain, shift):
    centre = lax.optimization_barrier(jnp.mean(stream, axis=-1, keepdims=True))
    centred = stream - centre
    spread = lax.optimization_barrier(jnp.mean(centred * centred, axis=-1, keepdims=True))
    return centred * lax.rsqrt(spread + norm_eps) * gain + shift

def causal_mask(scores, offset):
    rows = offset + lax.broadcasted_iota(jnp.int32, scores.shape[-2:], 0)
    cols = lax.broadcasted_iota(jnp.int32, scores.shape[-2:], 1)
    return jnp.where(rows >= cols, scores, masked_score)

def attend_block(query, keys, values, offset, causal):
    scores = low_back(jnp.einsum('qhd,khd->hqk', query, keys, precision=highest) * HEAD_DIM ** (-0.5))
    if causal:
        scores = causal_mask(scores, offset)
    top = lax.optimization_barrier(jnp.max(scores, axis=-1, keepdims=True))
    expo = jnp.exp(scores - top)
    probs = expo / lax.optimization_barrier(jnp.sum(expo, axis=-1, keepdims=True))
    return jnp.einsum('hqk,khd->qhd', low(probs), values, precision=highest)

def attention_rows(query, keys, values, causal):
    frames = query.shape[0]
    pieces = []
    for block_index in range(frames // ATT_BLOCK):
        start = block_index * ATT_BLOCK
        stop = start + ATT_BLOCK
        reach = stop if causal else keys.shape[0]
        block_fn = jax.checkpoint(partial(attend_block, offset=start, causal=causal))
        pieces.append(block_fn(query[start:stop], keys[:reach], values[:reach]))
    return jnp.concatenate(pieces, axis=0)

def layer_forward(stream, text_rows, gains, shifts, w_self, w_self_out, w_cross_q, w_cross_kv, w_cross_out, w_up, w_down):
    frames = stream.shape[0]
    normed = low(layer_norm(stream, gains[0], shifts[0]))
    proj = low_back(low(jnp.einsum('fd,dke->fke', normed, w_self, precision=highest)))
    split = proj.reshape(frames, 3, HEADS, HEAD_DIM)
    mixed = attention_rows(split[:, 0], split[:, 1], split[:, 2], True)
    joined = low_back(low(mixed.reshape(frames, D)))
    stream = stream + low_back(jnp.dot(joined, w_self_out, precision=highest))
    normed = low(layer_norm(stream, gains[1], shifts[1]))
    cross_query = low_back(low(jnp.dot(normed, w_cross_q, precision=highest))).reshape(frames, HEADS, HEAD_DIM)
    pairs = low_back(low(jnp.einsum('td,dke->tke', text_rows, w_cross_kv, precision=highest)))
    pairs = pairs.reshape(text_rows.shape[0], 2, HEADS, HEAD_DIM)
    mixed = attention_rows(cross_query, pairs[:, 0], pairs[:, 1], False)
    joined = low_back(low(mixed.reshape(frames, D)))
    stream = stream + low_back(jnp.dot(joined, w_cross_out, precision=highest))
    normed = low(layer_norm(stream, gains[2], shifts[2]))
    upper = low_back(jnp.dot(normed, w_up, precision=highest))
    active = low(jax.nn.gelu(upper, approximate=False))
    return stream + low_back(jnp.dot(active, w_down, precision=highest))

def stack_forward(stream, text_rows, weights):
    for layer_index in range(LAYERS):
        stream = layer_forward(stream, text_rows, *[member[layer_index] for member in weights])
    return stream

def reference(frames_in, text_states, ln_gain, ln_bias, w_self, w_self_out, w_cross_q, w_cross_kv, w_cross_out, w_up, w_down, cotangent):
    weights = tuple((member.astype(jnp.float32) for member in (ln_gain, ln_bias, w_self, w_self_out, w_cross_q, w_cross_kv, w_cross_out, w_up, w_down)))

    def one_clip(totals, item):
        clip_rows, text_rows, cot_rows = item
        output, pullback = jax.vjp(stack_forward, clip_rows.astype(jnp.float32), text_rows.astype(jnp.float32), weights)
        grad_clip, grad_text_rows, grad_weights = pullback(cot_rows.astype(jnp.float32))
        totals = jax.tree.map(jnp.add, totals, grad_weights)
        return (totals, (output.astype(jnp.bfloat16), grad_clip, grad_text_rows))
    zeros = jax.tree.map(jnp.zeros_like, weights)
    totals, (outputs, grad_frames, grad_text) = lax.scan(one_clip, zeros, (frames_in, text_states, cotangent))
    return (outputs, grad_frames, grad_text, totals[0], totals[1], totals[2], totals[3], totals[4], totals[5], totals[6], totals[7], totals[8])
```

```python
import functools
import jax
import jax.numpy as jnp
from jax import lax
from jax.sharding import Mesh, PartitionSpec as P

HEAD_DIM = 64
ATT_BLOCK = 512
NORM_EPS = 1e-05
MASKED = -1e30
F32 = jnp.float32
BF16 = jnp.bfloat16


def nn(a, b):
    return lax.dot_general(a, b, (((1,), (0,)), ((), ())), preferred_element_type=F32)


def nt(a, b):
    return lax.dot_general(a, b, (((1,), (1,)), ((), ())), preferred_element_type=F32)


def tn(a, b):
    return lax.dot_general(a, b, (((0,), (0,)), ((), ())), preferred_element_type=F32)


def flip(value, axis):
    return lax.ppermute(value, axis, [(0, 1), (1, 0)])


RING = [(0, 1), (1, 3), (3, 2), (2, 0)]
RING_BACK = [(b, a) for a, b in RING]
SWAP = [(1, 2), (2, 1)]


def diagonal():
    return lax.axis_index("c") == lax.axis_index("zh")


def swap(value):
    return jnp.where(diagonal(), value, lax.ppermute(value, ("c", "zh"), SWAP))


def spread_pair(shard):
    near = jnp.where(diagonal(), shard, lax.ppermute(shard, ("c", "zh"), SWAP))
    far = lax.ppermute(shard, ("c", "zh"), RING)
    return [near, far]


def fold_pair(near, far):
    kept = jnp.where(diagonal(), near, lax.ppermute(near, ("c", "zh"), SWAP))
    return kept.astype(F32) + lax.ppermute(far, ("c", "zh"), RING_BACK).astype(F32)


def spread_bits(parts, order, bits):
    held = {(): parts}
    table = {}
    blocks = {0: parts[0], 1: parts[1]}
    for name in order:
        weight = 2 << (len(bits) - 1 - bits.index(name))
        keys = sorted(blocks)
        packed = jnp.concatenate([blocks[k] for k in keys], axis=0)
        came = flip(packed, name)
        rows = blocks[keys[0]].shape[0]
        for place, k in enumerate(keys):
            blocks[k + weight] = came[place * rows : (place + 1) * rows]
    return jnp.concatenate([blocks[k] for k in sorted(blocks)], axis=0)


def fold_bits(grad, order, bits):
    count = 2 << len(bits)
    rows = grad.shape[0] // count
    blocks = {k: grad[k * rows : (k + 1) * rows] for k in range(count)}
    for name in order:
        weight = 2 << (len(bits) - 1 - bits.index(name))
        keys = sorted(k for k in blocks if not k & weight)
        send = jnp.concatenate([blocks[k + weight] for k in keys], axis=0)
        came = flip(send, name)
        blocks = {
            k: (
                blocks[k].astype(F32) + came[place * rows : (place + 1) * rows].astype(F32)
            ).astype(BF16)
            for place, k in enumerate(keys)
        }
    return blocks[0], blocks[1]


def gather_rows(own):
    over = flip(own, "zl")
    beside = flip(own, "c")
    return [own, beside, over, flip(over, "c")]


def scatter_rows(partial):
    across = partial[2] + flip(partial[3].astype(BF16), "c").astype(F32)
    here = partial[0] + flip(partial[1].astype(BF16), "c").astype(F32)
    return here + flip(across.astype(BF16), "zl").astype(F32)


def normalise(stream, gain, shift):
    centre = jnp.mean(stream, axis=-1, keepdims=True)
    centred = stream - centre
    spread = jnp.mean(centred * centred, axis=-1, keepdims=True)
    return (centred * lax.rsqrt(spread + NORM_EPS) * gain + shift).astype(BF16)


def normalise_back(stream, gain, grad_normed, grad_stream):
    centre = jnp.mean(stream, axis=-1, keepdims=True)
    centred = stream - centre
    spread = jnp.mean(centred * centred, axis=-1, keepdims=True)
    inverse = lax.rsqrt(spread + NORM_EPS)
    unit = centred * inverse
    grad_gain = jnp.sum(grad_normed * unit, axis=0)
    grad_shift = jnp.sum(grad_normed, axis=0)
    scaled = grad_normed * gain
    grad_input = inverse * (
        scaled
        - jnp.mean(scaled, axis=-1, keepdims=True)
        - unit * jnp.mean(scaled * unit, axis=-1, keepdims=True)
    )
    return grad_stream + grad_input, grad_gain, grad_shift


def gelu_pair(upper):
    cdf = 0.5 * (1.0 + lax.erf(upper * (0.5**0.5)))
    density = jnp.exp(-0.5 * upper * upper) * (0.5 / jnp.pi) ** 0.5
    return (upper * cdf).astype(BF16), (cdf + upper * density).astype(BF16)


def causal_mask(scores, offset):
    rows = offset + lax.broadcasted_iota(jnp.int32, scores.shape[-2:], 0)
    cols = lax.broadcasted_iota(jnp.int32, scores.shape[-2:], 1)
    return jnp.where(rows >= cols, scores, MASKED)


def attend_rows(query, keys, values, causal, scale):
    frames = query.shape[0]
    mixed_rows, logsums = [], []
    block = min(ATT_BLOCK, frames)
    for start in range(0, frames, block):
        stop = start + block
        reach = stop if causal else keys.shape[0]
        scores = (
            jnp.einsum(
                "qhd,khd->hqk", query[start:stop], keys[:reach], preferred_element_type=F32
            )
            * scale
        )
        if causal:
            scores = causal_mask(scores, start)
        top = jnp.max(scores, axis=-1, keepdims=True)
        expo = jnp.exp(scores - top)
        total = jnp.sum(expo, axis=-1, keepdims=True)
        probs = (expo / total).astype(BF16)
        mixed_rows.append(
            jnp.einsum("hqk,khd->qhd", probs, values[:reach], preferred_element_type=F32)
        )
        logsums.append(top + jnp.log(total))
    joined = jnp.concatenate(mixed_rows, axis=0).reshape(frames, -1).astype(BF16)
    return joined, logsums


def attend_rows_back(query, keys, values, grad_joined, logsums, causal, scale):
    frames, heads = query.shape[0], query.shape[1]
    length = keys.shape[0]
    grad_mixed = grad_joined.reshape(frames, heads, HEAD_DIM)
    query_parts = []
    grad_keys = jnp.zeros(keys.shape, F32)
    grad_values = jnp.zeros(values.shape, F32)
    block = min(ATT_BLOCK, frames)
    for index, start in enumerate(range(0, frames, block)):
        stop = start + block
        reach = stop if causal else length
        q, k, v, g = query[start:stop], keys[:reach], values[:reach], grad_mixed[start:stop]
        scores = jnp.einsum("qhd,khd->hqk", q, k, preferred_element_type=F32) * scale
        if causal:
            scores = causal_mask(scores, start)
        probs = jnp.exp(scores - logsums[index])
        grad_probs = jnp.einsum("qhd,khd->hqk", g, v, preferred_element_type=F32)
        part_values = jnp.einsum(
            "hqk,qhd->khd", probs.astype(BF16), g, preferred_element_type=F32
        )
        inner = jnp.sum(probs * grad_probs, axis=-1, keepdims=True)
        grad_scores = (probs * (grad_probs - inner)).astype(BF16)
        query_parts.append(
            jnp.einsum("hqk,khd->qhd", grad_scores, k, preferred_element_type=F32) * scale
        )
        part_keys = jnp.einsum("hqk,qhd->khd", grad_scores, q, preferred_element_type=F32) * scale
        padding = ((0, length - reach), (0, 0), (0, 0))
        grad_keys = grad_keys + jnp.pad(part_keys, padding)
        grad_values = grad_values + jnp.pad(part_values, padding)
    return jnp.concatenate(query_parts, axis=0), grad_keys, grad_values


def to_time(parts):
    own, beside, over, both = parts
    c_one = lax.axis_index("c") == 1
    z_one = lax.axis_index("zl") == 1
    first = [jnp.where(z_one, over, own), jnp.where(z_one, own, over)]
    second = [jnp.where(z_one, both, beside), jnp.where(z_one, beside, both)]
    low = [jnp.where(c_one, s, f) for f, s in zip(first, second)]
    high = [jnp.where(c_one, f, s) for f, s in zip(first, second)]
    return jnp.concatenate(low + high, axis=0)


def from_time(rows):
    size = rows.shape[0] // 4
    q = [rows[i * size : (i + 1) * size] for i in range(4)]
    c_one = lax.axis_index("c") == 1
    z_one = lax.axis_index("zl") == 1
    mine = [jnp.where(c_one, q[2 + i], q[i]) for i in range(2)]
    core = [jnp.where(c_one, q[i], q[2 + i]) for i in range(2)]
    own = jnp.where(z_one, mine[1], mine[0])
    over = jnp.where(z_one, mine[0], mine[1])
    beside = jnp.where(z_one, core[1], core[0])
    both = jnp.where(z_one, core[0], core[1])
    return [own, beside, over, both]


def body(bits, frames_in, text_states, ln_gain, ln_bias, w_self, w_self_out, w_cross_q,
         w_cross_kv, w_cross_out, w_up, w_down, cotangent):
    scale = float(HEAD_DIM) ** (-0.5)
    layers = w_self.shape[0]
    width = frames_in.shape[2]
    part = w_self.shape[1]
    blocks = width // part
    cols = w_self.shape[3]
    me = lax.axis_index("zh")
    for place, name in enumerate(reversed(bits)):
        me = me + (lax.axis_index(name) << (place + 1))

    row = lax.broadcasted_iota(jnp.int32, (width, width), 0)
    col = lax.broadcasted_iota(jnp.int32, (width, width), 1)
    permute = ((row // part == ((col // part) ^ me)) & (row % part == col % part)).astype(BF16)

    def reorder(value):
        return nn(value, permute)

    frames_own = swap(frames_in[0])
    text_own = jnp.where(diagonal(), text_states[0], flip(text_states[0], "c"))
    text_own = reorder(text_own).astype(BF16)
    stream = reorder(frames_own)

    norms = jnp.concatenate(
        [ln_gain.reshape(-1, part), ln_bias.reshape(-1, part)], axis=0
    )
    norms = lax.all_gather(norms, (*bits, "c"), axis=0)
    norms = jnp.transpose(norms, (1, 0, 2)).reshape(norms.shape[1], width)
    norms = reorder(norms)
    gains = norms[: 3 * layers].reshape(layers, 3, 1, width)
    shifts = norms[3 * layers :].reshape(layers, 3, 1, width)

    straight = list(bits)
    crossed = list(reversed(bits))
    kinds = {"self": straight, "self_out": crossed, "q": straight, "kv": crossed,
             "out": crossed, "up": straight, "down": crossed}

    weights = []
    for l in range(layers):
        shards = {
            "self": w_self[l].reshape(part, 3 * cols),
            "self_out": w_self_out[l].T,
            "q": w_cross_q[l],
            "kv": w_cross_kv[l].reshape(part, 2 * cols),
            "out": w_cross_out[l].T,
            "up": w_up[l],
            "down": w_down[l].T,
        }
        full = {}
        for name, shard in shards.items():
            full[name] = spread_bits(spread_pair(shard), kinds[name], bits)
        weights.append(full)

    def self_split(proj_rows):
        split = proj_rows.reshape(proj_rows.shape[0], 3, cols // HEAD_DIM, HEAD_DIM)
        return split[:, 0], split[:, 1], split[:, 2]

    records = []
    for l in range(layers):
        w = weights[l]
        saved = {"one": stream}
        first = gather_rows(normalise(stream, gains[l, 0], shifts[l, 0]))
        proj = to_time([nn(r, w["self"]).astype(BF16) for r in first])
        query, keys, values = self_split(proj)
        joined, logsum = attend_rows(query, keys, values, True, scale)
        joined = from_time(joined)
        stream = stream + scatter_rows([nt(r, w["self_out"]) for r in joined])
        saved.update(first=first, proj=proj, joined_self=joined, logsum_self=logsum, two=stream)

        second = gather_rows(normalise(stream, gains[l, 1], shifts[l, 1]))
        cross_query = [nn(r, w["q"]).astype(BF16) for r in second]
        cross_query = jnp.concatenate(cross_query, axis=0).reshape(-1, cols // HEAD_DIM, HEAD_DIM)
        pairs = nn(text_own, w["kv"]).astype(BF16).reshape(-1, 2, cols // HEAD_DIM, HEAD_DIM)
        joined, logsum = attend_rows(cross_query, pairs[:, 0], pairs[:, 1], False, scale)
        size = joined.shape[0] // 4
        joined_parts = [joined[i * size : (i + 1) * size] for i in range(4)]
        stream = stream + scatter_rows([nt(r, w["out"]) for r in joined_parts])
        saved.update(second=second, cross_query=cross_query, pairs=pairs, joined_cross=joined,
                     logsum_cross=logsum, three=stream)

        third = gather_rows(normalise(stream, gains[l, 2], shifts[l, 2]))
        both = [gelu_pair(nn(r, w["up"])) for r in third]
        stream = stream + scatter_rows([nt(a, w["down"]) for a, _ in both])
        saved.update(third=third, active=[a for a, _ in both], slope=[d for _, d in both])
        records.append(saved)
    result = swap(reorder(stream.astype(BF16)).astype(BF16))

    grad = reorder(swap(cotangent[0]))
    grad_text = jnp.zeros((text_own.shape[0], width), F32)
    weight_grads = [None] * layers
    norm_grads = [None] * layers
    cat = lambda parts: jnp.concatenate(parts, axis=0)

    def settle(name, value):
        near, far = fold_bits(value.astype(BF16), list(reversed(kinds[name])), bits)
        return fold_pair(near, far)

    for l in reversed(range(layers)):
        w, saved = weights[l], records[l]
        out = {}
        full = gather_rows(grad.astype(BF16))
        grad_upper = [
            (nn(g, w["down"]) * d.astype(F32)).astype(BF16) for g, d in zip(full, saved["slope"])
        ]
        grad_third = scatter_rows([nt(u, w["up"]) for u in grad_upper])
        out["down"] = settle("down", tn(cat(full), cat(saved["active"])))
        out["up"] = settle("up", tn(cat(saved["third"]), cat(grad_upper)))
        grad, gain_three, shift_three = normalise_back(
            saved["three"], gains[l, 2], grad_third, grad
        )

        full = gather_rows(grad.astype(BF16))
        rows = cat(full)
        out["out"] = settle("out", tn(rows, saved["joined_cross"]))
        grad_joined = nn(rows, w["out"]).astype(BF16)
        pairs = saved["pairs"]
        grad_query, grad_keys, grad_values = attend_rows_back(
            saved["cross_query"], pairs[:, 0], pairs[:, 1], grad_joined, saved["logsum_cross"],
            False, scale,
        )
        grad_query = grad_query.reshape(grad_query.shape[0], cols).astype(BF16)
        grad_pairs = jnp.stack([grad_keys, grad_values], axis=1)
        grad_pairs = grad_pairs.reshape(grad_pairs.shape[0], 2 * cols).astype(BF16)
        size = grad_query.shape[0] // 4
        grad_second = scatter_rows(
            [nt(grad_query[i * size : (i + 1) * size], w["q"]) for i in range(4)]
        )
        out["q"] = settle("q", tn(cat(saved["second"]), grad_query))
        out["kv"] = settle("kv", tn(text_own, grad_pairs))
        grad_text = grad_text + nt(grad_pairs, w["kv"])
        grad, gain_two, shift_two = normalise_back(saved["two"], gains[l, 1], grad_second, grad)

        full = gather_rows(grad.astype(BF16))
        out["self_out"] = settle("self_out", tn(cat(full), cat(saved["joined_self"])))
        grad_joined = to_time([nn(g, w["self_out"]).astype(BF16) for g in full])
        query, keys, values = self_split(saved["proj"])
        grad_parts = attend_rows_back(
            query, keys, values, grad_joined, saved["logsum_self"], True, scale
        )
        grad_proj = jnp.stack(grad_parts, axis=1).reshape(query.shape[0], 3 * cols).astype(BF16)
        grad_proj = from_time(grad_proj)
        grad_first = scatter_rows([nt(p, w["self"]) for p in grad_proj])
        out["self"] = settle("self", tn(cat(saved["first"]), cat(grad_proj)))
        grad, gain_one, shift_one = normalise_back(saved["one"], gains[l, 0], grad_first, grad)
        weight_grads[l] = out
        norm_grads[l] = (gain_one, gain_two, gain_three, shift_one, shift_two, shift_three)

    grad_frames = swap(reorder(grad.astype(BF16)).astype(BF16)).astype(F32)
    text_sum = lax.psum(grad_text.astype(BF16), ("zl", "c"))
    text_sum = swap(reorder(text_sum).astype(BF16)).astype(F32)

    small = jnp.stack([g[:3] for g in norm_grads] and [jnp.stack(g) for g in norm_grads])
    small = small.reshape(layers * 6, blocks, part)
    steps = len(bits) + 1
    small = small.reshape((layers * 6,) + (2,) * steps + (part,))
    for place in range(steps):
        name = bits[place] if place < len(bits) else "zh"
        small = jnp.where(lax.axis_index(name) == 1, jnp.flip(small, axis=1 + place), small)
    small = small.reshape(layers * 6, blocks, part)
    small = lax.psum(small, (*bits, "c", "zh", "zl"))
    mine = lax.axis_index("c")
    for place, name in enumerate(reversed(bits)):
        mine = mine + (lax.axis_index(name) << (place + 1))
    small = lax.dynamic_index_in_dim(small, mine, axis=1, keepdims=False)
    small = small.reshape(layers, 6, part)

    def stacked(name, shape=None, turned=False):
        members = [weight_grads[l][name] for l in range(layers)]
        if turned:
            members = [m.T for m in members]
        if shape is not None:
            members = [m.reshape(shape) for m in members]
        return jnp.stack(members)

    return (
        result[None],
        grad_frames[None],
        text_sum[None],
        small[:, :3],
        small[:, 3:],
        stacked("self", (part, 3, cols)),
        stacked("self_out", turned=True),
        stacked("q"),
        stacked("kv", (part, 2, cols)),
        stacked("out", turned=True),
        stacked("up"),
        stacked("down", turned=True),
    )


def solution(mesh):
    count = mesh.shape["dp"]
    bits = tuple(f"b{i}" for i in range(count.bit_length() - 2))
    dp = (*bits, "c")
    tensor = ("zh", "zl")
    inner = Mesh(mesh.devices.reshape((2,) * (len(bits) + 3)), (*dp, *tensor))
    return jax.shard_map(
        functools.partial(body, bits),
        mesh=inner,
        in_specs=(
            P(dp, tensor, None),
            P(dp, None, None),
            P(None, None, dp),
            P(None, None, dp),
            P(None, dp, None, tensor),
            P(None, tensor, dp),
            P(None, dp, tensor),
            P(None, dp, None, tensor),
            P(None, tensor, dp),
            P(None, dp, tensor),
            P(None, tensor, dp),
            P(dp, tensor, None),
        ),
        out_specs=(
            P(dp, tensor, None),
            P(dp, tensor, None),
            P(dp, None, None),
            P(None, None, dp),
            P(None, None, dp),
            P(None, dp, None, tensor),
            P(None, tensor, dp),
            P(None, dp, tensor),
            P(None, dp, None, tensor),
            P(None, tensor, dp),
            P(None, dp, tensor),
            P(None, tensor, dp),
        ),
        check_vma=False,
    )
```

```python
import functools
import jax
import jax.numpy as jnp
from jax import lax
from jax.experimental import pallas as pl
from jax.experimental.pallas import tpu as pltpu
from jax.sharding import Mesh, PartitionSpec as P

HEAD_DIM = 64
ATT_BLOCK = 512
NORM_EPS = 1e-05
MASKED = -1e30
TILE = 384
F32 = jnp.float32
BF16 = jnp.bfloat16
MESH = pl.DeviceIdType.MESH
ANY = pl.BlockSpec(memory_space=pl.ANY)


def nn(a, b):
    return lax.dot_general(a, b, (((1,), (0,)), ((), ())), preferred_element_type=F32)


def nt(a, b):
    return lax.dot_general(a, b, (((1,), (1,)), ((), ())), preferred_element_type=F32)


def tn(a, b):
    return lax.dot_general(a, b, (((0,), (0,)), ((), ())), preferred_element_type=F32)


def flip(value, axis):
    return lax.ppermute(value, axis, [(0, 1), (1, 0)])


def diagonal():
    return lax.axis_index("c") == lax.axis_index("zh")


def off_diagonal():
    return lax.rem(lax.axis_index("c") + lax.axis_index("zh"), 2)


def target(kind):
    c, zh = lax.axis_index("c"), lax.axis_index("zh")
    off = off_diagonal()
    if kind == "ring":
        return {"c": lax.rem(c + off, 2), "zh": lax.rem(zh + 1 + off, 2)}
    if kind == "back":
        return {"c": lax.rem(c + 1 + off, 2), "zh": lax.rem(zh + off, 2)}
    if kind == "swap":
        return {"c": 1 - c, "zh": 1 - zh}
    return {kind: 1 - lax.axis_index(kind)}


def greeted(kinds):
    names = []
    for kind in kinds:
        pairs = {"ring": [("c",), ("zh",)], "back": [("c",), ("zh",)],
                 "swap": [("c", "zh")], "stay": []}.get(kind, [(kind,)])
        names += [p for p in pairs if p not in names]
    return names


def greet(kinds):
    barrier = pltpu.get_barrier_semaphore()
    names = greeted(kinds)
    for group in names:
        pl.semaphore_signal(
            barrier, inc=1, device_id={n: 1 - lax.axis_index(n) for n in group},
            device_id_type=MESH,
        )
    pl.semaphore_wait(barrier, len(names))


class Copy:
    def __init__(self, kind, src, dst, send, recv):
        self.kind = kind
        if kind == "stay":
            self.copy = pltpu.make_async_copy(src, dst, send)
        else:
            self.copy = pltpu.make_async_remote_copy(
                src_ref=src, dst_ref=dst, send_sem=send, recv_sem=recv,
                device_id=target(kind), device_id_type=MESH,
            )

    def guarded(self, act):
        if self.kind == "swap":
            pl.when(off_diagonal() == 1)(act)
        elif self.kind == "stay":
            pl.when(off_diagonal() == 0)(act)
        else:
            act()

    def start(self):
        self.guarded(lambda: self.copy.start())

    def wait(self):
        self.guarded(lambda: self.copy.wait())


class Ride:
    def __init__(self, ins, outs, stages, kinds, count, alias=()):
        self.ins, self.outs, self.stages = list(ins), list(outs), stages
        self.kinds, self.count, self.alias = list(kinds), count, dict(alias)


def runs(keys):
    keys, out = sorted(keys), []
    for k in keys:
        if out and out[-1][0] + out[-1][1] == k:
            out[-1][1] += 1
        else:
            out.append([k, 1])
    return out


def pair_ride(shard, blocks):
    rows, cols = shard.shape
    out = jax.ShapeDtypeStruct((rows * blocks, cols), shard.dtype)

    def stages(ins, outs):
        near, far = outs[0].at[pl.ds(0, rows)], outs[0].at[pl.ds(rows, rows)]
        return [[("ring", ins[0], far), ("swap", ins[0], near), ("stay", ins[0], near)]]

    return Ride([shard], [out], stages, ["ring", "swap"], 3)


def spread_ride(buffer, pieces, levels, blocks):
    rows = buffer.shape[0] // blocks
    plan = []
    for level in levels:
        stage = []
        for first, cols, order in pieces:
            held = [0, 1]
            for name, weight in order[:level]:
                held = held + [k + weight for k in held]
            name, weight = order[level]
            for k, n in runs(held):
                stage.append((name, k, k + weight, n, first, cols))
        plan.append(stage)

    def stages(ins, outs):
        ref = outs[0]
        return [
            [
                (name, ref.at[pl.ds(a * rows, n * rows), pl.ds(first, cols)],
                 ref.at[pl.ds(b * rows, n * rows), pl.ds(first, cols)])
                for name, a, b, n, first, cols in stage
            ]
            for stage in plan
        ]

    kinds = [item[0] for stage in plan for item in stage]
    out = jax.ShapeDtypeStruct(buffer.shape, buffer.dtype)
    return Ride([buffer], [out], stages, kinds, sum(len(s) for s in plan), {0: 0})


def send_ride(value, kind):
    out = jax.ShapeDtypeStruct(value.shape, value.dtype)
    return Ride([value], [out], lambda ins, outs: [[(kind, ins[0], outs[0])]], [kind], 1)


def launch(name, number, main, ins, outs, scratch, kinds, rides, limit=48):
    in_arrays = list(ins)
    out_shapes = list(outs)
    aliases = {}
    spans = []
    for ride in rides:
        for a, b in ride.alias.items():
            aliases[len(in_arrays) + a] = len(out_shapes) + b
        spans.append((len(in_arrays), len(in_arrays) + len(ride.ins),
                      len(out_shapes), len(out_shapes) + len(ride.outs)))
        in_arrays += ride.ins
        out_shapes += ride.outs
    total = sum(r.count for r in rides)
    all_kinds = list(kinds) + [k for r in rides for k in r.kinds]
    ride_sems = [pltpu.SemaphoreType.DMA((max(total, 1),)) for _ in range(2)]

    def kernel(*refs):
        in_refs = refs[: len(in_arrays)]
        out_refs = refs[len(in_arrays) : len(in_arrays) + len(out_shapes)]
        rest = refs[len(in_arrays) + len(out_shapes) :]
        send, recv = rest[:2]
        early = main(in_refs[: len(ins)], out_refs[: len(outs)], rest[2:], True) if main else None
        greet(all_kinds)
        chains, place = [], 0
        for ride, (a, b, c, d) in zip(rides, spans):
            chain = []
            for stage in ride.stages(in_refs[a:b], out_refs[c:d]):
                chain.append([])
                for kind, src, dst in stage:
                    chain[-1].append(Copy(kind, src, dst, send.at[place], recv.at[place]))
                    place += 1
            chains.append(chain)
        for chain in chains:
            for copy in chain[0]:
                copy.start()
        if main:
            main(in_refs[: len(ins)], out_refs[: len(outs)], rest[2:], early)
        for level in range(max([len(c) for c in chains], default=0)):
            for chain in chains:
                if level < len(chain):
                    for copy in chain[level]:
                        copy.wait()
                    if level + 1 < len(chain):
                        for copy in chain[level + 1]:
                            copy.start()

    results = pl.pallas_call(
        kernel,
        out_shape=tuple(out_shapes),
        in_specs=[ANY] * len(in_arrays),
        out_specs=tuple([ANY] * len(out_shapes)),
        scratch_shapes=ride_sems + list(scratch),
        input_output_aliases=aliases,
        name=name,
        compiler_params=pltpu.CompilerParams(
            collective_id=number, has_side_effects=True, vmem_limit_bytes=limit << 20
        ),
    )(*in_arrays)
    main_outs = results[: len(outs)]
    return main_outs, [results[c:d] for _, _, c, d in spans]


def normalise_value(rows, gain, shift):
    centre = jnp.mean(rows, axis=-1, keepdims=True)
    centred = rows - centre
    spread = jnp.mean(centred * centred, axis=-1, keepdims=True)
    return (centred * lax.rsqrt(spread + NORM_EPS) * gain + shift).astype(BF16)


def gelu_pair(upper):
    cdf = 0.5 * (1.0 + lax.erf(upper * (0.5**0.5)))
    density = jnp.exp(-0.5 * upper * upper) * (0.5 / jnp.pi) ** 0.5
    return (upper * cdf).astype(BF16), (cdf + upper * density).astype(BF16)


def gather_multiply(number, rows_in, norm, weight, ending, slope, rides):
    size, width = rows_in.shape
    n = weight.shape[1]
    tile = min(TILE, n)
    ins = [rows_in, weight]
    if norm is not None:
        ins.append(jnp.concatenate([norm[0], norm[1]], axis=0))
    if slope is not None:
        ins.append(slope)
    double = ending == "gelu"
    outs = [jax.ShapeDtypeStruct((4, size, width), BF16)]
    outs += [jax.ShapeDtypeStruct((4, size, n), BF16)] * (2 if double else 1)
    half = size // 2
    scratch = [
        pltpu.VMEM((size, width), F32),
        pltpu.VMEM((width, n), BF16),
        pltpu.VMEM((2, width), F32),
        pltpu.VMEM((4, size, width), BF16),
        pltpu.VMEM((4, size, n), BF16),
        pltpu.VMEM((4, size, n) if (double or slope is not None) else (8, 128), BF16),
        pltpu.SemaphoreType.DMA((4,)),
        pltpu.SemaphoreType.DMA((6,)),
        pltpu.SemaphoreType.DMA((6,)),
        pltpu.SemaphoreType.DMA((3, 4)),
    ]

    def main(in_refs, out_refs, refs, stage):
        rows, w, norms, x, y, second, load, send, recv, store = refs
        if stage is True:
            loads = [
                pltpu.make_async_copy(in_refs[0], rows, load.at[0]),
                pltpu.make_async_copy(in_refs[1], w, load.at[1]),
            ]
            if norm is not None:
                loads.append(pltpu.make_async_copy(in_refs[2], norms, load.at[2]))
            if slope is not None:
                loads.append(pltpu.make_async_copy(in_refs[-1], second, load.at[3]))
            for copy in loads:
                copy.start()
            return loads
        loads = stage
        loads[0].wait()
        if norm is not None:
            loads[2].wait()
        over, beside, relay, stores = [], [], [], []
        for h in range(2):
            part = pl.ds(h * half, half)
            value = rows[part, :]
            if norm is not None:
                value = normalise_value(value, norms[0:1, :], norms[1:2, :])
            x[0, part, :] = value.astype(BF16)
            over.append(Copy("zl", x.at[0, part], x.at[2, part], send.at[h], recv.at[h]))
            over[-1].start()
        beside = Copy("c", x.at[0], x.at[1], send.at[2], recv.at[2])
        beside.start()
        loads[1].wait()
        if slope is not None:
            loads[-1].wait()

        def multiply(b):
            def step(j, carry):
                cols = pl.ds(pl.multiple_of(j * tile, tile), tile)
                value = nn(x[b], w[:, cols])
                if double:
                    y[b, :, cols], second[b, :, cols] = gelu_pair(value)
                elif slope is not None:
                    y[b, :, cols] = (value * second[b, :, cols].astype(F32)).astype(BF16)
                else:
                    y[b, :, cols] = value.astype(BF16)
                return carry

            lax.fori_loop(0, n // tile, step, 0)
            done = [pltpu.make_async_copy(x.at[b], out_refs[0].at[b], store.at[0, b]),
                    pltpu.make_async_copy(y.at[b], out_refs[1].at[b], store.at[1, b])]
            if double:
                done.append(pltpu.make_async_copy(second.at[b], out_refs[2].at[b], store.at[2, b]))
            for copy in done:
                copy.start()
            stores.extend(done)

        multiply(0)
        beside.wait()
        multiply(1)
        for h in range(2):
            part = pl.ds(h * half, half)
            over[h].wait()
            relay.append(Copy("c", x.at[2, part], x.at[3, part], send.at[3 + h], recv.at[3 + h]))
            relay[-1].start()
        multiply(2)
        for copy in relay:
            copy.wait()
        multiply(3)
        for copy in stores:
            copy.wait()

    return launch(f"gather_{number}", number, main, ins, outs, scratch, ["c", "zl"], rides)


def multiply_scatter(number, parts, weight, base, rides):
    _, size, n = parts.shape
    width = weight.shape[0]
    half = size // 2
    ins = [parts, weight] + ([base] if base is not None else [])
    outs = [jax.ShapeDtypeStruct((size, width), F32)]
    scratch = [
        pltpu.VMEM((4, size, n), BF16),
        pltpu.VMEM((width, n), BF16),
        pltpu.VMEM((size, width), F32),
        pltpu.VMEM((size, width), F32),
        pltpu.VMEM((2, size, width), BF16),
        pltpu.VMEM((2, size, width), BF16),
        pltpu.VMEM((size, width), BF16),
        pltpu.VMEM((size, width), BF16),
        pltpu.SemaphoreType.DMA((7,)),
        pltpu.SemaphoreType.DMA((6,)),
        pltpu.SemaphoreType.DMA((6,)),
    ]

    def main(in_refs, out_refs, refs, stage):
        y, w, total, far, give, came, across, over, load, send, recv = refs
        if stage is True:
            loads = [pltpu.make_async_copy(in_refs[1], w, load.at[0])]
            loads += [
                pltpu.make_async_copy(in_refs[0].at[b], y.at[b], load.at[1 + b])
                for b in range(4)
            ]
            if base is not None:
                loads.append(pltpu.make_async_copy(in_refs[2], total, load.at[5]))
            for place in (0, 4, 3, 2, 1, 5)[: len(loads)]:
                loads[place].start()
            return loads
        loads = stage

        def multiply(b, part, put):
            def step(j, carry):
                cols = pl.ds(pl.multiple_of(j * TILE, TILE), TILE)
                put(cols, nt(y[b, part, :], w[cols, :]))
                return carry

            lax.fori_loop(0, width // TILE, step, 0)

        whole = pl.ds(0, size)
        for place in (0, 4, 3):
            loads[place].wait()
        sent = []
        for h in range(2):
            part = pl.ds(h * half, half)

            def put_give(cols, value, part=part):
                give[0, part, cols] = value.astype(BF16)

            def put_far(cols, value, part=part):
                far[part, cols] = value

            multiply(3, part, put_give)
            copy = Copy("c", give.at[0, part], came.at[0, part], send.at[h], recv.at[h])
            copy.start()
            multiply(2, part, put_far)
            copy.wait()
            across[part, :] = (far[part, :] + came[0, part, :].astype(F32)).astype(BF16)
            copy = Copy("zl", across.at[part], over.at[part], send.at[2 + h], recv.at[2 + h])
            copy.start()
            sent.append(copy)
        loads[2].wait()

        def put_near(cols, value):
            give[1, :, cols] = value.astype(BF16)

        multiply(1, whole, put_near)
        near = Copy("c", give.at[1], came.at[1], send.at[4], recv.at[4])
        near.start()
        loads[1].wait()
        if base is not None:
            loads[5].wait()

        def put_total(cols, value):
            total[:, cols] = value + (total[:, cols] if base is not None else 0.0)

        multiply(0, whole, put_total)
        near.wait()
        total[...] += came[1].astype(F32)
        done = []
        for h in range(2):
            part = pl.ds(h * half, half)
            sent[h].wait()
            total[part, :] += over[part, :].astype(F32)
            copy = pltpu.make_async_copy(total.at[part], out_refs[0].at[part], load.at[5 + h])
            copy.start()
            done.append(copy)
        for copy in done:
            copy.wait()

    (out,), extra = launch(
        f"scatter_{number}", number, main, ins, outs, scratch, ["c", "zl"], rides
    )
    return out, extra


def normalise_back(stream, gain, grad_normed, grad_stream):
    centre = jnp.mean(stream, axis=-1, keepdims=True)
    centred = stream - centre
    spread = jnp.mean(centred * centred, axis=-1, keepdims=True)
    inverse = lax.rsqrt(spread + NORM_EPS)
    unit = centred * inverse
    grad_gain = jnp.sum(grad_normed * unit, axis=0)
    grad_shift = jnp.sum(grad_normed, axis=0)
    scaled = grad_normed * gain
    grad_input = inverse * (
        scaled
        - jnp.mean(scaled, axis=-1, keepdims=True)
        - unit * jnp.mean(scaled * unit, axis=-1, keepdims=True)
    )
    return grad_stream + grad_input, grad_gain, grad_shift


def causal_mask(scores, offset):
    rows = offset + lax.broadcasted_iota(jnp.int32, scores.shape[-2:], 0)
    cols = lax.broadcasted_iota(jnp.int32, scores.shape[-2:], 1)
    return jnp.where(rows >= cols, scores, MASKED)


def attend_rows(query, keys, values, causal, scale):
    frames = query.shape[0]
    mixed_rows, logsums = [], []
    block = min(ATT_BLOCK, frames)
    for start in range(0, frames, block):
        stop = start + block
        reach = stop if causal else keys.shape[0]
        scores = (
            jnp.einsum(
                "qhd,khd->hqk", query[start:stop], keys[:reach], preferred_element_type=F32
            )
            * scale
        )
        if causal:
            scores = causal_mask(scores, start)
        top = jnp.max(scores, axis=-1, keepdims=True)
        expo = jnp.exp(scores - top)
        total = jnp.sum(expo, axis=-1, keepdims=True)
        probs = (expo / total).astype(BF16)
        mixed_rows.append(
            jnp.einsum("hqk,khd->qhd", probs, values[:reach], preferred_element_type=F32)
        )
        logsums.append(top + jnp.log(total))
    joined = jnp.concatenate(mixed_rows, axis=0).reshape(frames, -1).astype(BF16)
    return joined, logsums


def attend_rows_back(query, keys, values, grad_joined, logsums, causal, scale):
    frames, heads = query.shape[0], query.shape[1]
    length = keys.shape[0]
    grad_mixed = grad_joined.reshape(frames, heads, HEAD_DIM)
    query_parts = []
    grad_keys = jnp.zeros(keys.shape, F32)
    grad_values = jnp.zeros(values.shape, F32)
    block = min(ATT_BLOCK, frames)
    for index, start in enumerate(range(0, frames, block)):
        stop = start + block
        reach = stop if causal else length
        q, k, v, g = query[start:stop], keys[:reach], values[:reach], grad_mixed[start:stop]
        scores = jnp.einsum("qhd,khd->hqk", q, k, preferred_element_type=F32) * scale
        if causal:
            scores = causal_mask(scores, start)
        probs = jnp.exp(scores - logsums[index])
        grad_probs = jnp.einsum("qhd,khd->hqk", g, v, preferred_element_type=F32)
        part_values = jnp.einsum(
            "hqk,qhd->khd", probs.astype(BF16), g, preferred_element_type=F32
        )
        inner = jnp.sum(probs * grad_probs, axis=-1, keepdims=True)
        grad_scores = (probs * (grad_probs - inner)).astype(BF16)
        query_parts.append(
            jnp.einsum("hqk,khd->qhd", grad_scores, k, preferred_element_type=F32) * scale
        )
        part_keys = jnp.einsum("hqk,qhd->khd", grad_scores, q, preferred_element_type=F32) * scale
        padding = ((0, length - reach), (0, 0), (0, 0))
        grad_keys = grad_keys + jnp.pad(part_keys, padding)
        grad_values = grad_values + jnp.pad(part_values, padding)
    return jnp.concatenate(query_parts, axis=0), grad_keys, grad_values


def to_time(parts):
    own, beside, over, both = [parts[i] for i in range(4)]
    c_one = lax.axis_index("c") == 1
    z_one = lax.axis_index("zl") == 1
    first = [jnp.where(z_one, over, own), jnp.where(z_one, own, over)]
    second = [jnp.where(z_one, both, beside), jnp.where(z_one, beside, both)]
    low = [jnp.where(c_one, s, f) for f, s in zip(first, second)]
    high = [jnp.where(c_one, f, s) for f, s in zip(first, second)]
    return jnp.concatenate(low + high, axis=0)


def from_time(rows):
    size = rows.shape[0] // 4
    q = [rows[i * size : (i + 1) * size] for i in range(4)]
    c_one = lax.axis_index("c") == 1
    z_one = lax.axis_index("zl") == 1
    mine = [jnp.where(c_one, q[2 + i], q[i]) for i in range(2)]
    core = [jnp.where(c_one, q[i], q[2 + i]) for i in range(2)]
    own = jnp.where(z_one, mine[1], mine[0])
    over = jnp.where(z_one, mine[0], mine[1])
    beside = jnp.where(z_one, core[1], core[0])
    both = jnp.where(z_one, core[0], core[1])
    return jnp.stack([own, beside, over, both])


def flat(parts):
    return parts.reshape(-1, parts.shape[-1])


def body(bits, frames_in, text_states, ln_gain, ln_bias, w_self, w_self_out, w_cross_q,
         w_cross_kv, w_cross_out, w_up, w_down, cotangent):
    scale = float(HEAD_DIM) ** (-0.5)
    layers = w_self.shape[0]
    width = frames_in.shape[2]
    part = w_self.shape[1]
    blocks = width // part
    cols = w_self.shape[3]
    hidden = w_up.shape[2]
    heads = cols // HEAD_DIM
    me = lax.axis_index("zh")
    for place, name in enumerate(reversed(bits)):
        me = me + (lax.axis_index(name) << (place + 1))

    row = lax.broadcasted_iota(jnp.int32, (width, width), 0)
    col = lax.broadcasted_iota(jnp.int32, (width, width), 1)
    permute = ((row // part == ((col // part) ^ me)) & (row % part == col % part)).astype(BF16)

    def reorder(value):
        return nn(value, permute)

    up = [(name, 2 << (len(bits) - 1 - place)) for place, name in enumerate(bits)]
    low_first = list(reversed(up))
    levels = len(bits)
    early, late = list(range(levels // 2)), list(range(levels // 2, levels))
    sizes = {"self": 3 * cols, "self_out": cols, "q": cols, "kv": 2 * cols, "out": cols,
             "up": hidden, "down": hidden, "norm": 128}

    def halves(name):
        n = sizes[name]
        if name == "self":
            return [(0, 2 * cols, low_first), (2 * cols, cols, up)]
        if name in ("up", "down"):
            return [(0, n // 2, low_first), (n // 2, n // 2, up)]
        return [(0, n, low_first if name == "kv" else up)]

    packs = {"a": ["self", "self_out"], "b": ["q", "kv", "out"], "c": ["up"], "d": ["down"]}
    shards = {}
    for l in range(layers):
        shards[l, "self"] = w_self[l].reshape(part, 3 * cols)
        shards[l, "self_out"] = w_self_out[l].T
        shards[l, "q"] = w_cross_q[l]
        shards[l, "kv"] = w_cross_kv[l].reshape(part, 2 * cols)
        shards[l, "out"] = w_cross_out[l].T
        shards[l, "up"] = w_up[l]
        shards[l, "down"] = w_down[l].T
    held = {}
    counter = [0]

    def number():
        counter[0] += 1
        return counter[0] - 1

    def weight_rides(todo):
        rides, keys = [], []
        for l, pack, stage in todo:
            for name in packs[pack]:
                key = (l, name)
                if stage == 1:
                    rides.append(pair_ride(shards[key], blocks))
                else:
                    rides.append(spread_ride(
                        held[key], halves(name), early if stage == 2 else late, blocks))
                keys.append(key)
        return rides, keys

    def keep(keys, extra):
        for key, value in zip(keys, extra):
            held[key] = value[0]

    forward = {
        0: [(0, "b", 2), (0, "c", 1)],
        1: [(0, "b", 3), (0, "c", 2)],
        2: [(0, "c", 3), (0, "d", 1)],
        3: [(0, "d", 2), (1, "a", 1)],
        4: [(0, "d", 3), (1, "a", 2)],
        5: [(1, "a", 3), (1, "b", 1)],
        6: [(1, "b", 2), (1, "c", 1)],
        7: [(1, "b", 3), (1, "c", 2)],
        8: [(1, "c", 3), (1, "d", 1)],
        9: [(1, "d", 2)],
        10: [(1, "d", 3)],
    }
    step = [0]

    def next_rides(more=()):
        todo = [t for t in forward.get(step[0], []) if t[0] < layers]
        step[0] += 1
        rides, keys = weight_rides(todo)
        return rides, keys

    def simple_launch(rides):
        return launch(f"move_{counter[0]}", number(), None, [], [], [], [], rides)[1]

    rides, keys = weight_rides([(0, "a", 1)])
    rides.append(send_ride(frames_in[0], "swap"))
    second, keys_b = weight_rides([(0, "b", 1)])
    extra = simple_launch(rides + second)
    keep(keys, extra[: len(keys)])
    keep(keys_b, extra[len(keys) + 1 :])
    frames_own = jnp.where(diagonal(), frames_in[0], extra[len(keys)][0])
    rides, keys = weight_rides([(0, "a", 2)])
    extra = simple_launch(rides)
    keep(keys, extra)
    rides, keys = weight_rides([(0, "a", 3)])
    extra = simple_launch(rides)
    keep(keys, extra)

    text_own = jnp.where(diagonal(), text_states[0], flip(text_states[0], "c"))
    text_own = reorder(text_own).astype(BF16)
    stream = reorder(frames_own)

    norms = jnp.concatenate([ln_gain.reshape(-1, part), ln_bias.reshape(-1, part)], axis=0)
    norms = lax.all_gather(norms, (*bits, "c"), axis=0)
    norms = jnp.transpose(norms, (1, 0, 2)).reshape(norms.shape[1], width)
    norms = reorder(norms)
    gains = norms[: 3 * layers].reshape(layers, 3, 1, width)
    shifts = norms[3 * layers :].reshape(layers, 3, 1, width)

    def self_split(proj_rows):
        split = proj_rows.reshape(proj_rows.shape[0], 3, heads, HEAD_DIM)
        return split[:, 0], split[:, 1], split[:, 2]

    def gathered(rows, norm, key, ending=None, slope=None, more=()):
        rides, keys = next_rides()
        outs, extra = gather_multiply(
            number(), rows, norm, held[key], ending, slope, rides + list(more))
        keep(keys, extra)
        return outs, [e[0] for e in extra[len(keys):]]

    def scattered(parts, key, base, more=()):
        rides, keys = next_rides()
        out, extra = multiply_scatter(number(), parts, held[key], base, rides + list(more))
        keep(keys, extra)
        return out, [e[0] for e in extra[len(keys):]]

    records = []
    for l in range(layers):
        saved = {"one": stream}
        more = [send_ride(cotangent[0], "swap")] if l == layers - 1 else []
        (first, proj), extra = gathered(stream, (gains[l, 0], shifts[l, 0]), (l, "self"),
                                        more=more)
        if more:
            cot_own = jnp.where(diagonal(), cotangent[0], extra[0])
        proj = to_time(proj)
        query, keys_, values = self_split(proj)
        joined, logsum = attend_rows(query, keys_, values, True, scale)
        joined = from_time(joined)
        stream, _ = scattered(joined, (l, "self_out"), stream)
        saved.update(first=first, proj=proj, joined_self=joined, logsum_self=logsum, two=stream)

        (normed, cross), _ = gathered(stream, (gains[l, 1], shifts[l, 1]), (l, "q"))
        cross_query = flat(cross).reshape(-1, heads, HEAD_DIM)
        pairs = nn(text_own, held[l, "kv"]).astype(BF16).reshape(-1, 2, heads, HEAD_DIM)
        joined, logsum = attend_rows(cross_query, pairs[:, 0], pairs[:, 1], False, scale)
        joined = joined.reshape(4, -1, cols)
        stream, _ = scattered(joined, (l, "out"), stream)
        saved.update(second=normed, cross_query=cross_query, pairs=pairs, joined_cross=joined,
                     logsum_cross=logsum, three=stream)

        (third, active, slope), _ = gathered(
            stream, (gains[l, 2], shifts[l, 2]), (l, "up"), "gelu")
        stream, _ = scattered(active, (l, "down"), stream)
        saved.update(third=third, active=active, slope=slope)
        records.append(saved)
    result_own = reorder(stream.astype(BF16)).astype(BF16)
    grad = reorder(cot_own)

    folding = []
    finished = {}
    grad_text = jnp.zeros((text_own.shape[0], width), F32)
    norm_grads = [None] * layers

    def fold_later(l, name, value):
        value = value.astype(BF16)
        for first, n, order in halves(name):
            chunk = value[:, first : first + n] if n != value.shape[1] else value
            table = {k: chunk[k * part : (k + 1) * part] for k in range(blocks)}
            folding.append({"key": (l, name, first), "table": table,
                            "order": list(reversed(order)), "level": 0})

    def fold_start(limit):
        rides, items, spent = [], [], 0
        for item in list(folding):
            if spent >= limit:
                break
            if item["level"] < len(item["order"]):
                name, weight = item["order"][item["level"]]
                away = sorted(k for k in item["table"] if k & weight)
                value = jnp.concatenate([item["table"][k] for k in away], axis=0)
                rides.append(send_ride(value, name))
                spent += value.size * 2
            else:
                near, far = item["table"][0], item["table"][1]
                ride = Ride(
                    [near, far],
                    [jax.ShapeDtypeStruct(near.shape, BF16)] * 2,
                    lambda ins, outs: [[("swap", ins[0], outs[0]), ("back", ins[1], outs[1])]],
                    ["swap", "back"], 2,
                )
                rides.append(ride)
                spent += near.size * 4
            items.append(item)
        return rides, items

    def fold_end(items, extra):
        for item, came in zip(items, extra):
            if item["level"] < len(item["order"]):
                name, weight = item["order"][item["level"]]
                stay = sorted(k for k in item["table"] if not k & weight)
                item["table"] = {
                    k: (
                        item["table"][k].astype(F32)
                        + came[0][i * part : (i + 1) * part].astype(F32)
                    ).astype(BF16)
                    for i, k in enumerate(stay)
                }
                item["level"] += 1
            else:
                near = jnp.where(diagonal(), item["table"][0], came[0])
                finished[item["key"]] = near.astype(F32) + came[1].astype(F32)
                folding.remove(item)

    budget = 5 << 20

    def back_gathered(rows, key, slope=None, more=()):
        rides, items = fold_start(budget)
        outs, extra = gather_multiply(
            number(), rows, None, held[key], None, slope, rides + list(more))
        fold_end(items, extra)
        return outs, [e[0] for e in extra[len(items):]]

    def back_scattered(parts, key):
        rides, items = fold_start(budget)
        out, extra = multiply_scatter(number(), parts, held[key], None, rides)
        fold_end(items, extra)
        return out

    for l in reversed(range(layers)):
        saved = records[l]
        more = [send_ride(result_own, "swap")] if l == layers - 1 else []
        (full, grad_upper), extra = back_gathered(grad, (l, "down"), saved["slope"], more)
        if more:
            result = jnp.where(diagonal(), result_own, extra[0])
        fold_later(l, "down", tn(flat(full), flat(saved["active"])))
        grad_third = back_scattered(grad_upper, (l, "up"))
        fold_later(l, "up", tn(flat(saved["third"]), flat(grad_upper)))
        grad, gain_three, shift_three = normalise_back(
            saved["three"], gains[l, 2], grad_third, grad)

        (full, grad_joined), _ = back_gathered(grad, (l, "out"))
        fold_later(l, "out", tn(flat(full), flat(saved["joined_cross"])))
        pairs = saved["pairs"]
        grad_query, grad_keys, grad_values = attend_rows_back(
            saved["cross_query"], pairs[:, 0], pairs[:, 1], flat(grad_joined),
            saved["logsum_cross"], False, scale)
        grad_query = grad_query.reshape(4, -1, cols).astype(BF16)
        grad_pairs = jnp.stack([grad_keys, grad_values], axis=1)
        grad_pairs = grad_pairs.reshape(grad_pairs.shape[0], 2 * cols).astype(BF16)
        grad_second = back_scattered(grad_query, (l, "q"))
        fold_later(l, "q", tn(flat(saved["second"]), flat(grad_query)))
        fold_later(l, "kv", tn(text_own, grad_pairs))
        grad_text = grad_text + nt(grad_pairs, held[l, "kv"])
        grad, gain_two, shift_two = normalise_back(saved["two"], gains[l, 1], grad_second, grad)

        (full, grad_joined), _ = back_gathered(grad, (l, "self_out"))
        fold_later(l, "self_out", tn(flat(full), flat(saved["joined_self"])))
        query, keys_, values = self_split(saved["proj"])
        grad_parts = attend_rows_back(
            query, keys_, values, to_time(grad_joined), saved["logsum_self"], True, scale)
        grad_proj = jnp.stack(grad_parts, axis=1).reshape(query.shape[0], 3 * cols).astype(BF16)
        grad_proj = from_time(grad_proj)
        grad_first = back_scattered(grad_proj, (l, "self"))
        fold_later(l, "self", tn(flat(saved["first"]), flat(grad_proj)))
        grad, gain_one, shift_one = normalise_back(saved["one"], gains[l, 0], grad_first, grad)
        norm_grads[l] = [gain_one, gain_two, gain_three, shift_one, shift_two, shift_three]

    small = jnp.stack([row for rows in norm_grads for row in rows], axis=1)
    small = jnp.pad(small, ((0, 0), (0, sizes["norm"] - small.shape[1])))
    fold_later(0, "norm", small)
    frames_back = reorder(grad.astype(BF16)).astype(BF16)
    text_back = grad_text.astype(BF16)
    extras = [send_ride(frames_back, "swap"), send_ride(text_back, "c")]
    round_ = 0
    while folding:
        rides, items = fold_start(1 << 40)
        extra = simple_launch(rides + extras)
        fold_end(items, extra)
        tail = [e[0] for e in extra[len(items):]]
        if round_ == 0:
            grad_frames = jnp.where(diagonal(), frames_back, tail[0]).astype(F32)
            text_sum = (text_back.astype(F32) + tail[1].astype(F32)).astype(BF16)
            extras = [send_ride(text_sum, "zl")]
        elif round_ == 1:
            text_sum = reorder((text_sum.astype(F32) + tail[0].astype(F32)).astype(BF16))
            text_sum = text_sum.astype(BF16)
            extras = [send_ride(text_sum, "swap")]
        elif round_ == 2:
            text_sum = jnp.where(diagonal(), text_sum, tail[0]).astype(F32)
            extras = []
        round_ += 1

    small = finished[0, "norm", 0][:, : 6 * layers]
    for name in ("zl", "zh"):
        small = small + flip(small, name)
    small = small.T.reshape(layers, 6, part)

    def gradient(l, name):
        pieces = [finished[l, name, first] for first, _, _ in halves(name)]
        return jnp.concatenate(pieces, axis=1) if len(pieces) > 1 else pieces[0]

    def stacked(name, shape=None, turned=False):
        members = [gradient(l, name) for l in range(layers)]
        if turned:
            members = [m.T for m in members]
        if shape is not None:
            members = [m.reshape(shape) for m in members]
        return jnp.stack(members)

    return (
        result[None],
        grad_frames[None],
        text_sum[None],
        small[:, :3],
        small[:, 3:],
        stacked("self", (part, 3, cols)),
        stacked("self_out", turned=True),
        stacked("q"),
        stacked("kv", (part, 2, cols)),
        stacked("out", turned=True),
        stacked("up"),
        stacked("down", turned=True),
    )


def solution(mesh):
    count = mesh.shape["dp"]
    bits = tuple(f"b{i}" for i in range(count.bit_length() - 2))
    dp = (*bits, "c")
    tensor = ("zh", "zl")
    inner = Mesh(mesh.devices.reshape((2,) * (len(bits) + 3)), (*dp, *tensor))
    return jax.shard_map(
        functools.partial(body, bits),
        mesh=inner,
        in_specs=(
            P(dp, tensor, None),
            P(dp, None, None),
            P(None, None, dp),
            P(None, None, dp),
            P(None, dp, None, tensor),
            P(None, tensor, dp),
            P(None, dp, tensor),
            P(None, dp, None, tensor),
            P(None, tensor, dp),
            P(None, dp, tensor),
            P(None, tensor, dp),
            P(dp, tensor, None),
        ),
        out_specs=(
            P(dp, tensor, None),
            P(dp, tensor, None),
            P(dp, None, None),
            P(None, None, dp),
            P(None, None, dp),
            P(None, dp, None, tensor),
            P(None, tensor, dp),
            P(None, dp, tensor),
            P(None, dp, None, tensor),
            P(None, tensor, dp),
            P(None, dp, tensor),
            P(None, tensor, dp),
        ),
        check_vma=False,
    )
```

```python
import functools
import jax
import jax.numpy as jnp
from jax import lax
from jax.experimental import pallas as pl
from jax.experimental.pallas import tpu as pltpu
from jax.sharding import Mesh, PartitionSpec as P

HEAD_DIM = 64
NORM_EPS = 1e-05
MASKED = -1e30
TILE = 384
LINK_BYTES = 1400000
F32 = jnp.float32
BF16 = jnp.bfloat16
MESH = pl.DeviceIdType.MESH
ANY = pl.BlockSpec(memory_space=pl.ANY)


def nn(a, b):
    return lax.dot_general(a, b, (((1,), (0,)), ((), ())), preferred_element_type=F32)


def nt(a, b):
    return lax.dot_general(a, b, (((1,), (1,)), ((), ())), preferred_element_type=F32)


def tn(a, b):
    return lax.dot_general(a, b, (((0,), (0,)), ((), ())), preferred_element_type=F32)


def flip(value, axis):
    return lax.ppermute(value, axis, [(0, 1), (1, 0)])


def diagonal():
    return lax.axis_index("c") == lax.axis_index("zh")


def off_diagonal():
    return lax.rem(lax.axis_index("c") + lax.axis_index("zh"), 2)


def target(kind):
    c, zh = lax.axis_index("c"), lax.axis_index("zh")
    off = off_diagonal()
    if kind == "ring":
        return {"c": lax.rem(c + off, 2), "zh": lax.rem(zh + 1 + off, 2)}
    if kind == "back":
        return {"c": lax.rem(c + 1 + off, 2), "zh": lax.rem(zh + off, 2)}
    if kind == "swap":
        return {"c": 1 - c, "zh": 1 - zh}
    return {kind: 1 - lax.axis_index(kind)}


def greeted(kinds):
    names = []
    for kind in kinds:
        pairs = {"ring": [("c",), ("zh",)], "back": [("c",), ("zh",)],
                 "swap": [("c", "zh")], "stay": []}.get(kind, [(kind,)])
        names += [p for p in pairs if p not in names]
    return names


def greet(kinds):
    barrier = pltpu.get_barrier_semaphore()
    names = greeted(kinds)
    for group in names:
        pl.semaphore_signal(
            barrier, inc=1, device_id={n: 1 - lax.axis_index(n) for n in group},
            device_id_type=MESH,
        )
    pl.semaphore_wait(barrier, len(names))


class Copy:
    def __init__(self, kind, src, dst, send, recv):
        self.kind = kind
        if kind == "stay":
            self.copy = pltpu.make_async_copy(src, dst, send)
        else:
            self.copy = pltpu.make_async_remote_copy(
                src_ref=src, dst_ref=dst, send_sem=send, recv_sem=recv,
                device_id=target(kind), device_id_type=MESH,
            )

    def guarded(self, act):
        if self.kind == "swap":
            pl.when(off_diagonal() == 1)(act)
        elif self.kind == "stay":
            pl.when(off_diagonal() == 0)(act)
        else:
            act()

    def start(self):
        self.guarded(lambda: self.copy.start())

    def wait(self):
        self.guarded(lambda: self.copy.wait())


class Ride:
    def __init__(self, ins, outs, stages, kinds, count, alias=()):
        self.ins, self.outs, self.stages = list(ins), list(outs), stages
        self.kinds, self.count, self.alias = list(kinds), count, dict(alias)


def runs(keys):
    keys, out = sorted(keys), []
    for k in keys:
        if out and out[-1][0] + out[-1][1] == k:
            out[-1][1] += 1
        else:
            out.append([k, 1])
    return out


def pair_ride(shard, blocks):
    rows, cols = shard.shape
    out = jax.ShapeDtypeStruct((rows * blocks, cols), shard.dtype)

    def stages(ins, outs):
        near, far = outs[0].at[pl.ds(0, rows)], outs[0].at[pl.ds(rows, rows)]
        return [[("ring", ins[0], far), ("swap", ins[0], near), ("stay", ins[0], near)]]

    return Ride([shard], [out], stages, ["ring", "swap"], 3)


def spread_ride(buffer, pieces, levels, blocks):
    rows = buffer.shape[0] // blocks
    plan = []
    for level in levels:
        stage = []
        for first, cols, order in pieces:
            held = [0, 1]
            for name, weight in order[:level]:
                held = held + [k + weight for k in held]
            name, weight = order[level]
            for k, n in runs(held):
                stage.append((name, k, k + weight, n, first, cols))
        plan.append(stage)

    def stages(ins, outs):
        ref = outs[0]
        return [
            [
                (name, ref.at[pl.ds(a * rows, n * rows), pl.ds(first, cols)],
                 ref.at[pl.ds(b * rows, n * rows), pl.ds(first, cols)])
                for name, a, b, n, first, cols in stage
            ]
            for stage in plan
        ]

    kinds = [item[0] for stage in plan for item in stage]
    out = jax.ShapeDtypeStruct(buffer.shape, buffer.dtype)
    return Ride([buffer], [out], stages, kinds, sum(len(s) for s in plan), {0: 0})


def chain_ride(shard, pieces, blocks):
    first = pair_ride(shard, blocks)
    rest = spread_ride(first.outs[0], pieces, range(len(pieces[0][2])), blocks)

    def stages(ins, outs):
        return first.stages(ins, outs) + rest.stages(ins, outs)

    return Ride([shard], first.outs, stages, first.kinds + rest.kinds, first.count + rest.count)


def send_ride(value, kind):
    out = jax.ShapeDtypeStruct(value.shape, value.dtype)
    return Ride([value], [out], lambda ins, outs: [[(kind, ins[0], outs[0])]], [kind], 1)


def launch(name, number, main, ins, outs, scratch, kinds, rides, limit=56):
    in_arrays = list(ins)
    out_shapes = list(outs)
    aliases = {}
    spans = []
    for ride in rides:
        for a, b in ride.alias.items():
            aliases[len(in_arrays) + a] = len(out_shapes) + b
        spans.append((len(in_arrays), len(in_arrays) + len(ride.ins),
                      len(out_shapes), len(out_shapes) + len(ride.outs)))
        in_arrays += ride.ins
        out_shapes += ride.outs
    total = sum(r.count for r in rides)
    all_kinds = list(kinds) + [k for r in rides for k in r.kinds]
    ride_sems = [pltpu.SemaphoreType.DMA((max(total, 1),)) for _ in range(2)]

    def kernel(*refs):
        in_refs = refs[: len(in_arrays)]
        out_refs = refs[len(in_arrays) : len(in_arrays) + len(out_shapes)]
        rest = refs[len(in_arrays) + len(out_shapes) :]
        send, recv = rest[:2]
        early = main(in_refs[: len(ins)], out_refs[: len(outs)], rest[2:], True) if main else None
        if all_kinds:
            greet(all_kinds)
        chains, place = [], 0
        for ride, (a, b, c, d) in zip(rides, spans):
            chain = []
            for stage in ride.stages(in_refs[a:b], out_refs[c:d]):
                chain.append([])
                for kind, src, dst in stage:
                    chain[-1].append(Copy(kind, src, dst, send.at[place], recv.at[place]))
                    place += 1
            chains.append(chain)
        for chain in chains:
            for copy in chain[0]:
                copy.start()
        if main:
            main(in_refs[: len(ins)], out_refs[: len(outs)], rest[2:], early)
        for level in range(max([len(c) for c in chains], default=0)):
            for chain in chains:
                if level < len(chain):
                    for copy in chain[level]:
                        copy.wait()
                    if level + 1 < len(chain):
                        for copy in chain[level + 1]:
                            copy.start()

    results = pl.pallas_call(
        kernel,
        out_shape=tuple(out_shapes),
        in_specs=[ANY] * len(in_arrays),
        out_specs=tuple([ANY] * len(out_shapes)),
        scratch_shapes=ride_sems + list(scratch),
        input_output_aliases=aliases,
        name=name,
        compiler_params=pltpu.CompilerParams(
            collective_id=number if all_kinds else None,
            has_side_effects=bool(all_kinds),
            vmem_limit_bytes=limit << 20,
        ),
    )(*in_arrays)
    main_outs = results[: len(outs)]
    return main_outs, [results[c:d] for _, _, c, d in spans]


def normalise_value(rows, gain, shift):
    centre = jnp.mean(rows, axis=-1, keepdims=True)
    centred = rows - centre
    spread = jnp.mean(centred * centred, axis=-1, keepdims=True)
    return (centred * lax.rsqrt(spread + NORM_EPS) * gain + shift).astype(BF16)


def gelu_pair(upper):
    cdf = 0.5 * (1.0 + lax.erf(upper * (0.5**0.5)))
    density = jnp.exp(-0.5 * upper * upper) * (0.5 / jnp.pi) ** 0.5
    return (upper * cdf).astype(BF16), (cdf + upper * density).astype(BF16)


def gather_multiply(number, rows_in, norm, weight, ending, slope, rides):
    size, width = rows_in.shape
    n = weight.shape[1]
    tile = min(TILE, n)
    ins = [rows_in, weight]
    if norm is not None:
        ins.append(jnp.concatenate([norm[0], norm[1]], axis=0))
    if slope is not None:
        ins.append(slope)
    double = ending == "gelu"
    outs = [jax.ShapeDtypeStruct((4, size, width), BF16)]
    outs += [jax.ShapeDtypeStruct((4, size, n), BF16)] * (2 if double else 1)
    half = size // 2
    scratch = [
        pltpu.VMEM((size, width), F32),
        pltpu.VMEM((width, n), BF16),
        pltpu.VMEM((2, width), F32),
        pltpu.VMEM((4, size, width), BF16),
        pltpu.VMEM((4, size, n), BF16),
        pltpu.VMEM((4, size, n) if (double or slope is not None) else (8, 128), BF16),
        pltpu.SemaphoreType.DMA((4,)),
        pltpu.SemaphoreType.DMA((6,)),
        pltpu.SemaphoreType.DMA((6,)),
        pltpu.SemaphoreType.DMA((3, 4)),
    ]

    def main(in_refs, out_refs, refs, stage):
        rows, w, norms, x, y, second, load, send, recv, store = refs
        if stage is True:
            loads = [
                pltpu.make_async_copy(in_refs[0], rows, load.at[0]),
                pltpu.make_async_copy(in_refs[1], w, load.at[1]),
            ]
            if norm is not None:
                loads.append(pltpu.make_async_copy(in_refs[2], norms, load.at[2]))
            if slope is not None:
                loads.append(pltpu.make_async_copy(in_refs[-1], second, load.at[3]))
            for copy in loads:
                copy.start()
            return loads
        loads = stage
        loads[0].wait()
        if norm is not None:
            loads[2].wait()
        over, beside, relay, stores = [], [], [], []
        for h in range(2):
            part = pl.ds(h * half, half)
            value = rows[part, :]
            if norm is not None:
                value = normalise_value(value, norms[0:1, :], norms[1:2, :])
            x[0, part, :] = value.astype(BF16)
            over.append(Copy("zl", x.at[0, part], x.at[2, part], send.at[h], recv.at[h]))
            over[-1].start()
        beside = Copy("c", x.at[0], x.at[1], send.at[2], recv.at[2])
        beside.start()
        loads[1].wait()
        if slope is not None:
            loads[-1].wait()

        def multiply(b):
            def step(j, carry):
                cols = pl.ds(pl.multiple_of(j * tile, tile), tile)
                value = nn(x[b], w[:, cols])
                if double:
                    y[b, :, cols], second[b, :, cols] = gelu_pair(value)
                elif slope is not None:
                    y[b, :, cols] = (value * second[b, :, cols].astype(F32)).astype(BF16)
                else:
                    y[b, :, cols] = value.astype(BF16)
                return carry

            lax.fori_loop(0, n // tile, step, 0)
            done = [pltpu.make_async_copy(x.at[b], out_refs[0].at[b], store.at[0, b]),
                    pltpu.make_async_copy(y.at[b], out_refs[1].at[b], store.at[1, b])]
            if double:
                done.append(pltpu.make_async_copy(second.at[b], out_refs[2].at[b], store.at[2, b]))
            for copy in done:
                copy.start()
            stores.extend(done)

        multiply(0)
        beside.wait()
        multiply(1)
        for h in range(2):
            part = pl.ds(h * half, half)
            over[h].wait()
            relay.append(Copy("c", x.at[2, part], x.at[3, part], send.at[3 + h], recv.at[3 + h]))
            relay[-1].start()
        multiply(2)
        for copy in relay:
            copy.wait()
        multiply(3)
        for copy in stores:
            copy.wait()

    return launch(f"gather_{number}", number, main, ins, outs, scratch, ["c", "zl"], rides)


def multiply_scatter(number, parts, weight, base, norm, fills, rides):
    _, size, n = parts.shape
    width = weight.shape[0]
    half = size // 2
    rows = 4 * size
    ins = [parts.reshape(rows, n), weight] + ([base] if base is not None else [])
    if norm is not None:
        ins += list(norm)
    fill_at = len(ins)
    fill_cols = []
    for a, b in fills:
        ins.append(a)
        if b is not None:
            ins.append(b)
        fill_cols.append(n if b is None else b.shape[1])
    outs = [jax.ShapeDtypeStruct((size, width), F32)]
    if norm is not None:
        outs.append(jax.ShapeDtypeStruct((2, width), F32))
    outs += [jax.ShapeDtypeStruct((width, k), BF16) for k in fill_cols]
    scratch = [
        pltpu.VMEM((rows, n), BF16),
        pltpu.VMEM((width, n), BF16),
        pltpu.VMEM((size, width), F32),
        pltpu.VMEM((size, width), F32),
        pltpu.VMEM((2, size, width), BF16),
        pltpu.VMEM((2, size, width), BF16),
        pltpu.VMEM((size, width), BF16),
        pltpu.VMEM((size, width), BF16),
        pltpu.SemaphoreType.DMA((8,)),
        pltpu.SemaphoreType.DMA((6,)),
        pltpu.SemaphoreType.DMA((6,)),
    ]
    if norm is not None:
        scratch += [
            pltpu.VMEM((size, width), F32),
            pltpu.VMEM((1, width), F32),
            pltpu.VMEM((size, width), F32),
            pltpu.VMEM((2, width), F32),
            pltpu.SemaphoreType.DMA((4,)),
        ]
    for (a, b), k in zip(fills, fill_cols):
        scratch.append(pltpu.VMEM((rows, width), BF16))
        if b is not None:
            scratch.append(pltpu.VMEM((rows, k), BF16))
        scratch += [pltpu.VMEM((width, k), BF16), pltpu.SemaphoreType.DMA((3,))]

    def main(in_refs, out_refs, refs, stage):
        y, w, total, far, give, came, across, over, load, send, recv = refs[:11]
        refs = list(refs[11:])
        if norm is not None:
            stream, gain, back, sums, norm_sem = refs[:5]
            refs = refs[5:]
        if stage is True:
            loads = [pltpu.make_async_copy(in_refs[1], w, load.at[0])]
            loads += [
                pltpu.make_async_copy(
                    in_refs[0].at[pl.ds(b * size, size)], y.at[pl.ds(b * size, size)],
                    load.at[1 + b])
                for b in range(4)
            ]
            if base is not None:
                loads.append(pltpu.make_async_copy(in_refs[2], total, load.at[5]))
            for place in (0, 4, 3, 2, 1, 5)[: len(loads)]:
                loads[place].start()
            others = []
            if norm is not None:
                at = 3 if base is not None else 2
                for i, ref in enumerate((stream, gain, back)):
                    others.append(pltpu.make_async_copy(in_refs[at + i], ref, norm_sem.at[i]))
            at = fill_at
            for a, b in fills:
                others.append(pltpu.make_async_copy(in_refs[at], refs[0], refs[2 if b is None else 3].at[0]))
                at += 1
                if b is not None:
                    others.append(pltpu.make_async_copy(in_refs[at], refs[1], refs[3].at[1]))
                    at += 1
                refs = refs[3 if b is None else 4 :]
            for copy in others:
                copy.start()
            return loads, others
        loads, others = stage

        def multiply(b, part, count, put):
            def step(j, carry):
                cols = pl.ds(pl.multiple_of(j * TILE, TILE), TILE)
                put(cols, nt(y[pl.ds(b * size + part, count), :], w[cols, :]))
                return carry

            lax.fori_loop(0, width // TILE, step, 0)

        for place in (0, 4, 3):
            loads[place].wait()
        sent = []
        for h in range(2):
            part = pl.ds(h * half, half)

            def put_give(cols, value, part=part):
                give[0, part, cols] = value.astype(BF16)

            def put_far(cols, value, part=part):
                far[part, cols] = value

            multiply(3, h * half, half, put_give)
            copy = Copy("c", give.at[0, part], came.at[0, part], send.at[h], recv.at[h])
            copy.start()
            multiply(2, h * half, half, put_far)
            copy.wait()
            across[part, :] = (far[part, :] + came[0, part, :].astype(F32)).astype(BF16)
            copy = Copy("zl", across.at[part], over.at[part], send.at[2 + h], recv.at[2 + h])
            copy.start()
            sent.append(copy)
        loads[2].wait()

        def put_near(cols, value):
            give[1, :, cols] = value.astype(BF16)

        multiply(1, 0, size, put_near)
        near = Copy("c", give.at[1], came.at[1], send.at[4], recv.at[4])
        near.start()
        loads[1].wait()
        if base is not None:
            loads[5].wait()

        def put_total(cols, value):
            total[:, cols] = value + (total[:, cols] if base is not None else 0.0)

        multiply(0, 0, size, put_total)
        for copy in others:
            copy.wait()
        stores = []
        fill_refs = refs
        for k, (a, b) in enumerate(fills):
            if b is None:
                left, result, sem = fill_refs[:3]
                right, fill_refs = y, fill_refs[3:]
            else:
                left, right, result, sem = fill_refs[:4]
                fill_refs = fill_refs[4:]
            count = fill_cols[k]
            wide = min(768, count)
            if count % wide:
                wide = count

            def step(j, carry, left=left, right=right, result=result, wide=wide, count=count):
                rows_ = pl.ds(pl.multiple_of(j * 256, 256), 256)
                turned = left[:, rows_].T
                for q in range(count // wide):
                    cols = slice(q * wide, (q + 1) * wide)
                    result[rows_, cols] = nn(turned, right[:, cols]).astype(BF16)
                return carry

            lax.fori_loop(0, width // 256, step, 0)
            where = len(outs) - len(fills) + k
            stores.append(pltpu.make_async_copy(result, out_refs[where], sem.at[2]))
            stores[-1].start()
        near.wait()
        total[...] += came[1].astype(F32)
        for h in range(2):
            part = pl.ds(h * half, half)
            sent[h].wait()
            total[part, :] += over[part, :].astype(F32)
            if norm is not None:
                value = total[part, :]
                rows_in = stream[part, :]
                centred = rows_in - jnp.mean(rows_in, axis=-1, keepdims=True)
                inverse = lax.rsqrt(jnp.mean(centred * centred, axis=-1, keepdims=True) + NORM_EPS)
                unit = centred * inverse
                gain_sum = jnp.sum(value * unit, axis=0, keepdims=True)
                shift_sum = jnp.sum(value, axis=0, keepdims=True)
                sums[0:1, :] = gain_sum if h == 0 else sums[0:1, :] + gain_sum
                sums[1:2, :] = shift_sum if h == 0 else sums[1:2, :] + shift_sum
                scaled = value * gain[...]
                total[part, :] = back[part, :] + inverse * (
                    scaled
                    - jnp.mean(scaled, axis=-1, keepdims=True)
                    - unit * jnp.mean(scaled * unit, axis=-1, keepdims=True)
                )
            copy = pltpu.make_async_copy(total.at[part], out_refs[0].at[part], load.at[6 + h])
            copy.start()
            stores.append(copy)
        if norm is not None:
            copy = pltpu.make_async_copy(sums, out_refs[1], norm_sem.at[3])
            copy.start()
            stores.append(copy)
        for copy in stores:
            copy.wait()

    return launch(f"scatter_{number}", number, main, ins, outs, scratch, ["c", "zl"], rides)


def place_of(i):
    c, zl = lax.axis_index("c"), lax.axis_index("zl")
    dc, dz = i // 2, i % 2
    return (c + dc) % 2 + 2 * ((zl + dz) % 2)


def head_only(value, u):
    lane = lax.broadcasted_iota(jnp.int32, value.shape, 1)
    keep = (lane < HEAD_DIM) if u == 0 else (lane >= HEAD_DIM)
    return jnp.where(keep, value, jnp.zeros_like(value))


def masked(scores):
    key = lax.broadcasted_iota(jnp.int32, scores.shape, 0)
    query = lax.broadcasted_iota(jnp.int32, scores.shape, 1)
    return jnp.where(key <= query, scores, MASKED)


def softmax_parts(parts, value_rows):
    top = parts[0].max(axis=0, keepdims=True)
    for scores in parts[1:]:
        top = jnp.maximum(top, scores.max(axis=0, keepdims=True))
    total, mixed = 0.0, 0.0
    for scores, values in zip(parts, value_rows):
        expo = jnp.exp(scores - top)
        total = total + expo.sum(axis=0, keepdims=True)
        mixed = mixed + nn(values, expo.astype(BF16))
    return mixed / total, top + jnp.log(total)


def softmax_back(scores, slopes, logsum):
    probs = [jnp.exp(s - logsum) for s in scores]
    inner = 0.0
    for p, d in zip(probs, slopes):
        inner = inner + (p * d).sum(axis=0, keepdims=True)
    return [p.astype(BF16) for p in probs], [
        (p * (d - inner)).astype(BF16) for p, d in zip(probs, slopes)
    ]


def attend_self(number, proj, scale, rides):
    _, size, wide = proj.shape
    cols = wide // 3
    frames, heads = 4 * size, cols // HEAD_DIM
    outs = [jax.ShapeDtypeStruct((4, size, cols), BF16), jax.ShapeDtypeStruct((heads, frames), F32)]
    scratch = [
        pltpu.VMEM((4, size, wide), BF16),
        pltpu.VMEM((frames, 128), BF16),
        pltpu.VMEM((128, frames), BF16),
        pltpu.VMEM((4, size, cols), BF16),
        pltpu.VMEM((heads, frames), F32),
        pltpu.SemaphoreType.DMA((3,)),
    ]

    def main(in_refs, out_refs, refs, stage):
        x, keys, values, out, logs, sem = refs
        if stage is True:
            copy = pltpu.make_async_copy(in_refs[0], x, sem.at[0])
            copy.start()
            return copy
        stage.wait()
        for g in range(cols // 128):
            lanes = [pl.ds(part * cols + g * 128, 128) for part in range(3)]
            for i in range(4):
                rows = pl.ds(i * size, size)
                keys[rows, :] = x[place_of(i), :, lanes[1]]
                values[:, rows] = x[place_of(i), :, lanes[2]].T
            for i in range(4):
                query = x[place_of(i), :, lanes[0]]
                before = i * size
                done = []
                for u in range(2):
                    q = head_only(query, u)
                    mine = pl.ds(u * HEAD_DIM, HEAD_DIM)
                    parts = [masked(nt(keys[pl.ds(before, size), :], q) * scale)]
                    rows = [values[mine, pl.ds(before, size)]]
                    if i:
                        parts.append(nt(keys[pl.ds(0, before), :], q) * scale)
                        rows.append(values[mine, pl.ds(0, before)])
                    mixed, logsum = softmax_parts(parts, rows)
                    done.append(mixed)
                    logs[pl.ds(2 * g + u, 1), pl.ds(before, size)] = logsum
                joined = jnp.concatenate(done, axis=0).T
                out[place_of(i), :, pl.ds(g * 128, 128)] = joined.astype(BF16)
        copies = [pltpu.make_async_copy(out, out_refs[0], sem.at[1]),
                  pltpu.make_async_copy(logs, out_refs[1], sem.at[2])]
        for copy in copies:
            copy.start()
        for copy in copies:
            copy.wait()

    return launch(f"attend_{number}", number, main, [proj], outs, scratch, [], rides)


def attend_self_back(number, proj, grad_joined, logsum, scale, rides):
    _, size, wide = proj.shape
    cols = wide // 3
    frames, heads = 4 * size, cols // HEAD_DIM
    outs = [jax.ShapeDtypeStruct((4, size, wide), BF16)]
    scratch = [
        pltpu.VMEM((4, size, wide), BF16),
        pltpu.VMEM((4, size, cols), BF16),
        pltpu.VMEM((heads, frames), F32),
        pltpu.VMEM((frames, 128), BF16),
        pltpu.VMEM((128, frames), BF16),
        pltpu.VMEM((frames, 128), BF16),
        pltpu.VMEM((frames, 128), F32),
        pltpu.VMEM((frames, 128), F32),
        pltpu.VMEM((4, size, wide), BF16),
        pltpu.SemaphoreType.DMA((4,)),
    ]

    def main(in_refs, out_refs, refs, stage):
        x, grads, logs, keys, keys_t, values, grad_k, grad_v, out, sem = refs
        if stage is True:
            copies = [
                pltpu.make_async_copy(in_refs[i], ref, sem.at[i])
                for i, ref in enumerate((x, grads, logs))
            ]
            for copy in copies:
                copy.start()
            return copies
        for copy in stage:
            copy.wait()
        for g in range(cols // 128):
            lanes = [pl.ds(part * cols + g * 128, 128) for part in range(3)]
            for i in range(4):
                rows = pl.ds(i * size, size)
                keys[rows, :] = x[place_of(i), :, lanes[1]]
                keys_t[:, rows] = x[place_of(i), :, lanes[1]].T
                values[rows, :] = x[place_of(i), :, lanes[2]]
            grad_k[...] = jnp.zeros_like(grad_k)
            grad_v[...] = jnp.zeros_like(grad_v)
            for i in range(4):
                query = x[place_of(i), :, lanes[0]]
                grad = grads[place_of(i), :, lanes[0]]
                before = i * size
                spans = [pl.ds(before, size)] + ([pl.ds(0, before)] if i else [])
                done = []
                for u in range(2):
                    q, go = head_only(query, u), head_only(grad, u)
                    mine = pl.ds(u * HEAD_DIM, HEAD_DIM)
                    scores = [nt(keys[span, :], q) * scale for span in spans]
                    scores[0] = masked(scores[0])
                    slopes = [nt(values[span, :], go) for span in spans]
                    probs, grad_scores = softmax_back(
                        scores, slopes, logs[pl.ds(2 * g + u, 1), pl.ds(before, size)])
                    grad_q = 0.0
                    for span, p, d in zip(spans, probs, grad_scores):
                        grad_v[span, :] += nn(p, go)
                        grad_k[span, :] += nn(d, q)
                        grad_q = grad_q + nn(keys_t[mine, span], d)
                    done.append(grad_q)
                grad_q = jnp.concatenate(done, axis=0).T * scale
                out[place_of(i), :, lanes[0]] = grad_q.astype(BF16)
            for i in range(4):
                rows = pl.ds(i * size, size)
                out[place_of(i), :, lanes[1]] = (grad_k[rows, :] * scale).astype(BF16)
                out[place_of(i), :, lanes[2]] = grad_v[rows, :].astype(BF16)
        copy = pltpu.make_async_copy(out, out_refs[0], sem.at[3])
        copy.start()
        copy.wait()

    return launch(f"attend_back_{number}", number, main, [proj, grad_joined, logsum], outs, scratch,
                  [], rides)


def attend_cross(number, query, pairs, scale, rides):
    _, size, cols = query.shape
    frames, heads, text = 4 * size, cols // HEAD_DIM, pairs.shape[0]
    outs = [jax.ShapeDtypeStruct((4, size, cols), BF16), jax.ShapeDtypeStruct((heads, frames), F32)]
    scratch = [
        pltpu.VMEM((4, size, cols), BF16),
        pltpu.VMEM((text, 2 * cols), BF16),
        pltpu.VMEM((4, size, cols), BF16),
        pltpu.VMEM((heads, frames), F32),
        pltpu.SemaphoreType.DMA((4,)),
    ]

    def main(in_refs, out_refs, refs, stage):
        x, kv, out, logs, sem = refs
        if stage is True:
            copies = [pltpu.make_async_copy(in_refs[0], x, sem.at[0]),
                      pltpu.make_async_copy(in_refs[1], kv, sem.at[1])]
            for copy in copies:
                copy.start()
            return copies
        for copy in stage:
            copy.wait()
        for g in range(cols // 128):
            lanes = pl.ds(g * 128, 128)
            keys = kv[:, lanes]
            values = kv[:, pl.ds(cols + g * 128, 128)].T
            for i in range(4):
                rows = x[i, :, lanes]
                done = []
                for u in range(2):
                    scores = nt(keys, head_only(rows, u)) * scale
                    mixed, logsum = softmax_parts(
                        [scores], [values[u * HEAD_DIM : (u + 1) * HEAD_DIM, :]])
                    done.append(mixed)
                    logs[pl.ds(2 * g + u, 1), pl.ds(i * size, size)] = logsum
                out[i, :, lanes] = jnp.concatenate(done, axis=0).T.astype(BF16)
        copies = [pltpu.make_async_copy(out, out_refs[0], sem.at[2]),
                  pltpu.make_async_copy(logs, out_refs[1], sem.at[3])]
        for copy in copies:
            copy.start()
        for copy in copies:
            copy.wait()

    return launch(f"cross_{number}", number, main, [query, pairs], outs, scratch, [], rides)


def attend_cross_back(number, query, pairs, grad_joined, logsum, scale, rides):
    _, size, cols = query.shape
    frames, heads, text = 4 * size, cols // HEAD_DIM, pairs.shape[0]
    outs = [jax.ShapeDtypeStruct((4, size, cols), BF16),
            jax.ShapeDtypeStruct((text, 2 * cols), BF16)]
    scratch = [
        pltpu.VMEM((4, size, cols), BF16),
        pltpu.VMEM((text, 2 * cols), BF16),
        pltpu.VMEM((4, size, cols), BF16),
        pltpu.VMEM((heads, frames), F32),
        pltpu.VMEM((4, size, cols), BF16),
        pltpu.VMEM((text, 2 * cols), BF16),
        pltpu.SemaphoreType.DMA((6,)),
    ]

    def main(in_refs, out_refs, refs, stage):
        x, kv, grads, logs, out, out_kv, sem = refs
        if stage is True:
            copies = [
                pltpu.make_async_copy(in_refs[i], ref, sem.at[i])
                for i, ref in enumerate((x, kv, grads, logs))
            ]
            for copy in copies:
                copy.start()
            return copies
        for copy in stage:
            copy.wait()
        for g in range(cols // 128):
            lanes, lanes_v = pl.ds(g * 128, 128), pl.ds(cols + g * 128, 128)
            keys, values = kv[:, lanes], kv[:, lanes_v]
            keys_t = keys.T
            grad_k, grad_v = 0.0, 0.0
            for i in range(4):
                done = []
                for u in range(2):
                    q, go = head_only(x[i, :, lanes], u), head_only(grads[i, :, lanes], u)
                    scores = nt(keys, q) * scale
                    probs, grad_scores = softmax_back(
                        [scores], [nt(values, go)],
                        logs[pl.ds(2 * g + u, 1), pl.ds(i * size, size)])
                    grad_v = grad_v + nn(probs[0], go)
                    grad_k = grad_k + nn(grad_scores[0], q)
                    done.append(nn(keys_t[u * HEAD_DIM : (u + 1) * HEAD_DIM, :], grad_scores[0]))
                out[i, :, lanes] = (jnp.concatenate(done, axis=0).T * scale).astype(BF16)
            out_kv[:, lanes] = (grad_k * scale).astype(BF16)
            out_kv[:, lanes_v] = grad_v.astype(BF16)
        copies = [pltpu.make_async_copy(out, out_refs[0], sem.at[4]),
                  pltpu.make_async_copy(out_kv, out_refs[1], sem.at[5])]
        for copy in copies:
            copy.start()
        for copy in copies:
            copy.wait()

    return launch(f"cross_back_{number}", number, main, [query, pairs, grad_joined, logsum], outs,
                  scratch, [], rides)


def flat(parts):
    return parts.reshape(-1, parts.shape[-1])


def body(bits, frames_in, text_states, ln_gain, ln_bias, w_self, w_self_out, w_cross_q,
         w_cross_kv, w_cross_out, w_up, w_down, cotangent):
    scale = float(HEAD_DIM) ** (-0.5)
    layers = w_self.shape[0]
    width = frames_in.shape[2]
    part = w_self.shape[1]
    blocks = width // part
    cols = w_self.shape[3]
    hidden = w_up.shape[2]
    me = lax.axis_index("zh")
    for place, name in enumerate(reversed(bits)):
        me = me + (lax.axis_index(name) << (place + 1))

    row = lax.broadcasted_iota(jnp.int32, (width, width), 0)
    col = lax.broadcasted_iota(jnp.int32, (width, width), 1)
    permute = ((row // part == ((col // part) ^ me)) & (row % part == col % part)).astype(BF16)

    def reorder(value):
        return nn(value, permute)

    up = [(name, 2 << (len(bits) - 1 - place)) for place, name in enumerate(bits)]
    low_first = list(reversed(up))
    levels = len(bits)
    early, late = list(range(levels // 2)), list(range(levels // 2, levels))
    sizes = {"self": 3 * cols, "self_out": cols, "q": cols, "kv": 2 * cols, "out": cols,
             "up": hidden, "down": hidden, "norm": 128}

    def halves(name):
        n = sizes[name]
        if name in ("self", "up", "down"):
            first = (n // 2 + 127) // 128 * 128
            return [(0, first, low_first), (first, n - first, up)]
        return [(0, n, low_first if name in ("kv", "norm") else up)]

    packs = {"a": ["self"], "o": ["self_out"], "b": ["q", "kv", "out"], "c": ["up"], "d": ["down"]}
    norm_rows = jnp.concatenate([ln_gain.reshape(-1, part), ln_bias.reshape(-1, part)], axis=0).T
    norm_rows = jnp.pad(norm_rows, ((0, 0), (0, sizes["norm"] - norm_rows.shape[1])))
    shards = {(0, "norm"): norm_rows}
    for l in range(layers):
        shards[l, "self"] = w_self[l].reshape(part, 3 * cols)
        shards[l, "self_out"] = w_self_out[l].T
        shards[l, "q"] = w_cross_q[l]
        shards[l, "kv"] = w_cross_kv[l].reshape(part, 2 * cols)
        shards[l, "out"] = w_cross_out[l].T
        shards[l, "up"] = w_up[l]
        shards[l, "down"] = w_down[l].T
    held = {}
    counter = [0]

    def number():
        counter[0] += 1
        return counter[0] - 1

    def weight_rides(todo):
        rides, keys = [], []
        for l, pack, stage in todo:
            for name in packs[pack]:
                key = (l, name)
                if stage == 1:
                    rides.append(pair_ride(shards[key], blocks))
                else:
                    which = {2: early, 3: late, 4: early + late}[stage]
                    rides.append(spread_ride(held[key], halves(name), which, blocks))
                keys.append(key)
        return rides, keys

    def keep(keys, extra):
        for key, value in zip(keys, extra):
            held[key] = value[0]

    forward = {
        0: [(0, "o", 4), (0, "b", 1)],
        1: [(0, "b", 2)],
        2: [(0, "b", 3), (0, "c", 1)],
        3: [(0, "c", 2), (0, "d", 1)],
        5: [(0, "c", 3), (0, "d", 2), (1, "a", 1)],
        6: [(0, "d", 3), (1, "a", 2), (1, "o", 1)],
        7: [(1, "a", 3), (1, "o", 2), (1, "b", 1)],
        8: [(1, "o", 3), (1, "b", 2), (1, "c", 1)],
        9: [(1, "b", 3)],
        10: [(1, "c", 2), (1, "d", 1)],
        11: [(1, "c", 3)],
        13: [(1, "d", 2)],
        14: [(1, "d", 3)],
    }
    step = [0]

    def next_rides():
        todo = [t for t in forward.get(step[0], []) if t[0] < layers]
        step[0] += 1
        return weight_rides(todo)

    def move(rides):
        return launch(f"move_{counter[0]}", number(), None, [], [], [], [], rides)[1]

    extra = move([
        chain_ride(shards[0, "self"], halves("self"), blocks),
        chain_ride(shards[0, "norm"], halves("norm"), blocks),
        send_ride(frames_in[0], "swap"),
        send_ride(text_states[0], "c"),
        pair_ride(shards[0, "self_out"], blocks),
    ])
    held[0, "self"], norms, frames_far, text_far, held[0, "self_out"] = [e[0] for e in extra]
    stream = reorder(jnp.where(diagonal(), frames_in[0], frames_far))
    text_own = reorder(jnp.where(diagonal(), text_states[0], text_far)).astype(BF16)
    norms = norms.astype(F32).T
    gains = norms[: 3 * layers].reshape(layers, 3, 1, width)
    shifts = norms[3 * layers : 6 * layers].reshape(layers, 3, 1, width)

    def riding(call, more=()):
        rides, keys = next_rides()
        outs, extra = call(rides + list(more))
        keep(keys, extra)
        return outs, [e[0] for e in extra[len(keys):]]

    records = []
    for l in range(layers):
        saved = {"one": stream}
        more = [send_ride(cotangent[0], "swap")] if l == layers - 1 else []
        (first, proj), extra = riding(lambda r: gather_multiply(
            number(), stream, (gains[l, 0], shifts[l, 0]), held[l, "self"], None, None, r), more)
        if more:
            cot_own = jnp.where(diagonal(), cotangent[0], extra[0])
        (joined, logsum), _ = riding(lambda r: attend_self(number(), proj, scale, r))
        (stream,), _ = riding(lambda r: multiply_scatter(
            number(), joined, held[l, "self_out"], stream, None, [], r))
        saved.update(first=first, proj=proj, joined_self=joined, logsum_self=logsum, two=stream)

        (second, query), _ = riding(lambda r: gather_multiply(
            number(), stream, (gains[l, 1], shifts[l, 1]), held[l, "q"], None, None, r))
        pairs = nn(text_own, held[l, "kv"]).astype(BF16)
        (joined, logsum), _ = riding(lambda r: attend_cross(number(), query, pairs, scale, r))
        (stream,), _ = riding(lambda r: multiply_scatter(
            number(), joined, held[l, "out"], stream, None, [], r))
        saved.update(second=second, query=query, pairs=pairs, joined_cross=joined,
                     logsum_cross=logsum, three=stream)

        (third, active, slope), _ = riding(lambda r: gather_multiply(
            number(), stream, (gains[l, 2], shifts[l, 2]), held[l, "up"], "gelu", None, r))
        (stream,), _ = riding(lambda r: multiply_scatter(
            number(), active, held[l, "down"], stream, None, [], r))
        saved.update(third=third, active=active, slope=slope)
        records.append(saved)
    result_own = reorder(stream.astype(BF16)).astype(BF16)
    grad = reorder(cot_own)

    folding = []
    finished = {}
    grad_text = jnp.zeros((text_own.shape[0], width), F32)
    norm_grads = {}

    def fold_later(l, name, value):
        value = value.astype(BF16)
        for first, n, order in halves(name):
            chunk = value[:, first : first + n] if n != value.shape[1] else value
            table = {k: chunk[k * part : (k + 1) * part] for k in range(blocks)}
            folding.append({"key": (l, name, first), "table": table,
                            "order": list(reversed(order)), "level": 0})

    def fold_start(limit):
        rides, items, spent = [], [], {}
        for item in folding:
            if item["level"] < len(item["order"]):
                name, weight = item["order"][item["level"]]
                away = sorted(k for k in item["table"] if k & weight)
                bytes_ = sum(item["table"][k].size for k in away) * 2
                if spent.get(name, 0) and spent[name] + bytes_ > limit:
                    continue
                value = jnp.concatenate([item["table"][k] for k in away], axis=0)
                rides.append(send_ride(value, name))
            else:
                name = "pair"
                near, far = item["table"][0], item["table"][1]
                bytes_ = near.size * 4
                if spent.get(name, 0) and spent[name] + bytes_ > limit // 2:
                    continue
                rides.append(Ride(
                    [near, far],
                    [jax.ShapeDtypeStruct(near.shape, BF16)] * 2,
                    lambda ins, outs: [[("swap", ins[0], outs[0]), ("back", ins[1], outs[1])]],
                    ["swap", "back"], 2,
                ))
            spent[name] = spent.get(name, 0) + bytes_
            items.append(item)
        return rides, items

    def fold_end(items, extra):
        for item, came in zip(items, extra):
            if item["level"] < len(item["order"]):
                name, weight = item["order"][item["level"]]
                stay = sorted(k for k in item["table"] if not k & weight)
                item["table"] = {
                    k: (
                        item["table"][k].astype(F32)
                        + came[0][i * part : (i + 1) * part].astype(F32)
                    ).astype(BF16)
                    for i, k in enumerate(stay)
                }
                item["level"] += 1
            else:
                near = jnp.where(diagonal(), item["table"][0], came[0])
                finished[item["key"]] = near.astype(F32) + came[1].astype(F32)
                folding.remove(item)

    def folds(call, more=(), limit=LINK_BYTES):
        rides, items = fold_start(limit)
        outs, extra = call(rides + list(more))
        fold_end(items, extra)
        return outs, [e[0] for e in extra[len(items):]]

    text_parts = []
    for l in reversed(range(layers)):
        saved = records[l]
        more = [send_ride(result_own, "swap")] if l == layers - 1 else []
        (full, grad_upper), extra = folds(lambda r: gather_multiply(
            number(), grad, None, held[l, "down"], None, saved["slope"], r), more)
        if more:
            result = jnp.where(diagonal(), result_own, extra[0])
        (grad, norm_grads[l, 2], down, up_), _ = folds(lambda r: multiply_scatter(
            number(), grad_upper, held[l, "up"], None, (saved["three"], gains[l, 2], grad),
            [(flat(full), flat(saved["active"])), (flat(saved["third"]), None)], r))
        fold_later(l, "down", down)
        fold_later(l, "up", up_)

        (full, grad_joined), _ = folds(lambda r: gather_multiply(
            number(), grad, None, held[l, "out"], None, None, r))
        (grad_query, grad_pairs), _ = folds(lambda r: attend_cross_back(
            number(), saved["query"], saved["pairs"], grad_joined, saved["logsum_cross"], scale,
            r), limit=LINK_BYTES // 4)
        grad_text = grad_text + nt(grad_pairs, held[l, "kv"])
        fold_later(l, "kv", tn(text_own, grad_pairs))
        (grad, norm_grads[l, 1], out_, q_), _ = folds(lambda r: multiply_scatter(
            number(), grad_query, held[l, "q"], None, (saved["two"], gains[l, 1], grad),
            [(flat(full), flat(saved["joined_cross"])), (flat(saved["second"]), None)], r))
        fold_later(l, "out", out_)
        fold_later(l, "q", q_)

        more = [send_ride(grad_text.astype(BF16), "c")] if l == 0 else []
        (full, grad_joined), extra = folds(lambda r: gather_multiply(
            number(), grad, None, held[l, "self_out"], None, None, r), more)
        if more:
            grad_text = grad_text.astype(BF16).astype(F32) + extra[0].astype(F32)
        (grad_proj,), _ = folds(lambda r: attend_self_back(
            number(), saved["proj"], grad_joined, saved["logsum_self"], scale, r))
        more = [send_ride(grad_text.astype(BF16), "zl")] if l == 0 else []
        (grad, norm_grads[l, 0], out_, self_), extra = folds(lambda r: multiply_scatter(
            number(), grad_proj, held[l, "self"], None, (saved["one"], gains[l, 0], grad),
            [(flat(full), flat(saved["joined_self"])), (flat(saved["first"]), None)], r), more)
        if more:
            grad_text = grad_text.astype(BF16).astype(F32) + extra[0].astype(F32)
        fold_later(l, "self_out", out_)
        fold_later(l, "self", self_)

    small = [norm_grads[l, j][k] for l in range(layers) for k in range(2) for j in range(3)]
    small = jnp.stack(small, axis=1)
    small = jnp.pad(small, ((0, 0), (0, sizes["norm"] - small.shape[1])))
    fold_later(0, "norm", small)
    frames_back = reorder(grad.astype(BF16)).astype(BF16)
    text_back = reorder(grad_text.astype(BF16)).astype(BF16)
    extras = [send_ride(frames_back, "swap"), send_ride(text_back, "swap")]
    while folding:
        rides, items = fold_start(1 << 40)
        extra = move(rides + extras)
        fold_end(items, extra)
        if extras:
            grad_frames, text_sum = [
                jnp.where(diagonal(), mine, came[0]).astype(F32)
                for mine, came in zip((frames_back, text_back), extra[len(items):])
            ]
            extras = []

    small = finished[0, "norm", 0][:, : 6 * layers]
    for name in ("zl", "zh"):
        small = small + flip(small, name)
    small = small.T.reshape(layers, 6, part)

    def gradient(l, name):
        pieces = [finished[l, name, first] for first, _, _ in halves(name)]
        return jnp.concatenate(pieces, axis=1) if len(pieces) > 1 else pieces[0]

    def stacked(name, shape=None, turned=False):
        members = [gradient(l, name) for l in range(layers)]
        if turned:
            members = [m.T for m in members]
        if shape is not None:
            members = [m.reshape(shape) for m in members]
        return jnp.stack(members)

    return (
        result[None],
        grad_frames[None],
        text_sum[None],
        small[:, :3],
        small[:, 3:],
        stacked("self", (part, 3, cols)),
        stacked("self_out", turned=True),
        stacked("q"),
        stacked("kv", (part, 2, cols)),
        stacked("out", turned=True),
        stacked("up"),
        stacked("down", turned=True),
    )


def solution(mesh):
    count = mesh.shape["dp"]
    bits = tuple(f"b{i}" for i in range(count.bit_length() - 2))
    dp = (*bits, "c")
    tensor = ("zh", "zl")
    inner = Mesh(mesh.devices.reshape((2,) * (len(bits) + 3)), (*dp, *tensor))
    return jax.shard_map(
        functools.partial(body, bits),
        mesh=inner,
        in_specs=(
            P(dp, tensor, None),
            P(dp, None, None),
            P(None, None, dp),
            P(None, None, dp),
            P(None, dp, None, tensor),
            P(None, tensor, dp),
            P(None, dp, tensor),
            P(None, dp, None, tensor),
            P(None, tensor, dp),
            P(None, dp, tensor),
            P(None, tensor, dp),
            P(dp, tensor, None),
        ),
        out_specs=(
            P(dp, tensor, None),
            P(dp, tensor, None),
            P(dp, None, None),
            P(None, None, dp),
            P(None, None, dp),
            P(None, dp, None, tensor),
            P(None, tensor, dp),
            P(None, dp, tensor),
            P(None, dp, None, tensor),
            P(None, tensor, dp),
            P(None, dp, tensor),
            P(None, tensor, dp),
        ),
        check_vma=False,
    )
```

```python
import functools
import jax
import jax.numpy as jnp
from jax import lax
from jax.experimental import pallas as pl
from jax.experimental.pallas import tpu as pltpu
from jax.sharding import Mesh, PartitionSpec as P

HEAD_DIM = 64
NORM_EPS = 1e-05
MASKED = -1e30
TILE = 384
F32 = jnp.float32
BF16 = jnp.bfloat16
MESH = pl.DeviceIdType.MESH
ANY = pl.BlockSpec(memory_space=pl.ANY)


def nn(a, b):
    return lax.dot_general(a, b, (((1,), (0,)), ((), ())), preferred_element_type=F32)


def nt(a, b):
    return lax.dot_general(a, b, (((1,), (1,)), ((), ())), preferred_element_type=F32)


def tn(a, b):
    return lax.dot_general(a, b, (((0,), (0,)), ((), ())), preferred_element_type=F32)


def flip(value, axis):
    return lax.ppermute(value, axis, [(0, 1), (1, 0)])


def diagonal():
    return lax.axis_index("c") == lax.axis_index("zh")


def off_diagonal():
    return lax.rem(lax.axis_index("c") + lax.axis_index("zh"), 2)


def target(kind):
    c, zh = lax.axis_index("c"), lax.axis_index("zh")
    off = off_diagonal()
    if kind == "ring":
        return {"c": lax.rem(c + off, 2), "zh": lax.rem(zh + 1 + off, 2)}
    if kind == "back":
        return {"c": lax.rem(c + 1 + off, 2), "zh": lax.rem(zh + off, 2)}
    if kind == "swap":
        return {"c": 1 - c, "zh": 1 - zh}
    return {kind: 1 - lax.axis_index(kind)}


def greeted(kinds):
    names = []
    for kind in kinds:
        pairs = {"ring": [("c",), ("zh",)], "back": [("c",), ("zh",)],
                 "swap": [("c", "zh")], "stay": []}.get(kind, [(kind,)])
        names += [p for p in pairs if p not in names]
    return names


def greet(kinds):
    barrier = pltpu.get_barrier_semaphore()
    names = greeted(kinds)
    for group in names:
        pl.semaphore_signal(
            barrier, inc=1, device_id={n: 1 - lax.axis_index(n) for n in group},
            device_id_type=MESH,
        )
    pl.semaphore_wait(barrier, len(names))


class Copy:
    def __init__(self, kind, src, dst, send, recv):
        self.kind = kind
        if kind == "stay":
            self.copy = pltpu.make_async_copy(src, dst, send)
        else:
            self.copy = pltpu.make_async_remote_copy(
                src_ref=src, dst_ref=dst, send_sem=send, recv_sem=recv,
                device_id=target(kind), device_id_type=MESH,
            )

    def guarded(self, act):
        if self.kind == "swap":
            pl.when(off_diagonal() == 1)(act)
        elif self.kind == "stay":
            pl.when(off_diagonal() == 0)(act)
        else:
            act()

    def start(self):
        self.guarded(lambda: self.copy.start())

    def wait(self):
        self.guarded(lambda: self.copy.wait())


class Ride:
    def __init__(self, ins, outs, stages, kinds, count, alias=()):
        self.ins, self.outs, self.stages = list(ins), list(outs), stages
        self.kinds, self.alias = list(kinds), dict(alias)
        self.scratch = [pltpu.SemaphoreType.DMA((count,)), pltpu.SemaphoreType.DMA((count,))]

    def chain(self, ins, outs, refs):
        return Chain(self.stages(ins, outs), *refs)


class Chain:
    def __init__(self, stages, send, recv):
        self.copies, place = [], 0
        for stage in stages:
            self.copies.append([])
            for kind, src, dst in stage:
                self.copies[-1].append(Copy(kind, src, dst, send.at[place], recv.at[place]))
                place += 1
        self.level, self.levels = 0, len(self.copies)

    def start(self):
        for copy in self.copies[0]:
            copy.start()

    def step(self):
        for copy in self.copies[self.level]:
            copy.wait()
        self.level += 1
        if self.level < self.levels:
            for copy in self.copies[self.level]:
                copy.start()


class Fold(Ride):
    def __init__(self, grad, first, cols, order, blocks, came=None, sums=()):
        self.rows, self.first, self.cols = grad.shape[0] // blocks, first, cols
        self.order, self.came, self.sums = order, came, list(sums)
        rows, half = self.rows, grad.shape[0] // 2
        keys = list(range(blocks))
        self.away0 = [k for k in keys if k & order[0][1]]
        self.held = [k for k in keys if not k & order[0][1]]
        self.ins = [grad] + ([came] if came is not None else [])
        self.outs = [jax.ShapeDtypeStruct((rows, cols), F32)]
        self.alias = {}
        self.kinds = [name for name, _ in order[0 if came is None else 1 :]]
        self.kinds += ["swap", "back"] + self.sums
        self.scratch = [pltpu.VMEM((half, cols), BF16), pltpu.VMEM((half, cols), BF16)]
        for level in range(1, len(order)):
            self.scratch.append(pltpu.VMEM((half >> level, cols), BF16))
        self.scratch += [
            pltpu.VMEM((2 * rows, cols), BF16),
            pltpu.VMEM((1 + len(self.sums), rows, cols), F32),
            pltpu.SemaphoreType.DMA((blocks + 2,)),
            pltpu.SemaphoreType.DMA((blocks * 2 + 4,)),
            pltpu.SemaphoreType.DMA((blocks * 2 + 4,)),
        ]
        self.levels = len(order) + 2 + len(self.sums)

    def chain(self, ins, outs, refs):
        self.in_refs, self.out = ins, outs[0]
        self.own, self.got = refs[0], list(refs[1 : 1 + len(self.order)])
        self.pair, self.total, self.load, self.send, self.recv = refs[1 + len(self.order) :]
        self.level, self.place, self.live = 0, 0, None
        return self

    def remote(self, kind, src, dst):
        copy = Copy(kind, src, dst, self.send.at[self.place], self.recv.at[self.place])
        self.place += 1
        copy.start()
        return copy

    def block(self, at, count=1):
        return pl.ds(at * self.rows, count * self.rows)

    def start(self):
        cols = pl.ds(self.first, self.cols)
        grad = self.in_refs[0]
        self.live, at = [], 0
        for i, (k, n) in enumerate(runs(self.held)):
            copy = pltpu.make_async_copy(
                grad.at[self.block(k, n), cols], self.own.at[self.block(at, n)], self.load.at[i])
            copy.start()
            self.live.append(copy)
            at += n
        if self.came is not None:
            copy = pltpu.make_async_copy(self.in_refs[1], self.got[0], self.load.at[len(self.live)])
            copy.start()
            self.live.append(copy)
        else:
            at = 0
            for k, n in runs(self.away0):
                self.live.append(self.remote(
                    self.order[0][0], grad.at[self.block(k, n), cols],
                    self.got[0].at[self.block(at, n)]))
                at += n

    def add(self, got, places):
        def one(i, p):
            value = self.own[self.block(p), :].astype(F32) + got[self.block(i), :].astype(F32)
            self.own[self.block(i), :] = value.astype(BF16)

        for i, p in enumerate(places):
            one(i, p)

    def step(self):
        for copy in self.live:
            copy.wait()
        bits = len(self.order)
        level = self.level
        self.level += 1
        if level < bits:
            if level == 0:
                self.add(self.got[0], range(len(self.held)))
            else:
                self.add(self.got[level], self.stay)
                self.held = [self.held[p] for p in self.stay]
            if level + 1 < bits:
                name, weight = self.order[level + 1]
                self.stay = [p for p, k in enumerate(self.held) if not k & weight]
                away = [p for p, k in enumerate(self.held) if k & weight]
                self.live, at = [], 0
                for p, n in runs(away):
                    self.live.append(self.remote(
                        name, self.own.at[self.block(p, n)],
                        self.got[level + 1].at[self.block(at, n)]))
                    at += n
            else:
                self.live = [
                    self.remote("swap", self.own.at[self.block(0)], self.pair.at[self.block(0)]),
                    self.remote("back", self.own.at[self.block(1)], self.pair.at[self.block(1)]),
                ]
            return
        if level == bits:
            def diagonal_sum():
                self.total[0] = (self.own[self.block(0), :].astype(F32)
                                 + self.pair[self.block(1), :].astype(F32))

            def other_sum():
                self.total[0] = (self.pair[self.block(0), :].astype(F32)
                                 + self.pair[self.block(1), :].astype(F32))

            pl.when(off_diagonal() == 0)(diagonal_sum)
            pl.when(off_diagonal() == 1)(other_sum)
        elif level <= bits + len(self.sums):
            self.total[0] = self.total[0] + self.total[level - bits]
        else:
            return
        nth = level - bits
        if nth < len(self.sums):
            self.live = [self.remote(self.sums[nth], self.total.at[0], self.total.at[nth + 1])]
        else:
            copy = pltpu.make_async_copy(self.total.at[0], self.out, self.load.at[0])
            copy.start()
            self.live = [copy]


def runs(keys):
    keys, out = sorted(keys), []
    for k in keys:
        if out and out[-1][0] + out[-1][1] == k:
            out[-1][1] += 1
        else:
            out.append([k, 1])
    return out


def pair_ride(shard, blocks):
    rows, cols = shard.shape
    out = jax.ShapeDtypeStruct((rows * blocks, cols), shard.dtype)

    def stages(ins, outs):
        near, far = outs[0].at[pl.ds(0, rows)], outs[0].at[pl.ds(rows, rows)]
        return [[("ring", ins[0], far), ("swap", ins[0], near), ("stay", ins[0], near)]]

    return Ride([shard], [out], stages, ["ring", "swap"], 3)


def spread_ride(buffer, pieces, levels, blocks):
    rows = buffer.shape[0] // blocks
    plan = []
    for level in levels:
        stage = []
        for first, cols, order in pieces:
            held = [0, 1]
            for name, weight in order[:level]:
                held = held + [k + weight for k in held]
            name, weight = order[level]
            for k, n in runs(held):
                stage.append((name, k, k + weight, n, first, cols))
        plan.append(stage)

    def stages(ins, outs):
        ref = outs[0]
        return [
            [
                (name, ref.at[pl.ds(a * rows, n * rows), pl.ds(first, cols)],
                 ref.at[pl.ds(b * rows, n * rows), pl.ds(first, cols)])
                for name, a, b, n, first, cols in stage
            ]
            for stage in plan
        ]

    kinds = [item[0] for stage in plan for item in stage]
    out = jax.ShapeDtypeStruct(buffer.shape, buffer.dtype)
    return Ride([buffer], [out], stages, kinds, sum(len(s) for s in plan), {0: 0})


def chain_ride(shard, pieces, levels, blocks):
    first = pair_ride(shard, blocks)
    rest = spread_ride(first.outs[0], pieces, levels, blocks)

    def stages(ins, outs):
        return first.stages(ins, outs) + rest.stages(ins, outs)

    count = len(first.kinds) + 1 + len(rest.kinds)
    return Ride([shard], first.outs, stages, first.kinds + rest.kinds, count)


def send_ride(value, kind, after=0):
    out = jax.ShapeDtypeStruct(value.shape, value.dtype)
    return Ride([value], [out], lambda ins, outs: [[]] * after + [[(kind, ins[0], outs[0])]],
                [kind], 1)


class Part:
    ins, outs, scratch, kinds = (), (), (), ()

    def early(self, in_refs, out_refs, refs):
        pass

    def begin(self):
        pass

    def run(self, rides):
        pass

    def settle(self):
        pass


class Rides:
    def __init__(self, chains, outs):
        self.chains, self.outs = chains, outs
        for chain in chains:
            chain.start()

    def advance(self, kind=object):
        for chain in self.chains:
            if chain.levels - chain.level > 1 and isinstance(chain, kind):
                chain.step()

    def finish(self, i):
        while self.chains[i].level < self.chains[i].levels:
            self.chains[i].step()

    def end(self):
        for level in range(max([c.levels for c in self.chains], default=0)):
            for chain in self.chains:
                if chain.level == level and level < chain.levels:
                    chain.step()


def launch(name, number, parts, rides, limit=62):
    ins = [x for p in parts for x in p.ins]
    outs = [x for p in parts for x in p.outs]
    in_arrays, out_shapes = list(ins), list(outs)
    aliases, spans = {}, []
    for ride in rides:
        for a, b in ride.alias.items():
            aliases[len(in_arrays) + a] = len(out_shapes) + b
        spans.append((len(in_arrays), len(in_arrays) + len(ride.ins),
                      len(out_shapes), len(out_shapes) + len(ride.outs)))
        in_arrays += ride.ins
        out_shapes += ride.outs
    kinds = [k for p in parts for k in p.kinds] + [k for r in rides for k in r.kinds]
    scratch = [x for p in parts for x in p.scratch]
    parts_scratch = len(scratch)
    scratch += [x for r in rides for x in r.scratch]

    def kernel(*refs):
        in_refs = refs[: len(in_arrays)]
        out_refs = refs[len(in_arrays) : len(in_arrays) + len(out_shapes)]
        rest = refs[len(in_arrays) + len(out_shapes) :]
        i, o, c = 0, 0, 0
        for p in parts:
            p.early(in_refs[i : i + len(p.ins)], out_refs[o : o + len(p.outs)],
                    rest[c : c + len(p.scratch)])
            i, o, c = i + len(p.ins), o + len(p.outs), c + len(p.scratch)
        if kinds:
            greet(kinds)
        chains, at = [], parts_scratch
        for ride, (a, b, c, d) in zip(rides, spans):
            more = len(ride.scratch)
            chains.append(ride.chain(in_refs[a:b], out_refs[c:d], rest[at : at + more]))
            at += more
        under_way = Rides(chains, [out_refs[c] for _, _, c, _ in spans])
        for p in parts:
            p.begin()
        for p in parts:
            p.run(under_way)
        for p in parts:
            p.settle()
        under_way.end()

    results = pl.pallas_call(
        kernel,
        out_shape=tuple(out_shapes),
        in_specs=[ANY] * len(in_arrays),
        out_specs=tuple([ANY] * len(out_shapes)),
        scratch_shapes=scratch,
        input_output_aliases=aliases,
        name=name,
        compiler_params=pltpu.CompilerParams(
            collective_id=number if kinds else None,
            has_side_effects=bool(kinds),
            vmem_limit_bytes=limit << 20,
        ),
    )(*in_arrays)
    main_outs, at = [], 0
    for p in parts:
        main_outs.append(results[at : at + len(p.outs)])
        at += len(p.outs)
    return main_outs, [results[c:d] for _, _, c, d in spans]


def normalise_value(rows, gain, shift):
    centre = jnp.mean(rows, axis=-1, keepdims=True)
    centred = rows - centre
    spread = jnp.mean(centred * centred, axis=-1, keepdims=True)
    return (centred * lax.rsqrt(spread + NORM_EPS) * gain + shift).astype(BF16)


def gelu_pair(upper):
    cdf = 0.5 * (1.0 + lax.erf(upper * (0.5**0.5)))
    density = jnp.exp(-0.5 * upper * upper) * (0.5 / jnp.pi) ** 0.5
    return (upper * cdf).astype(BF16), (cdf + upper * density).astype(BF16)


class Gather(Part):
    def __init__(self, rows, size, norm, weight, width, n, ending=None, slope=None):
        self.size, self.width, self.n = size, width, n
        self.has_rows, self.has_norm, self.has_slope = rows is not None, norm is not None, slope is not None
        self.double = ending == "gelu"
        self.filler = lambda: None
        self.ride = weight if isinstance(weight, int) else None
        self.kinds = ["c", "zl"]
        self.ins = []
        if self.has_rows:
            self.ins.append(rows)
        if self.ride is None:
            self.ins.append(weight)
        if self.has_norm:
            self.ins.append(jnp.concatenate([norm[0], norm[1]], axis=0))
        if self.has_slope:
            self.ins.append(slope)
        self.outs = [jax.ShapeDtypeStruct((4, size, width), BF16)]
        self.outs += [jax.ShapeDtypeStruct((4, size, n), BF16)] * (2 if self.double else 1)
        tall = self.double or self.has_slope
        self.scratch = [
            pltpu.VMEM((size, width) if self.has_rows else (8, 128), F32),
            pltpu.VMEM((width, n), BF16),
            pltpu.VMEM((2, width), F32),
            pltpu.VMEM((4, size, width), BF16),
            pltpu.VMEM((4, size, n), BF16),
            pltpu.VMEM((4, size, n) if tall else (1, 16, 128), BF16),
            pltpu.SemaphoreType.DMA((4,)),
            pltpu.SemaphoreType.DMA((6,)),
            pltpu.SemaphoreType.DMA((6,)),
            pltpu.SemaphoreType.DMA((3, 4)),
        ]

    def early(self, in_refs, out_refs, refs):
        self.rows, self.w, self.norms, self.x, self.y, self.second = refs[:6]
        self.load, self.send, self.recv, self.store = refs[6:]
        self.out_refs, self.over = out_refs, []
        todo, self.loads = list(in_refs), {}
        if self.has_rows:
            self.loads["rows"] = pltpu.make_async_copy(todo.pop(0), self.rows, self.load.at[0])
        if self.ride is None:
            self.loads["w"] = pltpu.make_async_copy(todo.pop(0), self.w, self.load.at[1])
        if self.has_norm:
            self.loads["norm"] = pltpu.make_async_copy(todo.pop(0), self.norms, self.load.at[2])
        if self.has_slope:
            self.loads["slope"] = pltpu.make_async_copy(todo.pop(0), self.second, self.load.at[3])
        for copy in self.loads.values():
            copy.start()

    def send_half(self, h, source):
        half = self.size // 2
        part = pl.ds(h * half, half)
        if h == 0 and self.has_norm:
            self.loads["norm"].wait()
        value = source[part, :]
        if self.has_norm:
            value = normalise_value(value, self.norms[0:1, :], self.norms[1:2, :])
        x = self.x
        x[0, part, :] = value.astype(BF16)
        self.over.append(
            Copy("zl", x.at[0, part], x.at[2, part], self.send.at[h], self.recv.at[h]))
        self.over[-1].start()
        if h == 1:
            self.beside = Copy("c", x.at[0], x.at[1], self.send.at[2], self.recv.at[2])
            self.beside.start()

    def begin(self):
        if self.has_rows:
            self.loads["rows"].wait()
            for h in range(2):
                self.send_half(h, self.rows)

    def run(self, rides):
        x, y, w, second, n = self.x, self.y, self.w, self.second, self.n
        tile, half = min(TILE, n), self.size // 2
        if self.ride is not None:
            rides.finish(self.ride)
            copy = pltpu.make_async_copy(rides.outs[self.ride], w, self.load.at[1])
            copy.start()
            copy.wait()
        else:
            self.loads["w"].wait()
        if self.has_slope:
            self.loads["slope"].wait()
        stores = []

        def multiply(b):
            def step(j, carry):
                cols = pl.ds(pl.multiple_of(j * tile, tile), tile)
                value = nn(x[b], w[:, cols])
                if self.double:
                    y[b, :, cols], second[b, :, cols] = gelu_pair(value)
                elif self.has_slope:
                    y[b, :, cols] = (value * second[b, :, cols].astype(F32)).astype(BF16)
                else:
                    y[b, :, cols] = value.astype(BF16)
                return carry

            lax.fori_loop(0, n // tile, step, 0)
            for k, ref in enumerate([x, y] + ([second] if self.double else [])):
                stores.append(pltpu.make_async_copy(
                    ref.at[b], self.out_refs[k].at[b], self.store.at[k, b]))
                stores[-1].start()

        multiply(0)
        self.beside.wait()
        multiply(1)
        self.filler()
        relay = []
        for h in range(2):
            part = pl.ds(h * half, half)
            self.over[h].wait()
            relay.append(Copy("c", x.at[2, part], x.at[3, part],
                              self.send.at[3 + h], self.recv.at[3 + h]))
            relay[-1].start()
        multiply(2)
        for copy in relay:
            copy.wait()
        multiply(3)
        for copy in stores:
            copy.wait()


class Scatter(Part):
    def __init__(self, parts, weight, base, norm, fills, hand=None):
        _, size, n = parts.shape
        width = weight.shape[0]
        half = size // 2
        rows = 4 * size
        ins = [parts.reshape(rows, n), weight] + ([base] if base is not None else [])
        if norm is not None:
            ins += list(norm)
        fill_at = len(ins)
        fill_cols = []
        for a, b, _ in fills:
            ins.append(a)
            if b is not None:
                ins.append(b)
            fill_cols.append(n if b is None else b.shape[1])
        outs = [jax.ShapeDtypeStruct((size, width), F32)]
        if norm is not None:
            outs.append(jax.ShapeDtypeStruct((2, width), F32))
        outs += [jax.ShapeDtypeStruct((width, k), BF16) for k in fill_cols]
        sends_at, copies = len(outs), 0
        for _, _, sends in fills:
            for _, rows_away, _, k in sends:
                outs.append(jax.ShapeDtypeStruct((sum(n for _, n in rows_away), k), BF16))
                copies += len(rows_away)
        scratch = [
            pltpu.VMEM((rows, n), BF16),
            pltpu.VMEM((width, n), BF16),
            pltpu.VMEM((size, width), F32),
            pltpu.VMEM((size, width), F32),
            pltpu.VMEM((2, size, width), BF16),
            pltpu.VMEM((2, size, width), BF16),
            pltpu.VMEM((size, width), BF16),
            pltpu.VMEM((size, width), BF16),
            pltpu.SemaphoreType.DMA((8,)),
            pltpu.SemaphoreType.DMA((6,)),
            pltpu.SemaphoreType.DMA((6,)),
        ]
        if norm is not None:
            scratch += [
                pltpu.VMEM((size, width), F32),
                pltpu.VMEM((1, width), F32),
                pltpu.VMEM((size, width), F32),
                pltpu.VMEM((2, width), F32),
                pltpu.SemaphoreType.DMA((4,)),
            ]
        for (a, b, _), k in zip(fills, fill_cols):
            scratch.append(pltpu.VMEM((rows, width), BF16))
            if b is not None:
                scratch.append(pltpu.VMEM((rows, k), BF16))
            scratch += [pltpu.VMEM((width, k), BF16), pltpu.SemaphoreType.DMA((3,))]
        scratch += [pltpu.SemaphoreType.DMA((max(copies, 1),))] * 2
        self.kinds = ["c", "zl"] + [name for _, _, sends in fills for name, _, _, _ in sends]
        self.sends_at = sends_at
        self.ins, self.outs, self.scratch = ins, outs, scratch
        self.facts = (size, n, width, half, base, norm, fills, fill_at, fill_cols, outs)
        self.hand = hand

    def early(self, in_refs, out_refs, refs):
        size, n, width, half, base, norm, fills, fill_at, fill_cols, outs = self.facts
        self.out_refs, self.refs = out_refs, refs
        y, w, total, far, give, came, across, over, load, send, recv = refs[:11]
        refs = list(refs[11:])
        if norm is not None:
            stream, gain, back, sums, norm_sem = refs[:5]
            refs = refs[5:]
        loads = [pltpu.make_async_copy(in_refs[1], w, load.at[0])]
        loads += [
            pltpu.make_async_copy(
                in_refs[0].at[pl.ds(b * size, size)], y.at[pl.ds(b * size, size)],
                load.at[1 + b])
            for b in range(4)
        ]
        if base is not None:
            loads.append(pltpu.make_async_copy(in_refs[2], total, load.at[5]))
        for place in (0, 4, 3, 2, 1, 5)[: len(loads)]:
            loads[place].start()
        others = []
        if norm is not None:
            at = 3 if base is not None else 2
            for i, ref in enumerate((stream, gain, back)):
                others.append(pltpu.make_async_copy(in_refs[at + i], ref, norm_sem.at[i]))
        at = fill_at
        for a, b, _ in fills:
            others.append(pltpu.make_async_copy(in_refs[at], refs[0], refs[2 if b is None else 3].at[0]))
            at += 1
            if b is not None:
                others.append(pltpu.make_async_copy(in_refs[at], refs[1], refs[3].at[1]))
                at += 1
            refs = refs[3 if b is None else 4 :]
        for copy in others:
            copy.start()
        self.loads, self.others = loads, others

    def run(self, rides):
        size, n, width, half, base, norm, fills, fill_at, fill_cols, outs = self.facts
        out_refs, refs = self.out_refs, self.refs
        y, w, total, far, give, came, across, over, load, send, recv = refs[:11]
        refs = list(refs[11:])
        if norm is not None:
            stream, gain, back, sums, norm_sem = refs[:5]
            refs = refs[5:]
        loads, others = self.loads, self.others

        def multiply(b, part, count, put):
            def step(j, carry):
                cols = pl.ds(pl.multiple_of(j * TILE, TILE), TILE)
                put(cols, nt(y[pl.ds(b * size + part, count), :], w[cols, :]))
                return carry

            lax.fori_loop(0, width // TILE, step, 0)

        for place in (0, 4, 3):
            loads[place].wait()
        sent = []
        for h in range(2):
            part = pl.ds(h * half, half)

            def put_give(cols, value, part=part):
                give[0, part, cols] = value.astype(BF16)

            def put_far(cols, value, part=part):
                far[part, cols] = value

            multiply(3, h * half, half, put_give)
            copy = Copy("c", give.at[0, part], came.at[0, part], send.at[h], recv.at[h])
            copy.start()
            multiply(2, h * half, half, put_far)
            copy.wait()
            across[part, :] = (far[part, :] + came[0, part, :].astype(F32)).astype(BF16)
            copy = Copy("zl", across.at[part], over.at[part], send.at[2 + h], recv.at[2 + h])
            copy.start()
            sent.append(copy)
        rides.advance(Fold)
        loads[2].wait()

        def put_near(cols, value):
            give[1, :, cols] = value.astype(BF16)

        multiply(1, 0, size, put_near)
        near = Copy("c", give.at[1], came.at[1], send.at[4], recv.at[4])
        near.start()
        loads[1].wait()
        if base is not None:
            loads[5].wait()

        def put_total(cols, value):
            total[:, cols] = value + (total[:, cols] if base is not None else 0.0)

        multiply(0, 0, size, put_total)
        for copy in others:
            copy.wait()
        stores, fill_refs, refs_all = [], refs, self.refs
        slot = [self.sends_at, 0]

        def fill(k, left, right, result, sem):
            count = fill_cols[k]
            wide = 768 if count % 768 == 0 else count

            def step(j, carry):
                rows_ = pl.ds(pl.multiple_of(j * 256, 256), 256)
                turned = left[:, rows_].T
                for q in range(count // wide):
                    cols = slice(q * wide, (q + 1) * wide)
                    result[rows_, cols] = nn(turned, right[:, cols]).astype(BF16)
                return carry

            lax.fori_loop(0, width // 256, step, 0)
            where = self.sends_at - len(fills) + k
            stores.append(pltpu.make_async_copy(result, out_refs[where], sem.at[2]))
            stores[-1].start()
            for name, rows_away, first, cols in fills[k][2]:
                at = 0
                for row, count in rows_away:
                    copy = Copy(name, result.at[pl.ds(row, count), pl.ds(first, cols)],
                                out_refs[slot[0]].at[pl.ds(at, count)],
                                refs_all[-2].at[slot[1]], refs_all[-1].at[slot[1]])
                    copy.start()
                    stores.append(copy)
                    at += count
                    slot[1] += 1
                slot[0] += 1

        for k, (a, b, _) in enumerate(fills):
            if b is None:
                left, result, sem = fill_refs[:3]
                right, fill_refs = y, fill_refs[3:]
            else:
                left, right, result, sem = fill_refs[:4]
                fill_refs = fill_refs[4:]
            job = functools.partial(fill, k, left, right, result, sem)
            if self.hand is not None and k == len(fills) - 1 and not fills[k][2]:
                self.hand.filler = job
            else:
                job()
        rides.advance()
        near.wait()
        total[...] += came[1].astype(F32)
        for h in range(2):
            part = pl.ds(h * half, half)
            sent[h].wait()
            total[part, :] += over[part, :].astype(F32)
            if norm is not None:
                value = total[part, :]
                rows_in = stream[part, :]
                centred = rows_in - jnp.mean(rows_in, axis=-1, keepdims=True)
                inverse = lax.rsqrt(jnp.mean(centred * centred, axis=-1, keepdims=True) + NORM_EPS)
                unit = centred * inverse
                gain_sum = jnp.sum(value * unit, axis=0, keepdims=True)
                shift_sum = jnp.sum(value, axis=0, keepdims=True)
                sums[0:1, :] = gain_sum if h == 0 else sums[0:1, :] + gain_sum
                sums[1:2, :] = shift_sum if h == 0 else sums[1:2, :] + shift_sum
                scaled = value * gain[...]
                total[part, :] = back[part, :] + inverse * (
                    scaled
                    - jnp.mean(scaled, axis=-1, keepdims=True)
                    - unit * jnp.mean(scaled * unit, axis=-1, keepdims=True)
                )
            if self.hand is not None:
                self.hand.send_half(h, total)
            copy = pltpu.make_async_copy(total.at[part], out_refs[0].at[part], load.at[6 + h])
            copy.start()
            stores.append(copy)
        if norm is not None:
            copy = pltpu.make_async_copy(sums, out_refs[1], norm_sem.at[3])
            copy.start()
            stores.append(copy)
        self.stores = stores

    def settle(self):
        for copy in self.stores:
            copy.wait()


def place_of(i):
    c, zl = lax.axis_index("c"), lax.axis_index("zl")
    dc, dz = i // 2, i % 2
    return (c + dc) % 2 + 2 * ((zl + dz) % 2)


def head_only(value, u):
    lane = lax.broadcasted_iota(jnp.int32, value.shape, 1)
    keep = (lane < HEAD_DIM) if u == 0 else (lane >= HEAD_DIM)
    return jnp.where(keep, value, jnp.zeros_like(value))


def masked(scores):
    key = lax.broadcasted_iota(jnp.int32, scores.shape, 0)
    query = lax.broadcasted_iota(jnp.int32, scores.shape, 1)
    return jnp.where(key <= query, scores, MASKED)


def softmax_parts(parts, value_rows):
    top = parts[0].max(axis=0, keepdims=True)
    for scores in parts[1:]:
        top = jnp.maximum(top, scores.max(axis=0, keepdims=True))
    total, mixed = 0.0, 0.0
    for scores, values in zip(parts, value_rows):
        expo = jnp.exp(scores - top)
        total = total + expo.sum(axis=0, keepdims=True)
        mixed = mixed + nn(values, expo.astype(BF16))
    return mixed / total, top + jnp.log(total)


def softmax_back(scores, slopes, logsum):
    probs = [jnp.exp(s - logsum) for s in scores]
    inner = 0.0
    for p, d in zip(probs, slopes):
        inner = inner + (p * d).sum(axis=0, keepdims=True)
    return [p.astype(BF16) for p in probs], [
        (p * (d - inner)).astype(BF16) for p, d in zip(probs, slopes)
    ]


class Local(Part):
    def __init__(self, ins, outs, scratch, main):
        self.ins, self.outs, self.scratch, self.main = ins, outs, scratch, main

    def early(self, in_refs, out_refs, refs):
        self.refs = (in_refs, out_refs, refs)
        self.stage = self.main(in_refs, out_refs, refs, True)

    def run(self, rides):
        self.main(*self.refs, self.stage, rides)


def attend_self(proj, scale):
    _, size, wide = proj.shape
    cols = wide // 3
    frames, heads = 4 * size, cols // HEAD_DIM
    outs = [jax.ShapeDtypeStruct((4, size, cols), BF16), jax.ShapeDtypeStruct((heads, frames), F32)]
    scratch = [
        pltpu.VMEM((4, size, wide), BF16),
        pltpu.VMEM((frames, 128), BF16),
        pltpu.VMEM((128, frames), BF16),
        pltpu.VMEM((4, size, cols), BF16),
        pltpu.VMEM((heads, frames), F32),
        pltpu.SemaphoreType.DMA((3,)),
    ]

    def main(in_refs, out_refs, refs, stage, rides=None):
        x, keys, values, out, logs, sem = refs
        if stage is True:
            copy = pltpu.make_async_copy(in_refs[0], x, sem.at[0])
            copy.start()
            return copy
        stage.wait()
        for g in range(cols // 128):
            if g:
                rides.advance()
            lanes = [pl.ds(part * cols + g * 128, 128) for part in range(3)]
            for i in range(4):
                rows = pl.ds(i * size, size)
                keys[rows, :] = x[place_of(i), :, lanes[1]]
                values[:, rows] = x[place_of(i), :, lanes[2]].T
            for i in range(4):
                query = x[place_of(i), :, lanes[0]]
                before = i * size
                done = []
                for u in range(2):
                    q = head_only(query, u)
                    mine = pl.ds(u * HEAD_DIM, HEAD_DIM)
                    parts = [masked(nt(keys[pl.ds(before, size), :], q) * scale)]
                    rows = [values[mine, pl.ds(before, size)]]
                    if i:
                        parts.append(nt(keys[pl.ds(0, before), :], q) * scale)
                        rows.append(values[mine, pl.ds(0, before)])
                    mixed, logsum = softmax_parts(parts, rows)
                    done.append(mixed)
                    logs[pl.ds(2 * g + u, 1), pl.ds(before, size)] = logsum
                joined = jnp.concatenate(done, axis=0).T
                out[place_of(i), :, pl.ds(g * 128, 128)] = joined.astype(BF16)
        copies = [pltpu.make_async_copy(out, out_refs[0], sem.at[1]),
                  pltpu.make_async_copy(logs, out_refs[1], sem.at[2])]
        for copy in copies:
            copy.start()
        for copy in copies:
            copy.wait()

    return Local([proj], outs, scratch, main)


def attend_self_back(proj, grad_joined, logsum, scale):
    _, size, wide = proj.shape
    cols = wide // 3
    frames, heads = 4 * size, cols // HEAD_DIM
    outs = [jax.ShapeDtypeStruct((4, size, wide), BF16)]
    scratch = [
        pltpu.VMEM((4, size, wide), BF16),
        pltpu.VMEM((4, size, cols), BF16),
        pltpu.VMEM((heads, frames), F32),
        pltpu.VMEM((frames, 128), BF16),
        pltpu.VMEM((128, frames), BF16),
        pltpu.VMEM((frames, 128), BF16),
        pltpu.VMEM((frames, 128), F32),
        pltpu.VMEM((frames, 128), F32),
        pltpu.VMEM((4, size, wide), BF16),
        pltpu.SemaphoreType.DMA((4,)),
    ]

    def main(in_refs, out_refs, refs, stage, rides=None):
        x, grads, logs, keys, keys_t, values, grad_k, grad_v, out, sem = refs
        if stage is True:
            copies = [
                pltpu.make_async_copy(in_refs[i], ref, sem.at[i])
                for i, ref in enumerate((x, grads, logs))
            ]
            for copy in copies:
                copy.start()
            return copies
        for copy in stage:
            copy.wait()
        for g in range(cols // 128):
            if g < 2:
                rides.advance(Fold)
            lanes = [pl.ds(part * cols + g * 128, 128) for part in range(3)]
            for i in range(4):
                rows = pl.ds(i * size, size)
                keys[rows, :] = x[place_of(i), :, lanes[1]]
                keys_t[:, rows] = x[place_of(i), :, lanes[1]].T
                values[rows, :] = x[place_of(i), :, lanes[2]]
            grad_k[...] = jnp.zeros_like(grad_k)
            grad_v[...] = jnp.zeros_like(grad_v)
            for i in range(4):
                query = x[place_of(i), :, lanes[0]]
                grad = grads[place_of(i), :, lanes[0]]
                before = i * size
                spans = [pl.ds(before, size)] + ([pl.ds(0, before)] if i else [])
                done = []
                for u in range(2):
                    q, go = head_only(query, u), head_only(grad, u)
                    mine = pl.ds(u * HEAD_DIM, HEAD_DIM)
                    scores = [nt(keys[span, :], q) * scale for span in spans]
                    scores[0] = masked(scores[0])
                    slopes = [nt(values[span, :], go) for span in spans]
                    probs, grad_scores = softmax_back(
                        scores, slopes, logs[pl.ds(2 * g + u, 1), pl.ds(before, size)])
                    grad_q = 0.0
                    for span, p, d in zip(spans, probs, grad_scores):
                        grad_v[span, :] += nn(p, go)
                        grad_k[span, :] += nn(d, q)
                        grad_q = grad_q + nn(keys_t[mine, span], d)
                    done.append(grad_q)
                grad_q = jnp.concatenate(done, axis=0).T * scale
                out[place_of(i), :, lanes[0]] = grad_q.astype(BF16)
            for i in range(4):
                rows = pl.ds(i * size, size)
                out[place_of(i), :, lanes[1]] = (grad_k[rows, :] * scale).astype(BF16)
                out[place_of(i), :, lanes[2]] = grad_v[rows, :].astype(BF16)
        copy = pltpu.make_async_copy(out, out_refs[0], sem.at[3])
        copy.start()
        copy.wait()

    return Local([proj, grad_joined, logsum], outs, scratch, main)


def attend_cross(query, text, weight, scale):
    _, size, cols = query.shape
    frames, heads = 4 * size, cols // HEAD_DIM
    states, width = text.shape
    outs = [jax.ShapeDtypeStruct((4, size, cols), BF16), jax.ShapeDtypeStruct((heads, frames), F32),
            jax.ShapeDtypeStruct((states, 2 * cols), BF16)]
    scratch = [
        pltpu.VMEM((4, size, cols), BF16),
        pltpu.VMEM((states, 2 * cols), BF16),
        pltpu.VMEM((4, size, cols), BF16),
        pltpu.VMEM((heads, frames), F32),
        pltpu.VMEM((states, width), BF16),
        pltpu.VMEM((width, 2 * cols), BF16),
        pltpu.SemaphoreType.DMA((6,)),
    ]

    def main(in_refs, out_refs, refs, stage, rides=None):
        x, kv, out, logs, states_in, w, sem = refs
        if stage is True:
            copies = [
                pltpu.make_async_copy(in_refs[i], ref, sem.at[i])
                for i, ref in enumerate((x, states_in, w))
            ]
            for copy in copies:
                copy.start()
            return copies
        for copy in stage:
            copy.wait()
        kv[...] = nn(states_in[...], w[...]).astype(BF16)
        for g in range(cols // 128):
            lanes = pl.ds(g * 128, 128)
            keys = kv[:, lanes]
            values = kv[:, pl.ds(cols + g * 128, 128)].T
            for i in range(4):
                rows = x[i, :, lanes]
                done = []
                for u in range(2):
                    scores = nt(keys, head_only(rows, u)) * scale
                    mixed, logsum = softmax_parts(
                        [scores], [values[u * HEAD_DIM : (u + 1) * HEAD_DIM, :]])
                    done.append(mixed)
                    logs[pl.ds(2 * g + u, 1), pl.ds(i * size, size)] = logsum
                out[i, :, lanes] = jnp.concatenate(done, axis=0).T.astype(BF16)
        copies = [
            pltpu.make_async_copy(ref, out_refs[i], sem.at[3 + i])
            for i, ref in enumerate((out, logs, kv))
        ]
        for copy in copies:
            copy.start()
        for copy in copies:
            copy.wait()

    return Local([query, text, weight], outs, scratch, main)


def attend_cross_back(query, pairs, grad_joined, logsum, text, weight, scale):
    _, size, cols = query.shape
    frames, heads = 4 * size, cols // HEAD_DIM
    states, width = text.shape
    outs = [jax.ShapeDtypeStruct((4, size, cols), BF16),
            jax.ShapeDtypeStruct((width, 2 * cols), BF16),
            jax.ShapeDtypeStruct((states, width), F32)]
    scratch = [
        pltpu.VMEM((4, size, cols), BF16),
        pltpu.VMEM((states, 2 * cols), BF16),
        pltpu.VMEM((4, size, cols), BF16),
        pltpu.VMEM((heads, frames), F32),
        pltpu.VMEM((states, width), BF16),
        pltpu.VMEM((width, 2 * cols), BF16),
        pltpu.VMEM((4, size, cols), BF16),
        pltpu.VMEM((states, 2 * cols), BF16),
        pltpu.VMEM((width, 2 * cols), BF16),
        pltpu.VMEM((states, width), F32),
        pltpu.SemaphoreType.DMA((9,)),
    ]

    def main(in_refs, out_refs, refs, stage, rides=None):
        x, kv, grads, logs, states_in, w, out, out_kv, out_w, out_text, sem = refs
        if stage is True:
            copies = [
                pltpu.make_async_copy(in_refs[i], ref, sem.at[i])
                for i, ref in enumerate((x, kv, grads, logs, states_in, w))
            ]
            for copy in copies:
                copy.start()
            return copies
        for copy in stage:
            copy.wait()
        for g in range(cols // 128):
            if g:
                rides.advance()
            lanes, lanes_v = pl.ds(g * 128, 128), pl.ds(cols + g * 128, 128)
            keys, values = kv[:, lanes], kv[:, lanes_v]
            keys_t = keys.T
            grad_k, grad_v = 0.0, 0.0
            for i in range(4):
                done = []
                for u in range(2):
                    q, go = head_only(x[i, :, lanes], u), head_only(grads[i, :, lanes], u)
                    scores = nt(keys, q) * scale
                    probs, grad_scores = softmax_back(
                        [scores], [nt(values, go)],
                        logs[pl.ds(2 * g + u, 1), pl.ds(i * size, size)])
                    grad_v = grad_v + nn(probs[0], go)
                    grad_k = grad_k + nn(grad_scores[0], q)
                    done.append(nn(keys_t[u * HEAD_DIM : (u + 1) * HEAD_DIM, :], grad_scores[0]))
                out[i, :, lanes] = (jnp.concatenate(done, axis=0).T * scale).astype(BF16)
            out_kv[:, lanes] = (grad_k * scale).astype(BF16)
            out_kv[:, lanes_v] = grad_v.astype(BF16)
        grad_pairs = out_kv[...]
        out_w[...] = nn(states_in[...].T, grad_pairs).astype(BF16)
        out_text[...] = nt(grad_pairs, w[...])
        copies = [
            pltpu.make_async_copy(ref, out_refs[i], sem.at[6 + i])
            for i, ref in enumerate((out, out_w, out_text))
        ]
        for copy in copies:
            copy.start()
        for copy in copies:
            copy.wait()

    return Local([query, pairs, grad_joined, logsum, text, weight], outs, scratch, main)


def flat(parts):
    return parts.reshape(-1, parts.shape[-1])


def body(bits, frames_in, text_states, ln_gain, ln_bias, w_self, w_self_out, w_cross_q,
         w_cross_kv, w_cross_out, w_up, w_down, cotangent):
    scale = float(HEAD_DIM) ** (-0.5)
    layers = w_self.shape[0]
    width = frames_in.shape[2]
    part = w_self.shape[1]
    blocks = width // part
    cols = w_self.shape[3]
    hidden = w_up.shape[2]
    me = lax.axis_index("zh")
    for place, name in enumerate(reversed(bits)):
        me = me + (lax.axis_index(name) << (place + 1))

    row = lax.broadcasted_iota(jnp.int32, (width, width), 0)
    col = lax.broadcasted_iota(jnp.int32, (width, width), 1)
    permute = ((row // part == ((col // part) ^ me)) & (row % part == col % part)).astype(BF16)

    def reorder(value):
        return nn(value, permute)

    up = [(name, 2 << (len(bits) - 1 - place)) for place, name in enumerate(bits)]
    low_first = list(reversed(up))
    levels = len(bits)
    early, late = list(range(levels // 2)), list(range(levels // 2, levels))
    sizes = {"self": 3 * cols, "self_out": cols, "q": cols, "kv": 2 * cols, "out": cols,
             "up": hidden, "down": hidden, "norm": 128}

    def halves(name):
        n = sizes[name]
        if name in ("self", "kv", "up", "down"):
            first = (n // 2 + 127) // 128 * 128
            return [(0, first, low_first), (first, n - first, up)]
        return [(0, n, low_first if name in ("q", "norm") else up)]

    packs = {"a": "self", "o": "self_out", "q": "q", "k": "kv", "u": "out", "c": "up", "d": "down"}
    norm_rows = jnp.concatenate([ln_gain.reshape(-1, part), ln_bias.reshape(-1, part)], axis=0).T
    norm_rows = jnp.pad(norm_rows, ((0, 0), (0, sizes["norm"] - norm_rows.shape[1])))
    shards = {}
    for l in range(layers):
        shards[l, "self"] = w_self[l].reshape(part, 3 * cols)
        shards[l, "self_out"] = w_self_out[l].T
        shards[l, "q"] = w_cross_q[l]
        shards[l, "kv"] = w_cross_kv[l].reshape(part, 2 * cols)
        shards[l, "out"] = w_cross_out[l].T
        shards[l, "up"] = w_up[l]
        shards[l, "down"] = w_down[l].T
    held = {}
    counter = [0]

    def number():
        counter[0] += 1
        return counter[0] - 1

    def forward(parts, todo=(), more=()):
        rides, keys = [], []
        for word in todo:
            l, name, stage = int(word[0]), packs[word[1]], int(word[2])
            if l >= layers:
                continue
            if stage == 1:
                rides.append(pair_ride(shards[l, name], blocks))
            else:
                which = {2: early, 3: late, 4: early + late}[stage]
                rides.append(spread_ride(held[l, name], halves(name), which, blocks))
            keys.append((l, name))
        outs, extra = launch(f"step_{counter[0]}", number(), parts, rides + list(more))
        for key, value in zip(keys, extra):
            held[key] = value[0]
        return outs, [e[0] for e in extra[len(keys):]]

    def move(rides):
        return launch(f"move_{counter[0]}", number(), [], rides)[1]

    extra = move([
        chain_ride(shards[0, "self"], halves("self"), early, blocks),
        chain_ride(norm_rows, halves("norm"), early + late, blocks),
        send_ride(text_states[0], "c"),
        send_ride(frames_in[0], "swap", 1),
    ])
    held[0, "self"], norms, text_far, frames_far = [e[0] for e in extra]
    stream = reorder(jnp.where(diagonal(), frames_in[0], frames_far))
    text_own = reorder(jnp.where(diagonal(), text_states[0], text_far)).astype(BF16)
    norms = norms.astype(F32).T
    gains = norms[: 3 * layers].reshape(layers, 3, 1, width)
    shifts = norms[3 * layers : 6 * layers].reshape(layers, 3, 1, width)
    size = stream.shape[0]

    def norm_of(l, j):
        return gains[l, j], shifts[l, j]

    records = []
    (((first, proj),), _) = forward(
        [Gather(stream, size, norm_of(0, 0), 0, width, 3 * cols)], ["0a3", "0o1", "0q1", "0k1", "0u1"])
    for l in range(layers):
        n = l + 1
        saved = {"one": stream, "first": first, "proj": proj}
        (((joined, logsum),), _) = forward(
            [attend_self(proj, scale)], [f"{l}o4", f"{l}q4", f"{l}c1"])
        saved.update(joined_self=joined, logsum_self=logsum)
        hand = Gather(None, size, norm_of(l, 1), held[l, "q"], width, cols)
        (((stream,), (second, query)), _) = forward(
            [Scatter(joined, held[l, "self_out"], stream, None, [], hand), hand],
            [f"{l}k4", f"{l}u4", f"{l}c2", f"{l}d1"])
        saved.update(two=stream, second=second, query=query)

        (((joined, logsum, pairs),), _) = forward(
            [attend_cross(query, text_own, held[l, "kv"], scale)], [f"{l}d2"])
        saved.update(pairs=pairs, joined_cross=joined, logsum_cross=logsum)
        hand = Gather(None, size, norm_of(l, 2), 0, width, hidden, "gelu")
        more = [send_ride(cotangent[0], "swap")] if n == layers else []
        (((stream,), (third, active, slope)), extra) = forward(
            [Scatter(joined, held[l, "out"], stream, None, [], hand), hand],
            [f"{l}c3", f"{l}d3", f"{n}a1"], more)
        saved.update(three=stream, third=third, active=active, slope=slope)
        records.append(saved)

        if n < layers:
            hand = Gather(None, size, norm_of(n, 0), 0, width, 3 * cols)
            (((stream,), (first, proj)), _) = forward(
                [Scatter(active, held[l, "down"], stream, None, [], hand), hand],
                [f"{n}a4", f"{n}o1", f"{n}q1", f"{n}k1", f"{n}u1"])
        else:
            grad = reorder(jnp.where(diagonal(), cotangent[0], extra[0]))
            gather = Gather(grad, size, None, held[l, "down"], width, hidden, slope=slope)
            (((stream,), (full, grad_upper)), _) = forward(
                [Scatter(active, held[l, "down"], stream, None, []), gather])
    result_own = reorder(stream.astype(BF16)).astype(BF16)

    folding = []
    finished = {}
    grad_text = jnp.zeros((text_own.shape[0], width), F32)
    norm_grads = {}

    def fold_later(l, name, value, came=None):
        for i, (first, n, order) in enumerate(halves(name)):
            folding.append({"key": (l, name, first), "grad": value.astype(BF16), "first": first,
                            "cols": n, "order": list(reversed(order)),
                            "came": came[i] if came else None})

    def first_sends(name):
        sends = []
        for first, n, order in halves(name):
            axis, weight = order[-1]
            away = runs([k for k in range(blocks) if k & weight])
            sends.append((axis, [(k * part, count * part) for k, count in away], first, n))
        return sends

    def fold_ride(item):
        sums = ("zl", "zh") if item["key"][1] == "norm" else ()
        return Fold(item["grad"], item["first"], item["cols"], item["order"], blocks,
                    item["came"], sums)

    def first_ride(item):
        name, weight = item["order"][0]
        away = runs([k for k in range(blocks) if k & weight])
        grad, first, n = item["grad"], item["first"], item["cols"]
        out = jax.ShapeDtypeStruct((grad.shape[0] // 2, n), BF16)

        def stages(ins, outs):
            copies, at = [], 0
            for k, count in away:
                copies.append((name, ins[0].at[pl.ds(k * part, count * part), pl.ds(first, n)],
                               outs[0].at[pl.ds(at * part, count * part)]))
                at += count
            return [copies]

        return Ride([grad], [out], stages, [name] * len(away), len(away))

    def folds(parts, end=(), begin=(), more=()):
        ending = [i for i in folding if i["key"][:2] in end]
        beginning = [i for i in folding if i["key"][:2] in begin]
        rides = [fold_ride(i) for i in ending] + [first_ride(i) for i in beginning]
        outs, extra = launch(f"step_{counter[0]}", number(), parts, rides + list(more))
        for item, came in zip(ending, extra):
            finished[item["key"]] = came[0]
            folding.remove(item)
        for item, came in zip(beginning, extra[len(ending):]):
            item["came"] = came[0]
        return outs, [e[0] for e in extra[len(rides):]]

    for l in reversed(range(layers)):
        saved = records[l]
        more = [send_ride(result_own, "swap")] if l == layers - 1 else []
        hand = Gather(None, size, None, held[l, "out"], width, cols)
        fills = [(flat(full), flat(saved["active"]), first_sends("down")),
                 (flat(saved["third"]), None, [])]
        (((grad, norm_grads[l, 2], down, up_, *came), (full, grad_joined)), extra) = folds(
            [Scatter(grad_upper, held[l, "up"], None, (saved["three"], gains[l, 2], grad), fills,
                     hand), hand], [(l + 1, "self_out"), (l + 1, "self")], (), more)
        if more:
            result = jnp.where(diagonal(), result_own, extra[0])
        fold_later(l, "down", down, came)
        fold_later(l, "up", up_)

        (((grad_query, kv_, text_part),), _) = folds(
            [attend_cross_back(saved["query"], saved["pairs"], grad_joined,
                               saved["logsum_cross"], text_own, held[l, "kv"], scale)],
            (), [(l, "up")])
        grad_text = grad_text + text_part
        fold_later(l, "kv", kv_)
        more = [send_ride(grad_text.astype(BF16), "c")] if l == 0 else []
        hand = Gather(None, size, None, held[l, "self_out"], width, cols)
        fills = [(flat(full), flat(saved["joined_cross"]), first_sends("out")),
                 (flat(saved["second"]), None, first_sends("q"))]
        (((grad, norm_grads[l, 1], out_, q_, *came), (full, grad_joined)), extra) = folds(
            [Scatter(grad_query, held[l, "q"], None, (saved["two"], gains[l, 1], grad), fills,
                     hand), hand], [(l, "down")], [(l, "kv")], more)
        fold_later(l, "out", out_, came[:1])
        fold_later(l, "q", q_, came[1:])
        if more:
            grad_text = grad_text.astype(BF16).astype(F32) + extra[0].astype(F32)
            more = [send_ride(grad_text.astype(BF16), "zl")]

        (((grad_proj,),), extra) = folds(
            [attend_self_back(saved["proj"], grad_joined, saved["logsum_self"], scale)],
            [(l, "up")], (), more)
        if more:
            grad_text = grad_text.astype(BF16).astype(F32) + extra[0].astype(F32)
        fills = [(flat(full), flat(saved["joined_self"]), first_sends("self_out")),
                 (flat(saved["first"]), None, first_sends("self"))]
        chain = (saved["one"], gains[l, 0], grad)
        parts = [Scatter(grad_proj, held[l, "self"], None, chain, fills)]
        if l:
            hand = Gather(None, size, None, held[l - 1, "down"], width, hidden,
                          slope=records[l - 1]["slope"])
            parts = [Scatter(grad_proj, held[l, "self"], None, chain, fills, hand), hand]
        (((grad, norm_grads[l, 0], out_, self_, *came), *after), _) = folds(
            parts, [(l, "out"), (l, "q"), (l, "kv")])
        if l:
            ((full, grad_upper),) = after
        fold_later(l, "self_out", out_, came[:1])
        fold_later(l, "self", self_, came[1:])

    small = [norm_grads[l, j][k] for l in range(layers) for k in range(2) for j in range(3)]
    small = jnp.stack(small, axis=1)
    small = jnp.pad(small, ((0, 0), (0, sizes["norm"] - small.shape[1])))
    fold_later(0, "norm", small)
    frames_back = reorder(grad.astype(BF16)).astype(BF16)
    text_back = reorder(grad_text.astype(BF16)).astype(BF16)
    folds_left = [fold_ride(item) for item in folding]
    extra = move(folds_left + [send_ride(frames_back, "swap"), send_ride(text_back, "swap")])
    for item, came in zip(folding, extra):
        finished[item["key"]] = came[0]
    grad_frames, text_sum = [
        jnp.where(diagonal(), mine, came[0]).astype(F32)
        for mine, came in zip((frames_back, text_back), extra[len(folds_left):])
    ]
    small = finished[0, "norm", 0][:, : 6 * layers]
    small = small.T.reshape(layers, 6, part)

    def gradient(l, name):
        pieces = [finished[l, name, first] for first, _, _ in halves(name)]
        return jnp.concatenate(pieces, axis=1) if len(pieces) > 1 else pieces[0]

    def stacked(name, shape=None, turned=False):
        members = [gradient(l, name) for l in range(layers)]
        if turned:
            members = [m.T for m in members]
        if shape is not None:
            members = [m.reshape(shape) for m in members]
        return jnp.stack(members)

    return (
        result[None],
        grad_frames[None],
        text_sum[None],
        small[:, :3],
        small[:, 3:],
        stacked("self", (part, 3, cols)),
        stacked("self_out", turned=True),
        stacked("q"),
        stacked("kv", (part, 2, cols)),
        stacked("out", turned=True),
        stacked("up"),
        stacked("down", turned=True),
    )


def solution(mesh):
    count = mesh.shape["dp"]
    bits = tuple(f"b{i}" for i in range(count.bit_length() - 2))
    dp = (*bits, "c")
    tensor = ("zh", "zl")
    inner = Mesh(mesh.devices.reshape((2,) * (len(bits) + 3)), (*dp, *tensor))
    return jax.shard_map(
        functools.partial(body, bits),
        mesh=inner,
        in_specs=(
            P(dp, tensor, None),
            P(dp, None, None),
            P(None, None, dp),
            P(None, None, dp),
            P(None, dp, None, tensor),
            P(None, tensor, dp),
            P(None, dp, tensor),
            P(None, dp, None, tensor),
            P(None, tensor, dp),
            P(None, dp, tensor),
            P(None, tensor, dp),
            P(dp, tensor, None),
        ),
        out_specs=(
            P(dp, tensor, None),
            P(dp, tensor, None),
            P(dp, None, None),
            P(None, None, dp),
            P(None, None, dp),
            P(None, dp, None, tensor),
            P(None, tensor, dp),
            P(None, dp, tensor),
            P(None, dp, None, tensor),
            P(None, tensor, dp),
            P(None, dp, tensor),
            P(None, tensor, dp),
        ),
        check_vma=False,
    )
```

```python
import functools
import jax
import jax.numpy as jnp
from jax import lax
from jax.experimental import pallas as pl
from jax.experimental.pallas import tpu as pltpu
from jax.sharding import Mesh, PartitionSpec as P

HEAD_DIM = 64
NORM_EPS = 1e-05
MASKED = -1e30
TILE = 384
F32 = jnp.float32
BF16 = jnp.bfloat16
MESH = pl.DeviceIdType.MESH
ANY = pl.BlockSpec(memory_space=pl.ANY)


def nn(a, b):
    return lax.dot_general(a, b, (((1,), (0,)), ((), ())), preferred_element_type=F32)


def nt(a, b):
    return lax.dot_general(a, b, (((1,), (1,)), ((), ())), preferred_element_type=F32)


def tn(a, b):
    return lax.dot_general(a, b, (((0,), (0,)), ((), ())), preferred_element_type=F32)


def flip(value, axis):
    return lax.ppermute(value, axis, [(0, 1), (1, 0)])


def diagonal():
    return lax.axis_index("c") == lax.axis_index("zh")


def off_diagonal():
    return lax.rem(lax.axis_index("c") + lax.axis_index("zh"), 2)


def target(kind):
    c, zh = lax.axis_index("c"), lax.axis_index("zh")
    off = off_diagonal()
    if kind == "ring":
        return {"c": lax.rem(c + off, 2), "zh": lax.rem(zh + 1 + off, 2)}
    if kind == "back":
        return {"c": lax.rem(c + 1 + off, 2), "zh": lax.rem(zh + off, 2)}
    if kind == "swap":
        return {"c": 1 - c, "zh": 1 - zh}
    return {kind: 1 - lax.axis_index(kind)}


def greeted(kinds):
    names = []
    for kind in kinds:
        pairs = {"ring": [("c",), ("zh",)], "back": [("c",), ("zh",)],
                 "swap": [("c", "zh")], "stay": []}.get(kind, [(kind,)])
        names += [p for p in pairs if p not in names]
    return names


def greet(kinds):
    barrier = pltpu.get_barrier_semaphore()
    names = greeted(kinds)
    for group in names:
        pl.semaphore_signal(
            barrier, inc=1, device_id={n: 1 - lax.axis_index(n) for n in group},
            device_id_type=MESH,
        )
    pl.semaphore_wait(barrier, len(names))


class Copy:
    def __init__(self, kind, src, dst, send, recv):
        self.kind = kind
        if kind == "stay":
            self.copy = pltpu.make_async_copy(src, dst, send)
        else:
            self.copy = pltpu.make_async_remote_copy(
                src_ref=src, dst_ref=dst, send_sem=send, recv_sem=recv,
                device_id=target(kind), device_id_type=MESH,
            )

    def guarded(self, act):
        if self.kind == "swap":
            pl.when(off_diagonal() == 1)(act)
        elif self.kind == "stay":
            pl.when(off_diagonal() == 0)(act)
        else:
            act()

    def start(self):
        self.guarded(lambda: self.copy.start())

    def wait(self):
        self.guarded(lambda: self.copy.wait())


class Ride:
    def __init__(self, ins, outs, stages, kinds, count, alias=()):
        self.ins, self.outs, self.stages = list(ins), list(outs), stages
        self.kinds, self.alias = list(kinds), dict(alias)
        self.scratch = [pltpu.SemaphoreType.DMA((count,)), pltpu.SemaphoreType.DMA((count,))]

    def chain(self, ins, outs, refs):
        return Chain(self.stages(ins, outs), *refs)


class Chain:
    def __init__(self, stages, send, recv):
        self.copies, place = [], 0
        for stage in stages:
            self.copies.append([])
            for kind, src, dst in stage:
                self.copies[-1].append(Copy(kind, src, dst, send.at[place], recv.at[place]))
                place += 1
        self.level, self.levels, self.until = 0, len(self.copies), len(self.copies)

    def start(self):
        for copy in self.copies[0]:
            copy.start()

    def step(self):
        for copy in self.copies[self.level]:
            copy.wait()
        self.level += 1
        if self.level < self.levels:
            for copy in self.copies[self.level]:
                copy.start()


class Fold(Ride):
    def __init__(self, grad, first, cols, order, blocks, came=None, sums=(), phase="all"):
        self.phase = phase
        if phase == "pair":
            order, blocks = [(None, 2)], 4
        rows = grad.shape[0] // (2 if phase == "pair" else blocks)
        half = rows * blocks // 2
        self.rows, self.first, self.cols = rows, first, cols
        self.order, self.came, self.sums = order, came, list(sums)
        keys = list(range(blocks))
        self.away0 = [k for k in keys if k & order[0][1]]
        self.held = [k for k in keys if not k & order[0][1]]
        self.ins = [grad] + ([came] if came is not None else [])
        self.outs = [jax.ShapeDtypeStruct((rows, cols), F32)]
        self.alias = {}
        self.kinds = [name for name, _ in order[0 if came is None else 1 :]]
        if phase == "exchange":
            self.outs = [jax.ShapeDtypeStruct((2 * rows, cols), BF16)]
        elif phase == "pair":
            self.kinds = ["swap", "back"]
        else:
            self.kinds += ["swap", "back"] + self.sums
        self.scratch = [pltpu.VMEM((half, cols), BF16), pltpu.VMEM((half, cols), BF16)]
        for level in range(1, len(order)):
            self.scratch.append(pltpu.VMEM((half >> level, cols), BF16))
        self.scratch += [
            pltpu.VMEM((2 * rows, cols), BF16),
            pltpu.VMEM((1 + len(self.sums), rows, cols), F32),
            pltpu.SemaphoreType.DMA((blocks + 2,)),
            pltpu.SemaphoreType.DMA((blocks * 2 + 4,)),
            pltpu.SemaphoreType.DMA((blocks * 2 + 4,)),
        ]
        self.levels = len(order) + (1 if phase == "exchange" else 2 + len(self.sums))
        self.until = {"all": self.levels, "exchange": 1, "pair": 0}[phase]

    def chain(self, ins, outs, refs):
        self.in_refs, self.out = ins, outs[0]
        self.own, self.got = refs[0], list(refs[1 : 1 + len(self.order)])
        self.pair, self.total, self.load, self.send, self.recv = refs[1 + len(self.order) :]
        self.level, self.place, self.live = 0, 0, None
        return self

    def remote(self, kind, src, dst):
        copy = Copy(kind, src, dst, self.send.at[self.place], self.recv.at[self.place])
        self.place += 1
        copy.start()
        return copy

    def block(self, at, count=1):
        return pl.ds(at * self.rows, count * self.rows)

    def start(self):
        cols = pl.ds(self.first, self.cols)
        grad = self.in_refs[0]
        self.live, at = [], 0
        if self.phase == "pair":
            self.level = len(self.order)
            copy = pltpu.make_async_copy(grad, self.own, self.load.at[0])
            copy.start()
            self.live = [copy] + [
                self.remote(kind, grad.at[self.block(k)], self.pair.at[self.block(k)])
                for k, kind in enumerate(("swap", "back"))
            ]
            return
        for i, (k, n) in enumerate(runs(self.held)):
            copy = pltpu.make_async_copy(
                grad.at[self.block(k, n), cols], self.own.at[self.block(at, n)], self.load.at[i])
            copy.start()
            self.live.append(copy)
            at += n
        if self.came is not None:
            copy = pltpu.make_async_copy(self.in_refs[1], self.got[0], self.load.at[len(self.live)])
            copy.start()
            self.live.append(copy)
        else:
            at = 0
            for k, n in runs(self.away0):
                self.live.append(self.remote(
                    self.order[0][0], grad.at[self.block(k, n), cols],
                    self.got[0].at[self.block(at, n)]))
                at += n

    def add(self, got, places):
        def one(i, p):
            value = self.own[self.block(p), :].astype(F32) + got[self.block(i), :].astype(F32)
            self.own[self.block(i), :] = value.astype(BF16)

        for i, p in enumerate(places):
            one(i, p)

    def step(self):
        for copy in self.live:
            copy.wait()
        bits = len(self.order)
        level = self.level
        self.level += 1
        if level < bits:
            if level == 0:
                self.add(self.got[0], range(len(self.held)))
            else:
                self.add(self.got[level], self.stay)
                self.held = [self.held[p] for p in self.stay]
            if level + 1 < bits:
                name, weight = self.order[level + 1]
                self.stay = [p for p, k in enumerate(self.held) if not k & weight]
                away = [p for p, k in enumerate(self.held) if k & weight]
                self.live, at = [], 0
                for p, n in runs(away):
                    self.live.append(self.remote(
                        name, self.own.at[self.block(p, n)],
                        self.got[level + 1].at[self.block(at, n)]))
                    at += n
            elif self.phase == "exchange":
                copy = pltpu.make_async_copy(
                    self.own.at[self.block(0, 2)], self.out, self.load.at[0])
                copy.start()
                self.live = [copy]
            else:
                self.live = [
                    self.remote("swap", self.own.at[self.block(0)], self.pair.at[self.block(0)]),
                    self.remote("back", self.own.at[self.block(1)], self.pair.at[self.block(1)]),
                ]
            return
        if self.phase == "exchange":
            return
        if level == bits:
            def diagonal_sum():
                self.total[0] = (self.own[self.block(0), :].astype(F32)
                                 + self.pair[self.block(1), :].astype(F32))

            def other_sum():
                self.total[0] = (self.pair[self.block(0), :].astype(F32)
                                 + self.pair[self.block(1), :].astype(F32))

            pl.when(off_diagonal() == 0)(diagonal_sum)
            pl.when(off_diagonal() == 1)(other_sum)
        elif level <= bits + len(self.sums):
            self.total[0] = self.total[0] + self.total[level - bits]
        else:
            return
        nth = level - bits
        if nth < len(self.sums):
            self.live = [self.remote(self.sums[nth], self.total.at[0], self.total.at[nth + 1])]
        else:
            copy = pltpu.make_async_copy(self.total.at[0], self.out, self.load.at[0])
            copy.start()
            self.live = [copy]


def runs(keys):
    keys, out = sorted(keys), []
    for k in keys:
        if out and out[-1][0] + out[-1][1] == k:
            out[-1][1] += 1
        else:
            out.append([k, 1])
    return out


def pair_ride(shard, blocks):
    rows, cols = shard.shape
    out = jax.ShapeDtypeStruct((rows * blocks, cols), shard.dtype)

    def stages(ins, outs):
        near, far = outs[0].at[pl.ds(0, rows)], outs[0].at[pl.ds(rows, rows)]
        return [[("ring", ins[0], far), ("swap", ins[0], near), ("stay", ins[0], near)]]

    return Ride([shard], [out], stages, ["ring", "swap"], 3)


def spread_ride(buffer, pieces, levels, blocks):
    rows = buffer.shape[0] // blocks
    plan = []
    for level in levels:
        stage = []
        for first, cols, order in pieces:
            held = [0, 1]
            for name, weight in order[:level]:
                held = held + [k + weight for k in held]
            name, weight = order[level]
            for k, n in runs(held):
                stage.append((name, k, k + weight, n, first, cols))
        plan.append(stage)

    def stages(ins, outs):
        ref = outs[0]
        return [
            [
                (name, ref.at[pl.ds(a * rows, n * rows), pl.ds(first, cols)],
                 ref.at[pl.ds(b * rows, n * rows), pl.ds(first, cols)])
                for name, a, b, n, first, cols in stage
            ]
            for stage in plan
        ]

    kinds = [item[0] for stage in plan for item in stage]
    out = jax.ShapeDtypeStruct(buffer.shape, buffer.dtype)
    return Ride([buffer], [out], stages, kinds, sum(len(s) for s in plan), {0: 0})


def chain_ride(shard, pieces, levels, blocks):
    first = pair_ride(shard, blocks)
    rest = spread_ride(first.outs[0], pieces, levels, blocks)

    def stages(ins, outs):
        return first.stages(ins, outs) + rest.stages(ins, outs)

    count = len(first.kinds) + 1 + len(rest.kinds)
    return Ride([shard], first.outs, stages, first.kinds + rest.kinds, count)


def send_ride(value, kind, after=0):
    out = jax.ShapeDtypeStruct(value.shape, value.dtype)
    return Ride([value], [out], lambda ins, outs: [[]] * after + [[(kind, ins[0], outs[0])]],
                [kind], 1)


class Part:
    ins, outs, scratch, kinds = (), (), (), ()

    def early(self, in_refs, out_refs, refs):
        pass

    def begin(self):
        pass

    def run(self, rides):
        pass

    def settle(self):
        pass


class Rides:
    def __init__(self, chains, outs):
        self.chains, self.outs = chains, outs
        for chain in chains:
            chain.start()

    def advance(self, kind=object):
        for chain in self.chains:
            more = chain.levels - chain.level > 1 and chain.level < chain.until
            if more and isinstance(chain, kind):
                chain.step()

    def finish(self, i):
        while self.chains[i].level < self.chains[i].levels:
            self.chains[i].step()

    def end(self):
        for level in range(max([c.levels for c in self.chains], default=0)):
            for chain in self.chains:
                if chain.level == level and level < chain.levels:
                    chain.step()


def launch(name, number, parts, rides, quick=(), limit=62):
    ins = [x for p in parts for x in p.ins]
    outs = [x for p in parts for x in p.outs]
    in_arrays, out_shapes = list(ins), list(outs)
    aliases, spans = {}, []
    for ride in rides:
        for a, b in ride.alias.items():
            aliases[len(in_arrays) + a] = len(out_shapes) + b
        spans.append((len(in_arrays), len(in_arrays) + len(ride.ins),
                      len(out_shapes), len(out_shapes) + len(ride.outs)))
        in_arrays += ride.ins
        out_shapes += ride.outs
    kinds = [k for p in parts for k in p.kinds] + [k for r in rides for k in r.kinds]
    scratch = [x for p in parts for x in p.scratch]
    parts_scratch = len(scratch)
    scratch += [x for r in rides for x in r.scratch]

    def kernel(*refs):
        in_refs = refs[: len(in_arrays)]
        out_refs = refs[len(in_arrays) : len(in_arrays) + len(out_shapes)]
        rest = refs[len(in_arrays) + len(out_shapes) :]
        i, o, c = 0, 0, 0
        for p in parts:
            p.early(in_refs[i : i + len(p.ins)], out_refs[o : o + len(p.outs)],
                    rest[c : c + len(p.scratch)])
            i, o, c = i + len(p.ins), o + len(p.outs), c + len(p.scratch)
        if kinds:
            greet(kinds)
        chains, at = [], parts_scratch
        for ride, (a, b, c, d) in zip(rides, spans):
            more = len(ride.scratch)
            chains.append(ride.chain(in_refs[a:b], out_refs[c:d], rest[at : at + more]))
            at += more
        under_way = Rides(chains, [out_refs[c] for _, _, c, _ in spans])
        for p in parts:
            p.begin()
        for p in parts:
            p.run(under_way)
        for p in parts:
            p.settle()
        if quick:
            under_way.advance(Fold)
        for i in quick:
            under_way.finish(i)
        under_way.end()

    results = pl.pallas_call(
        kernel,
        out_shape=tuple(out_shapes),
        in_specs=[ANY] * len(in_arrays),
        out_specs=tuple([ANY] * len(out_shapes)),
        scratch_shapes=scratch,
        input_output_aliases=aliases,
        name=name,
        compiler_params=pltpu.CompilerParams(
            collective_id=number if kinds else None,
            has_side_effects=bool(kinds),
            vmem_limit_bytes=limit << 20,
        ),
    )(*in_arrays)
    main_outs, at = [], 0
    for p in parts:
        main_outs.append(results[at : at + len(p.outs)])
        at += len(p.outs)
    return main_outs, [results[c:d] for _, _, c, d in spans]


def normalise_value(rows, gain, shift):
    centre = jnp.mean(rows, axis=-1, keepdims=True)
    centred = rows - centre
    spread = jnp.mean(centred * centred, axis=-1, keepdims=True)
    return (centred * lax.rsqrt(spread + NORM_EPS) * gain + shift).astype(BF16)


def gelu_pair(upper):
    cdf = 0.5 * (1.0 + lax.erf(upper * (0.5**0.5)))
    density = jnp.exp(-0.5 * upper * upper) * (0.5 / jnp.pi) ** 0.5
    return (upper * cdf).astype(BF16), (cdf + upper * density).astype(BF16)


class Gather(Part):
    def __init__(self, rows, size, norm, weight, width, n, ending=None, slope=None):
        self.size, self.width, self.n = size, width, n
        self.has_rows, self.has_norm, self.has_slope = rows is not None, norm is not None, slope is not None
        self.double = ending == "gelu"
        self.filler = lambda: None
        self.ride = weight if isinstance(weight, int) else None
        self.kinds = ["c", "zl"]
        self.ins = []
        if self.has_rows:
            self.ins.append(rows)
        if self.ride is None:
            self.ins.append(weight)
        if self.has_norm:
            self.ins.append(jnp.concatenate([norm[0], norm[1]], axis=0))
        if self.has_slope:
            self.ins.append(slope)
        self.outs = [jax.ShapeDtypeStruct((4, size, width), BF16)]
        self.outs += [jax.ShapeDtypeStruct((4, size, n), BF16)] * (2 if self.double else 1)
        tall = self.double or self.has_slope
        self.scratch = [
            pltpu.VMEM((size, width) if self.has_rows else (8, 128), F32),
            pltpu.VMEM((width, n), BF16),
            pltpu.VMEM((2, width), F32),
            pltpu.VMEM((4, size, width), BF16),
            pltpu.VMEM((4, size, n), BF16),
            pltpu.VMEM((4, size, n) if tall else (1, 16, 128), BF16),
            pltpu.SemaphoreType.DMA((4,)),
            pltpu.SemaphoreType.DMA((6,)),
            pltpu.SemaphoreType.DMA((6,)),
            pltpu.SemaphoreType.DMA((3, 4)),
        ]

    def early(self, in_refs, out_refs, refs):
        self.rows, self.w, self.norms, self.x, self.y, self.second = refs[:6]
        self.load, self.send, self.recv, self.store = refs[6:]
        self.out_refs, self.over = out_refs, []
        todo, self.loads = list(in_refs), {}
        if self.has_rows:
            self.loads["rows"] = pltpu.make_async_copy(todo.pop(0), self.rows, self.load.at[0])
        if self.ride is None:
            self.loads["w"] = pltpu.make_async_copy(todo.pop(0), self.w, self.load.at[1])
        if self.has_norm:
            self.loads["norm"] = pltpu.make_async_copy(todo.pop(0), self.norms, self.load.at[2])
        if self.has_slope:
            self.loads["slope"] = pltpu.make_async_copy(todo.pop(0), self.second, self.load.at[3])
        for copy in self.loads.values():
            copy.start()

    def send_half(self, h, source):
        half = self.size // 2
        part = pl.ds(h * half, half)
        if h == 0 and self.has_norm:
            self.loads["norm"].wait()
        value = source[part, :]
        if self.has_norm:
            value = normalise_value(value, self.norms[0:1, :], self.norms[1:2, :])
        x = self.x
        x[0, part, :] = value.astype(BF16)
        self.over.append(
            Copy("zl", x.at[0, part], x.at[2, part], self.send.at[h], self.recv.at[h]))
        self.over[-1].start()
        if h == 1:
            self.beside = Copy("c", x.at[0], x.at[1], self.send.at[2], self.recv.at[2])
            self.beside.start()

    def begin(self):
        if self.has_rows:
            self.loads["rows"].wait()
            for h in range(2):
                self.send_half(h, self.rows)

    def run(self, rides):
        x, y, w, second, n = self.x, self.y, self.w, self.second, self.n
        tile, half = min(TILE, n), self.size // 2
        if self.ride is not None:
            rides.finish(self.ride)
            copy = pltpu.make_async_copy(rides.outs[self.ride], w, self.load.at[1])
            copy.start()
            copy.wait()
        else:
            self.loads["w"].wait()
        if self.has_slope:
            self.loads["slope"].wait()
        stores = []

        def multiply(b):
            def step(j, carry):
                cols = pl.ds(pl.multiple_of(j * tile, tile), tile)
                value = nn(x[b], w[:, cols])
                if self.double:
                    y[b, :, cols], second[b, :, cols] = gelu_pair(value)
                elif self.has_slope:
                    y[b, :, cols] = (value * second[b, :, cols].astype(F32)).astype(BF16)
                else:
                    y[b, :, cols] = value.astype(BF16)
                return carry

            lax.fori_loop(0, n // tile, step, 0)
            for k, ref in enumerate([x, y] + ([second] if self.double else [])):
                stores.append(pltpu.make_async_copy(
                    ref.at[b], self.out_refs[k].at[b], self.store.at[k, b]))
                stores[-1].start()

        multiply(0)
        self.beside.wait()
        multiply(1)
        self.filler()
        relay = []
        for h in range(2):
            part = pl.ds(h * half, half)
            self.over[h].wait()
            relay.append(Copy("c", x.at[2, part], x.at[3, part],
                              self.send.at[3 + h], self.recv.at[3 + h]))
            relay[-1].start()
        multiply(2)
        for copy in relay:
            copy.wait()
        multiply(3)
        for copy in stores:
            copy.wait()


class Scatter(Part):
    def __init__(self, parts, weight, base, norm, fills, hand=None):
        _, size, n = parts.shape
        width = weight.shape[0]
        half = size // 2
        rows = 4 * size
        ins = [parts.reshape(rows, n), weight] + ([base] if base is not None else [])
        if norm is not None:
            ins += list(norm)
        fill_at = len(ins)
        fill_cols = []
        for a, b, _ in fills:
            ins.append(a)
            if b is not None:
                ins.append(b)
            fill_cols.append(n if b is None else b.shape[1])
        outs = [jax.ShapeDtypeStruct((size, width), F32)]
        if norm is not None:
            outs.append(jax.ShapeDtypeStruct((2, width), F32))
        outs += [jax.ShapeDtypeStruct((width, k), BF16) for k in fill_cols]
        sends_at, copies = len(outs), 0
        for _, _, sends in fills:
            for _, rows_away, _, k in sends:
                outs.append(jax.ShapeDtypeStruct((sum(n for _, n in rows_away), k), BF16))
                copies += len(rows_away)
        scratch = [
            pltpu.VMEM((rows, n), BF16),
            pltpu.VMEM((width, n), BF16),
            pltpu.VMEM((size, width), F32),
            pltpu.VMEM((size, width), F32),
            pltpu.VMEM((2, size, width), BF16),
            pltpu.VMEM((2, size, width), BF16),
            pltpu.VMEM((size, width), BF16),
            pltpu.VMEM((size, width), BF16),
            pltpu.SemaphoreType.DMA((8,)),
            pltpu.SemaphoreType.DMA((6,)),
            pltpu.SemaphoreType.DMA((6,)),
        ]
        if norm is not None:
            scratch += [
                pltpu.VMEM((size, width), F32),
                pltpu.VMEM((1, width), F32),
                pltpu.VMEM((size, width), F32),
                pltpu.VMEM((2, width), F32),
                pltpu.SemaphoreType.DMA((4,)),
            ]
        for (a, b, _), k in zip(fills, fill_cols):
            scratch.append(pltpu.VMEM((rows, width), BF16))
            if b is not None:
                scratch.append(pltpu.VMEM((rows, k), BF16))
            scratch += [pltpu.VMEM((width, k), BF16), pltpu.SemaphoreType.DMA((3,))]
        scratch += [pltpu.SemaphoreType.DMA((max(copies, 1),))] * 2
        self.kinds = ["c", "zl"] + [name for _, _, sends in fills for name, _, _, _ in sends]
        self.sends_at = sends_at
        self.ins, self.outs, self.scratch = ins, outs, scratch
        self.facts = (size, n, width, half, base, norm, fills, fill_at, fill_cols, outs)
        self.hand = hand

    def early(self, in_refs, out_refs, refs):
        size, n, width, half, base, norm, fills, fill_at, fill_cols, outs = self.facts
        self.out_refs, self.refs = out_refs, refs
        y, w, total, far, give, came, across, over, load, send, recv = refs[:11]
        refs = list(refs[11:])
        if norm is not None:
            stream, gain, back, sums, norm_sem = refs[:5]
            refs = refs[5:]
        loads = [pltpu.make_async_copy(in_refs[1], w, load.at[0])]
        loads += [
            pltpu.make_async_copy(
                in_refs[0].at[pl.ds(b * size, size)], y.at[pl.ds(b * size, size)],
                load.at[1 + b])
            for b in range(4)
        ]
        if base is not None:
            loads.append(pltpu.make_async_copy(in_refs[2], total, load.at[5]))
        for place in (0, 4, 3, 2, 1, 5)[: len(loads)]:
            loads[place].start()
        others = []
        if norm is not None:
            at = 3 if base is not None else 2
            for i, ref in enumerate((stream, gain, back)):
                others.append(pltpu.make_async_copy(in_refs[at + i], ref, norm_sem.at[i]))
        at = fill_at
        for a, b, _ in fills:
            others.append(pltpu.make_async_copy(in_refs[at], refs[0], refs[2 if b is None else 3].at[0]))
            at += 1
            if b is not None:
                others.append(pltpu.make_async_copy(in_refs[at], refs[1], refs[3].at[1]))
                at += 1
            refs = refs[3 if b is None else 4 :]
        for copy in others:
            copy.start()
        self.loads, self.others = loads, others

    def run(self, rides):
        size, n, width, half, base, norm, fills, fill_at, fill_cols, outs = self.facts
        out_refs, refs = self.out_refs, self.refs
        y, w, total, far, give, came, across, over, load, send, recv = refs[:11]
        refs = list(refs[11:])
        if norm is not None:
            stream, gain, back, sums, norm_sem = refs[:5]
            refs = refs[5:]
        loads, others = self.loads, self.others

        def multiply(b, part, count, put):
            def step(j, carry):
                cols = pl.ds(pl.multiple_of(j * TILE, TILE), TILE)
                put(cols, nt(y[pl.ds(b * size + part, count), :], w[cols, :]))
                return carry

            lax.fori_loop(0, width // TILE, step, 0)

        for place in (0, 4, 3):
            loads[place].wait()
        sent = []
        for h in range(2):
            part = pl.ds(h * half, half)

            def put_give(cols, value, part=part):
                give[0, part, cols] = value.astype(BF16)

            def put_far(cols, value, part=part):
                far[part, cols] = value

            multiply(3, h * half, half, put_give)
            copy = Copy("c", give.at[0, part], came.at[0, part], send.at[h], recv.at[h])
            copy.start()
            multiply(2, h * half, half, put_far)
            copy.wait()
            across[part, :] = (far[part, :] + came[0, part, :].astype(F32)).astype(BF16)
            copy = Copy("zl", across.at[part], over.at[part], send.at[2 + h], recv.at[2 + h])
            copy.start()
            sent.append(copy)
        rides.advance(Fold)
        loads[2].wait()

        def put_near(cols, value):
            give[1, :, cols] = value.astype(BF16)

        multiply(1, 0, size, put_near)
        near = Copy("c", give.at[1], came.at[1], send.at[4], recv.at[4])
        near.start()
        loads[1].wait()
        if base is not None:
            loads[5].wait()

        def put_total(cols, value):
            total[:, cols] = value + (total[:, cols] if base is not None else 0.0)

        multiply(0, 0, size, put_total)
        for copy in others:
            copy.wait()
        stores, fill_refs, refs_all = [], refs, self.refs
        slot = [self.sends_at, 0]

        def fill(k, left, right, result, sem):
            count = fill_cols[k]
            wide = 768 if count % 768 == 0 else count

            def step(j, carry):
                rows_ = pl.ds(pl.multiple_of(j * 256, 256), 256)
                turned = left[:, rows_].T
                for q in range(count // wide):
                    cols = slice(q * wide, (q + 1) * wide)
                    result[rows_, cols] = nn(turned, right[:, cols]).astype(BF16)
                return carry

            lax.fori_loop(0, width // 256, step, 0)
            where = self.sends_at - len(fills) + k
            stores.append(pltpu.make_async_copy(result, out_refs[where], sem.at[2]))
            stores[-1].start()
            for name, rows_away, first, cols in fills[k][2]:
                at = 0
                for row, count in rows_away:
                    copy = Copy(name, result.at[pl.ds(row, count), pl.ds(first, cols)],
                                out_refs[slot[0]].at[pl.ds(at, count)],
                                refs_all[-2].at[slot[1]], refs_all[-1].at[slot[1]])
                    copy.start()
                    stores.append(copy)
                    at += count
                    slot[1] += 1
                slot[0] += 1

        for k, (a, b, _) in enumerate(fills):
            if b is None:
                left, result, sem = fill_refs[:3]
                right, fill_refs = y, fill_refs[3:]
            else:
                left, right, result, sem = fill_refs[:4]
                fill_refs = fill_refs[4:]
            job = functools.partial(fill, k, left, right, result, sem)
            if self.hand is not None and k == len(fills) - 1 and not fills[k][2]:
                self.hand.filler = job
            else:
                job()
        rides.advance()
        near.wait()
        total[...] += came[1].astype(F32)
        for h in range(2):
            part = pl.ds(h * half, half)
            sent[h].wait()
            total[part, :] += over[part, :].astype(F32)
            if norm is not None:
                value = total[part, :]
                rows_in = stream[part, :]
                centred = rows_in - jnp.mean(rows_in, axis=-1, keepdims=True)
                inverse = lax.rsqrt(jnp.mean(centred * centred, axis=-1, keepdims=True) + NORM_EPS)
                unit = centred * inverse
                gain_sum = jnp.sum(value * unit, axis=0, keepdims=True)
                shift_sum = jnp.sum(value, axis=0, keepdims=True)
                sums[0:1, :] = gain_sum if h == 0 else sums[0:1, :] + gain_sum
                sums[1:2, :] = shift_sum if h == 0 else sums[1:2, :] + shift_sum
                scaled = value * gain[...]
                total[part, :] = back[part, :] + inverse * (
                    scaled
                    - jnp.mean(scaled, axis=-1, keepdims=True)
                    - unit * jnp.mean(scaled * unit, axis=-1, keepdims=True)
                )
            if self.hand is not None:
                self.hand.send_half(h, total)
            copy = pltpu.make_async_copy(total.at[part], out_refs[0].at[part], load.at[6 + h])
            copy.start()
            stores.append(copy)
        if norm is not None:
            copy = pltpu.make_async_copy(sums, out_refs[1], norm_sem.at[3])
            copy.start()
            stores.append(copy)
        self.stores = stores

    def settle(self):
        for copy in self.stores:
            copy.wait()


def place_of(i):
    c, zl = lax.axis_index("c"), lax.axis_index("zl")
    dc, dz = i // 2, i % 2
    return (c + dc) % 2 + 2 * ((zl + dz) % 2)


def head_only(value, u):
    lane = lax.broadcasted_iota(jnp.int32, value.shape, 1)
    keep = (lane < HEAD_DIM) if u == 0 else (lane >= HEAD_DIM)
    return jnp.where(keep, value, jnp.zeros_like(value))


def masked(scores):
    key = lax.broadcasted_iota(jnp.int32, scores.shape, 0)
    query = lax.broadcasted_iota(jnp.int32, scores.shape, 1)
    return jnp.where(key <= query, scores, MASKED)


def softmax_parts(parts, value_rows):
    top = parts[0].max(axis=0, keepdims=True)
    for scores in parts[1:]:
        top = jnp.maximum(top, scores.max(axis=0, keepdims=True))
    total, mixed = 0.0, 0.0
    for scores, values in zip(parts, value_rows):
        expo = jnp.exp(scores - top)
        total = total + expo.sum(axis=0, keepdims=True)
        mixed = mixed + nn(values, expo.astype(BF16))
    return mixed / total, top + jnp.log(total)


def softmax_back(scores, slopes, logsum):
    probs = [jnp.exp(s - logsum) for s in scores]
    inner = 0.0
    for p, d in zip(probs, slopes):
        inner = inner + (p * d).sum(axis=0, keepdims=True)
    return [p.astype(BF16) for p in probs], [
        (p * (d - inner)).astype(BF16) for p, d in zip(probs, slopes)
    ]


class Local(Part):
    def __init__(self, ins, outs, scratch, main):
        self.ins, self.outs, self.scratch, self.main = ins, outs, scratch, main

    def early(self, in_refs, out_refs, refs):
        self.refs = (in_refs, out_refs, refs)
        self.stage = self.main(in_refs, out_refs, refs, True)

    def run(self, rides):
        self.main(*self.refs, self.stage, rides)


def attend_self(proj, scale):
    _, size, wide = proj.shape
    cols = wide // 3
    frames, heads = 4 * size, cols // HEAD_DIM
    outs = [jax.ShapeDtypeStruct((4, size, cols), BF16), jax.ShapeDtypeStruct((heads, frames), F32)]
    scratch = [
        pltpu.VMEM((4, size, wide), BF16),
        pltpu.VMEM((frames, 128), BF16),
        pltpu.VMEM((128, frames), BF16),
        pltpu.VMEM((4, size, cols), BF16),
        pltpu.VMEM((heads, frames), F32),
        pltpu.SemaphoreType.DMA((3,)),
    ]

    def main(in_refs, out_refs, refs, stage, rides=None):
        x, keys, values, out, logs, sem = refs
        if stage is True:
            copy = pltpu.make_async_copy(in_refs[0], x, sem.at[0])
            copy.start()
            return copy
        stage.wait()
        for g in range(cols // 128):
            if g:
                rides.advance()
            lanes = [pl.ds(part * cols + g * 128, 128) for part in range(3)]
            for i in range(4):
                rows = pl.ds(i * size, size)
                keys[rows, :] = x[place_of(i), :, lanes[1]]
                values[:, rows] = x[place_of(i), :, lanes[2]].T
            for i in range(4):
                query = x[place_of(i), :, lanes[0]]
                before = i * size
                done = []
                for u in range(2):
                    q = head_only(query, u)
                    mine = pl.ds(u * HEAD_DIM, HEAD_DIM)
                    parts = [masked(nt(keys[pl.ds(before, size), :], q) * scale)]
                    rows = [values[mine, pl.ds(before, size)]]
                    if i:
                        parts.append(nt(keys[pl.ds(0, before), :], q) * scale)
                        rows.append(values[mine, pl.ds(0, before)])
                    mixed, logsum = softmax_parts(parts, rows)
                    done.append(mixed)
                    logs[pl.ds(2 * g + u, 1), pl.ds(before, size)] = logsum
                joined = jnp.concatenate(done, axis=0).T
                out[place_of(i), :, pl.ds(g * 128, 128)] = joined.astype(BF16)
        copies = [pltpu.make_async_copy(out, out_refs[0], sem.at[1]),
                  pltpu.make_async_copy(logs, out_refs[1], sem.at[2])]
        for copy in copies:
            copy.start()
        for copy in copies:
            copy.wait()

    return Local([proj], outs, scratch, main)


def attend_self_back(proj, grad_joined, logsum, scale):
    _, size, wide = proj.shape
    cols = wide // 3
    frames, heads = 4 * size, cols // HEAD_DIM
    outs = [jax.ShapeDtypeStruct((4, size, wide), BF16)]
    scratch = [
        pltpu.VMEM((4, size, wide), BF16),
        pltpu.VMEM((4, size, cols), BF16),
        pltpu.VMEM((heads, frames), F32),
        pltpu.VMEM((frames, 128), BF16),
        pltpu.VMEM((128, frames), BF16),
        pltpu.VMEM((frames, 128), BF16),
        pltpu.VMEM((frames, 128), F32),
        pltpu.VMEM((frames, 128), F32),
        pltpu.VMEM((4, size, wide), BF16),
        pltpu.SemaphoreType.DMA((4,)),
    ]

    def main(in_refs, out_refs, refs, stage, rides=None):
        x, grads, logs, keys, keys_t, values, grad_k, grad_v, out, sem = refs
        if stage is True:
            copies = [
                pltpu.make_async_copy(in_refs[i], ref, sem.at[i])
                for i, ref in enumerate((x, grads, logs))
            ]
            for copy in copies:
                copy.start()
            return copies
        for copy in stage:
            copy.wait()
        for g in range(cols // 128):
            if g < 2:
                rides.advance(Fold)
            lanes = [pl.ds(part * cols + g * 128, 128) for part in range(3)]
            for i in range(4):
                rows = pl.ds(i * size, size)
                keys[rows, :] = x[place_of(i), :, lanes[1]]
                keys_t[:, rows] = x[place_of(i), :, lanes[1]].T
                values[rows, :] = x[place_of(i), :, lanes[2]]
            grad_k[...] = jnp.zeros_like(grad_k)
            grad_v[...] = jnp.zeros_like(grad_v)
            for i in range(4):
                query = x[place_of(i), :, lanes[0]]
                grad = grads[place_of(i), :, lanes[0]]
                before = i * size
                spans = [pl.ds(before, size)] + ([pl.ds(0, before)] if i else [])
                done = []
                for u in range(2):
                    q, go = head_only(query, u), head_only(grad, u)
                    mine = pl.ds(u * HEAD_DIM, HEAD_DIM)
                    scores = [nt(keys[span, :], q) * scale for span in spans]
                    scores[0] = masked(scores[0])
                    slopes = [nt(values[span, :], go) for span in spans]
                    probs, grad_scores = softmax_back(
                        scores, slopes, logs[pl.ds(2 * g + u, 1), pl.ds(before, size)])
                    grad_q = 0.0
                    for span, p, d in zip(spans, probs, grad_scores):
                        grad_v[span, :] += nn(p, go)
                        grad_k[span, :] += nn(d, q)
                        grad_q = grad_q + nn(keys_t[mine, span], d)
                    done.append(grad_q)
                grad_q = jnp.concatenate(done, axis=0).T * scale
                out[place_of(i), :, lanes[0]] = grad_q.astype(BF16)
            for i in range(4):
                rows = pl.ds(i * size, size)
                out[place_of(i), :, lanes[1]] = (grad_k[rows, :] * scale).astype(BF16)
                out[place_of(i), :, lanes[2]] = grad_v[rows, :].astype(BF16)
        copy = pltpu.make_async_copy(out, out_refs[0], sem.at[3])
        copy.start()
        copy.wait()

    return Local([proj, grad_joined, logsum], outs, scratch, main)


def attend_cross(query, text, weight, scale):
    _, size, cols = query.shape
    frames, heads = 4 * size, cols // HEAD_DIM
    states, width = text.shape
    outs = [jax.ShapeDtypeStruct((4, size, cols), BF16), jax.ShapeDtypeStruct((heads, frames), F32),
            jax.ShapeDtypeStruct((states, 2 * cols), BF16)]
    scratch = [
        pltpu.VMEM((4, size, cols), BF16),
        pltpu.VMEM((states, 2 * cols), BF16),
        pltpu.VMEM((4, size, cols), BF16),
        pltpu.VMEM((heads, frames), F32),
        pltpu.VMEM((states, width), BF16),
        pltpu.VMEM((width, 2 * cols), BF16),
        pltpu.SemaphoreType.DMA((6,)),
    ]

    def main(in_refs, out_refs, refs, stage, rides=None):
        x, kv, out, logs, states_in, w, sem = refs
        if stage is True:
            copies = [
                pltpu.make_async_copy(in_refs[i], ref, sem.at[i])
                for i, ref in enumerate((x, states_in, w))
            ]
            for copy in copies:
                copy.start()
            return copies
        for copy in stage:
            copy.wait()
        kv[...] = nn(states_in[...], w[...]).astype(BF16)
        for g in range(cols // 128):
            lanes = pl.ds(g * 128, 128)
            keys = kv[:, lanes]
            values = kv[:, pl.ds(cols + g * 128, 128)].T
            for i in range(4):
                rows = x[i, :, lanes]
                done = []
                for u in range(2):
                    scores = nt(keys, head_only(rows, u)) * scale
                    mixed, logsum = softmax_parts(
                        [scores], [values[u * HEAD_DIM : (u + 1) * HEAD_DIM, :]])
                    done.append(mixed)
                    logs[pl.ds(2 * g + u, 1), pl.ds(i * size, size)] = logsum
                out[i, :, lanes] = jnp.concatenate(done, axis=0).T.astype(BF16)
        copies = [
            pltpu.make_async_copy(ref, out_refs[i], sem.at[3 + i])
            for i, ref in enumerate((out, logs, kv))
        ]
        for copy in copies:
            copy.start()
        for copy in copies:
            copy.wait()

    return Local([query, text, weight], outs, scratch, main)


def attend_cross_back(query, pairs, grad_joined, logsum, text, weight, scale):
    _, size, cols = query.shape
    frames, heads = 4 * size, cols // HEAD_DIM
    states, width = text.shape
    outs = [jax.ShapeDtypeStruct((4, size, cols), BF16),
            jax.ShapeDtypeStruct((width, 2 * cols), BF16),
            jax.ShapeDtypeStruct((states, width), F32)]
    scratch = [
        pltpu.VMEM((4, size, cols), BF16),
        pltpu.VMEM((states, 2 * cols), BF16),
        pltpu.VMEM((4, size, cols), BF16),
        pltpu.VMEM((heads, frames), F32),
        pltpu.VMEM((states, width), BF16),
        pltpu.VMEM((width, 2 * cols), BF16),
        pltpu.VMEM((4, size, cols), BF16),
        pltpu.VMEM((states, 2 * cols), BF16),
        pltpu.VMEM((width, 2 * cols), BF16),
        pltpu.VMEM((states, width), F32),
        pltpu.SemaphoreType.DMA((9,)),
    ]

    def main(in_refs, out_refs, refs, stage, rides=None):
        x, kv, grads, logs, states_in, w, out, out_kv, out_w, out_text, sem = refs
        if stage is True:
            copies = [
                pltpu.make_async_copy(in_refs[i], ref, sem.at[i])
                for i, ref in enumerate((x, kv, grads, logs, states_in, w))
            ]
            for copy in copies:
                copy.start()
            return copies
        for copy in stage:
            copy.wait()
        for g in range(cols // 128):
            if g:
                rides.advance()
            lanes, lanes_v = pl.ds(g * 128, 128), pl.ds(cols + g * 128, 128)
            keys, values = kv[:, lanes], kv[:, lanes_v]
            keys_t = keys.T
            grad_k, grad_v = 0.0, 0.0
            for i in range(4):
                done = []
                for u in range(2):
                    q, go = head_only(x[i, :, lanes], u), head_only(grads[i, :, lanes], u)
                    scores = nt(keys, q) * scale
                    probs, grad_scores = softmax_back(
                        [scores], [nt(values, go)],
                        logs[pl.ds(2 * g + u, 1), pl.ds(i * size, size)])
                    grad_v = grad_v + nn(probs[0], go)
                    grad_k = grad_k + nn(grad_scores[0], q)
                    done.append(nn(keys_t[u * HEAD_DIM : (u + 1) * HEAD_DIM, :], grad_scores[0]))
                out[i, :, lanes] = (jnp.concatenate(done, axis=0).T * scale).astype(BF16)
            out_kv[:, lanes] = (grad_k * scale).astype(BF16)
            out_kv[:, lanes_v] = grad_v.astype(BF16)
        grad_pairs = out_kv[...]
        out_w[...] = nn(states_in[...].T, grad_pairs).astype(BF16)
        out_text[...] = nt(grad_pairs, w[...])
        copies = [
            pltpu.make_async_copy(ref, out_refs[i], sem.at[6 + i])
            for i, ref in enumerate((out, out_w, out_text))
        ]
        for copy in copies:
            copy.start()
        for copy in copies:
            copy.wait()

    return Local([query, pairs, grad_joined, logsum, text, weight], outs, scratch, main)


def flat(parts):
    return parts.reshape(-1, parts.shape[-1])


def body(bits, frames_in, text_states, ln_gain, ln_bias, w_self, w_self_out, w_cross_q,
         w_cross_kv, w_cross_out, w_up, w_down, cotangent):
    scale = float(HEAD_DIM) ** (-0.5)
    layers = w_self.shape[0]
    width = frames_in.shape[2]
    part = w_self.shape[1]
    blocks = width // part
    cols = w_self.shape[3]
    hidden = w_up.shape[2]
    me = lax.axis_index("zh")
    for place, name in enumerate(reversed(bits)):
        me = me + (lax.axis_index(name) << (place + 1))

    row = lax.broadcasted_iota(jnp.int32, (width, width), 0)
    col = lax.broadcasted_iota(jnp.int32, (width, width), 1)
    permute = ((row // part == ((col // part) ^ me)) & (row % part == col % part)).astype(BF16)

    def reorder(value):
        return nn(value, permute)

    up = [(name, 2 << (len(bits) - 1 - place)) for place, name in enumerate(bits)]
    low_first = list(reversed(up))
    levels = len(bits)
    early, late = list(range(levels // 2)), list(range(levels // 2, levels))
    sizes = {"self": 3 * cols, "self_out": cols, "q": cols, "kv": 2 * cols, "out": cols,
             "up": hidden, "down": hidden, "norm": 128}

    def halves(name):
        n = sizes[name]
        if name in ("self", "kv", "up", "down"):
            first = (n // 2 + 127) // 128 * 128
            return [(0, first, low_first), (first, n - first, up)]
        return [(0, n, low_first if name in ("q", "norm") else up)]

    packs = {"a": "self", "o": "self_out", "q": "q", "k": "kv", "u": "out", "c": "up", "d": "down"}
    norm_rows = jnp.concatenate([ln_gain.reshape(-1, part), ln_bias.reshape(-1, part)], axis=0).T
    norm_rows = jnp.pad(norm_rows, ((0, 0), (0, sizes["norm"] - norm_rows.shape[1])))
    shards = {}
    for l in range(layers):
        shards[l, "self"] = w_self[l].reshape(part, 3 * cols)
        shards[l, "self_out"] = w_self_out[l].T
        shards[l, "q"] = w_cross_q[l]
        shards[l, "kv"] = w_cross_kv[l].reshape(part, 2 * cols)
        shards[l, "out"] = w_cross_out[l].T
        shards[l, "up"] = w_up[l]
        shards[l, "down"] = w_down[l].T
    held = {}
    counter = [0]

    def number():
        counter[0] += 1
        return counter[0] - 1

    def forward(parts, todo=(), more=()):
        rides, keys = [], []
        for word in todo:
            l, name, stage = int(word[0]), packs[word[1]], int(word[2])
            if l >= layers:
                continue
            if stage == 1:
                rides.append(pair_ride(shards[l, name], blocks))
            else:
                which = {2: early, 3: late, 4: early + late}[stage]
                rides.append(spread_ride(held[l, name], halves(name), which, blocks))
            keys.append((l, name))
        outs, extra = launch(f"step_{counter[0]}", number(), parts, rides + list(more))
        for key, value in zip(keys, extra):
            held[key] = value[0]
        return outs, [e[0] for e in extra[len(keys):]]

    def move(rides, quick=()):
        return launch(f"move_{counter[0]}", number(), [], rides, quick)[1]

    extra = move([
        chain_ride(shards[0, "self"], halves("self"), early, blocks),
        chain_ride(norm_rows, halves("norm"), early + late, blocks),
        send_ride(text_states[0], "c"),
        send_ride(frames_in[0], "swap", 1),
    ])
    held[0, "self"], norms, text_far, frames_far = [e[0] for e in extra]
    stream = reorder(jnp.where(diagonal(), frames_in[0], frames_far))
    text_own = reorder(jnp.where(diagonal(), text_states[0], text_far)).astype(BF16)
    norms = norms.astype(F32).T
    gains = norms[: 3 * layers].reshape(layers, 3, 1, width)
    shifts = norms[3 * layers : 6 * layers].reshape(layers, 3, 1, width)
    size = stream.shape[0]

    def norm_of(l, j):
        return gains[l, j], shifts[l, j]

    records = []
    (((first, proj),), _) = forward(
        [Gather(stream, size, norm_of(0, 0), 0, width, 3 * cols)], ["0a3", "0o1", "0q1", "0k1", "0u1"])
    for l in range(layers):
        n = l + 1
        saved = {"one": stream, "first": first, "proj": proj}
        (((joined, logsum),), _) = forward(
            [attend_self(proj, scale)], [f"{l}o4", f"{l}q4", f"{l}c1"])
        saved.update(joined_self=joined, logsum_self=logsum)
        hand = Gather(None, size, norm_of(l, 1), held[l, "q"], width, cols)
        (((stream,), (second, query)), _) = forward(
            [Scatter(joined, held[l, "self_out"], stream, None, [], hand), hand],
            [f"{l}k4", f"{l}u4", f"{l}c2", f"{l}d1"])
        saved.update(two=stream, second=second, query=query)

        (((joined, logsum, pairs),), _) = forward(
            [attend_cross(query, text_own, held[l, "kv"], scale)], [f"{l}d2", f"{n}k1"])
        saved.update(pairs=pairs, joined_cross=joined, logsum_cross=logsum)
        hand = Gather(None, size, norm_of(l, 2), 0, width, hidden, "gelu")
        more = [send_ride(cotangent[0], "swap")] if n == layers else []
        (((stream,), (third, active, slope)), extra) = forward(
            [Scatter(joined, held[l, "out"], stream, None, [], hand), hand],
            [f"{l}c3", f"{l}d3", f"{n}a1"], more)
        saved.update(three=stream, third=third, active=active, slope=slope)
        records.append(saved)

        if n < layers:
            hand = Gather(None, size, norm_of(n, 0), 0, width, 3 * cols)
            (((stream,), (first, proj)), _) = forward(
                [Scatter(active, held[l, "down"], stream, None, [], hand), hand],
                [f"{n}a4", f"{n}o1", f"{n}q1", f"{n}u1"])
        else:
            grad = reorder(jnp.where(diagonal(), cotangent[0], extra[0]))
            gather = Gather(grad, size, None, held[l, "down"], width, hidden, slope=slope)
            (((stream,), (full, grad_upper)), _) = forward(
                [Scatter(active, held[l, "down"], stream, None, []), gather])
    result_own = reorder(stream.astype(BF16)).astype(BF16)

    folding = []
    finished = {}
    grad_text = jnp.zeros((text_own.shape[0], width), F32)
    norm_grads = {}

    def fold_later(l, name, value, came=None):
        for i, (first, n, order) in enumerate(halves(name)):
            folding.append({"key": (l, name, first), "grad": value.astype(BF16), "first": first,
                            "cols": n, "order": list(reversed(order)),
                            "came": came[i] if came else None, "pair": None})

    def first_sends(name):
        sends = []
        for first, n, order in halves(name):
            axis, weight = order[-1]
            away = runs([k for k in range(blocks) if k & weight])
            sends.append((axis, [(k * part, count * part) for k, count in away], first, n))
        return sends

    def fold_ride(item, phase="all"):
        if phase == "pair":
            return Fold(item["pair"], 0, item["cols"], None, 4, phase=phase)
        sums = ("zl", "zh") if item["key"][1] == "norm" else ()
        return Fold(item["grad"], item["first"], item["cols"], item["order"], blocks,
                    item["came"], sums, phase)

    def first_ride(item):
        name, weight = item["order"][0]
        away = runs([k for k in range(blocks) if k & weight])
        grad, first, n = item["grad"], item["first"], item["cols"]
        out = jax.ShapeDtypeStruct((grad.shape[0] // 2, n), BF16)

        def stages(ins, outs):
            copies, at = [], 0
            for k, count in away:
                copies.append((name, ins[0].at[pl.ds(k * part, count * part), pl.ds(first, n)],
                               outs[0].at[pl.ds(at * part, count * part)]))
                at += count
            return [copies]

        return Ride([grad], [out], stages, [name] * len(away), len(away))

    def folds(parts, begin=(), exchange=(), pair=(), end=(), more=()):
        def of(names):
            return [i for i in folding if i["key"][:2] in names]

        begins, exchanges, pairs, ends = of(begin), of(exchange), of(pair), of(end)
        rides = [first_ride(i) for i in begins]
        rides += [fold_ride(i, "exchange") for i in exchanges]
        rides += [fold_ride(i, "pair") for i in pairs]
        rides += [fold_ride(i) for i in ends]
        outs, extra = launch(f"step_{counter[0]}", number(), parts, rides + list(more))
        extra = [e[0] for e in extra]
        for item in begins:
            item["came"] = extra.pop(0)
        for item in exchanges:
            item["pair"] = extra.pop(0)
        for item in pairs + ends:
            finished[item["key"]] = extra.pop(0)
            folding.remove(item)
        return outs, extra

    for l in reversed(range(layers)):
        saved = records[l]
        more = [send_ride(result_own, "swap")] if l == layers - 1 else []
        hand = Gather(None, size, None, held[l, "out"], width, cols)
        fills = [(flat(full), flat(saved["active"]), first_sends("down")),
                 (flat(saved["third"]), None, [])]
        (((grad, norm_grads[l, 2], down, up_, *came), (full, grad_joined)), extra) = folds(
            [Scatter(grad_upper, held[l, "up"], None, (saved["three"], gains[l, 2], grad), fills,
                     hand), hand], exchange=[(l + 1, "self_out"), (l + 1, "self")],
            pair=[(l + 1, "out"), (l + 1, "q"), (l + 1, "kv")], more=more)
        if more:
            result = jnp.where(diagonal(), result_own, extra[0])
        fold_later(l, "down", down, came)
        fold_later(l, "up", up_)

        (((grad_query, kv_, text_part),), _) = folds(
            [attend_cross_back(saved["query"], saved["pairs"], grad_joined,
                               saved["logsum_cross"], text_own, held[l, "kv"], scale)],
            begin=[(l, "up")], pair=[(l + 1, "self_out"), (l + 1, "self")])
        grad_text = grad_text + text_part
        fold_later(l, "kv", kv_)
        more = [send_ride(grad_text.astype(BF16), "c")] if l == 0 else []
        hand = Gather(None, size, None, held[l, "self_out"], width, cols)
        fills = [(flat(full), flat(saved["joined_cross"]), first_sends("out")),
                 (flat(saved["second"]), None, first_sends("q"))]
        (((grad, norm_grads[l, 1], out_, q_, *came), (full, grad_joined)), extra) = folds(
            [Scatter(grad_query, held[l, "q"], None, (saved["two"], gains[l, 1], grad), fills,
                     hand), hand], begin=[(l, "kv")], exchange=[(l, "down")], more=more)
        fold_later(l, "out", out_, came[:1])
        fold_later(l, "q", q_, came[1:])
        if more:
            grad_text = grad_text.astype(BF16).astype(F32) + extra[0].astype(F32)
            more = [send_ride(grad_text.astype(BF16), "zl")]

        (((grad_proj,),), extra) = folds(
            [attend_self_back(saved["proj"], grad_joined, saved["logsum_self"], scale)],
            exchange=[(l, "up")], pair=[(l, "down")], more=more)
        if more:
            grad_text = grad_text.astype(BF16).astype(F32) + extra[0].astype(F32)
        fills = [(flat(full), flat(saved["joined_self"]), first_sends("self_out")),
                 (flat(saved["first"]), None, first_sends("self"))]
        chain = (saved["one"], gains[l, 0], grad)
        parts = [Scatter(grad_proj, held[l, "self"], None, chain, fills)]
        if l:
            hand = Gather(None, size, None, held[l - 1, "down"], width, hidden,
                          slope=records[l - 1]["slope"])
            parts = [Scatter(grad_proj, held[l, "self"], None, chain, fills, hand), hand]
        (((grad, norm_grads[l, 0], out_, self_, *came), *after), _) = folds(
            parts, pair=[(l, "up")],
            **{"exchange" if l else "end": [(l, "out"), (l, "q"), (l, "kv")]})
        if l:
            ((full, grad_upper),) = after
        fold_later(l, "self_out", out_, came[:1])
        fold_later(l, "self", self_, came[1:])

    small = [norm_grads[l, j][k] for l in range(layers) for k in range(2) for j in range(3)]
    small = jnp.stack(small, axis=1)
    small = jnp.pad(small, ((0, 0), (0, sizes["norm"] - small.shape[1])))
    fold_later(0, "norm", small)
    frames_back = reorder(grad.astype(BF16)).astype(BF16)
    text_back = reorder(grad_text.astype(BF16)).astype(BF16)
    folds_left = [fold_ride(item) for item in folding]
    quick = [i for i, item in enumerate(folding) if item["key"][1] == "norm"]
    extra = move(
        folds_left + [send_ride(frames_back, "swap"), send_ride(text_back, "swap")], quick)
    for item, came in zip(folding, extra):
        finished[item["key"]] = came[0]
    grad_frames, text_sum = [
        jnp.where(diagonal(), mine, came[0]).astype(F32)
        for mine, came in zip((frames_back, text_back), extra[len(folds_left):])
    ]
    small = finished[0, "norm", 0][:, : 6 * layers]
    small = small.T.reshape(layers, 6, part)

    def gradient(l, name):
        pieces = [finished[l, name, first] for first, _, _ in halves(name)]
        return jnp.concatenate(pieces, axis=1) if len(pieces) > 1 else pieces[0]

    def stacked(name, shape=None, turned=False):
        members = [gradient(l, name) for l in range(layers)]
        if turned:
            members = [m.T for m in members]
        if shape is not None:
            members = [m.reshape(shape) for m in members]
        return jnp.stack(members)

    return (
        result[None],
        grad_frames[None],
        text_sum[None],
        small[:, :3],
        small[:, 3:],
        stacked("self", (part, 3, cols)),
        stacked("self_out", turned=True),
        stacked("q"),
        stacked("kv", (part, 2, cols)),
        stacked("out", turned=True),
        stacked("up"),
        stacked("down", turned=True),
    )


def solution(mesh):
    count = mesh.shape["dp"]
    bits = tuple(f"b{i}" for i in range(count.bit_length() - 2))
    dp = (*bits, "c")
    tensor = ("zh", "zl")
    inner = Mesh(mesh.devices.reshape((2,) * (len(bits) + 3)), (*dp, *tensor))
    return jax.shard_map(
        functools.partial(body, bits),
        mesh=inner,
        in_specs=(
            P(dp, tensor, None),
            P(dp, None, None),
            P(None, None, dp),
            P(None, None, dp),
            P(None, dp, None, tensor),
            P(None, tensor, dp),
            P(None, dp, tensor),
            P(None, dp, None, tensor),
            P(None, tensor, dp),
            P(None, dp, tensor),
            P(None, tensor, dp),
            P(dp, tensor, None),
        ),
        out_specs=(
            P(dp, tensor, None),
            P(dp, tensor, None),
            P(dp, None, None),
            P(None, None, dp),
            P(None, None, dp),
            P(None, dp, None, tensor),
            P(None, tensor, dp),
            P(None, dp, tensor),
            P(None, dp, None, tensor),
            P(None, tensor, dp),
            P(None, dp, tensor),
            P(None, tensor, dp),
        ),
        check_vma=False,
    )
```

```python
import functools
import jax
import jax.numpy as jnp
from jax import lax
from jax.experimental import pallas as pl
from jax.experimental.pallas import tpu as pltpu
from jax.sharding import Mesh, PartitionSpec as P

HEAD_DIM = 64
NORM_EPS = 1e-05
MASKED = -1e30
TILE = 384
F32 = jnp.float32
BF16 = jnp.bfloat16
MESH = pl.DeviceIdType.MESH
ANY = pl.BlockSpec(memory_space=pl.ANY)


def nn(a, b):
    return lax.dot_general(a, b, (((1,), (0,)), ((), ())), preferred_element_type=F32)


def nt(a, b):
    return lax.dot_general(a, b, (((1,), (1,)), ((), ())), preferred_element_type=F32)


def tn(a, b):
    return lax.dot_general(a, b, (((0,), (0,)), ((), ())), preferred_element_type=F32)


def flip(value, axis):
    return lax.ppermute(value, axis, [(0, 1), (1, 0)])


def diagonal():
    return lax.axis_index("c") == lax.axis_index("zh")


def off_diagonal():
    return lax.rem(lax.axis_index("c") + lax.axis_index("zh"), 2)


def target(kind):
    c, zh = lax.axis_index("c"), lax.axis_index("zh")
    off = off_diagonal()
    if kind == "ring":
        return {"c": lax.rem(c + off, 2), "zh": lax.rem(zh + 1 + off, 2)}
    if kind == "back":
        return {"c": lax.rem(c + 1 + off, 2), "zh": lax.rem(zh + off, 2)}
    if kind == "swap":
        return {"c": 1 - c, "zh": 1 - zh}
    return {kind: 1 - lax.axis_index(kind)}


def greeted(kinds):
    names = []
    for kind in kinds:
        pairs = {"ring": [("c",), ("zh",)], "back": [("c",), ("zh",)],
                 "swap": [("c", "zh")], "stay": []}.get(kind, [(kind,)])
        names += [p for p in pairs if p not in names]
    return names


def greet(kinds):
    barrier = pltpu.get_barrier_semaphore()
    names = greeted(kinds)
    for group in names:
        pl.semaphore_signal(
            barrier, inc=1, device_id={n: 1 - lax.axis_index(n) for n in group},
            device_id_type=MESH,
        )
    pl.semaphore_wait(barrier, len(names))


class Copy:
    def __init__(self, kind, src, dst, send, recv):
        self.kind = kind
        if kind == "stay":
            self.copy = pltpu.make_async_copy(src, dst, send)
        else:
            self.copy = pltpu.make_async_remote_copy(
                src_ref=src, dst_ref=dst, send_sem=send, recv_sem=recv,
                device_id=target(kind), device_id_type=MESH,
            )

    def guarded(self, act):
        if self.kind == "swap":
            pl.when(off_diagonal() == 1)(act)
        elif self.kind == "stay":
            pl.when(off_diagonal() == 0)(act)
        else:
            act()

    def start(self):
        self.guarded(lambda: self.copy.start())

    def wait(self):
        self.guarded(lambda: self.copy.wait())


class Ride:
    def __init__(self, ins, outs, stages, kinds, count, alias=()):
        self.ins, self.outs, self.stages = list(ins), list(outs), stages
        self.kinds, self.alias = list(kinds), dict(alias)
        self.scratch = [pltpu.SemaphoreType.DMA((count,)), pltpu.SemaphoreType.DMA((count,))]

    def chain(self, ins, outs, refs):
        return Chain(self.stages(ins, outs), *refs)


class Chain:
    def __init__(self, stages, send, recv):
        self.copies, place = [], 0
        for stage in stages:
            self.copies.append([])
            for kind, src, dst in stage:
                self.copies[-1].append(Copy(kind, src, dst, send.at[place], recv.at[place]))
                place += 1
        self.level, self.levels, self.until = 0, len(self.copies), len(self.copies)

    def start(self):
        for copy in self.copies[0]:
            copy.start()

    def step(self):
        for copy in self.copies[self.level]:
            copy.wait()
        self.level += 1
        if self.level < self.levels:
            for copy in self.copies[self.level]:
                copy.start()


class Fold(Ride):
    def __init__(self, grad, first, cols, order, blocks, came=None, sums=(), phase="all"):
        self.phase = phase
        if phase == "pair":
            order, blocks = [(None, 2)], 4
        rows = grad.shape[0] // (2 if phase == "pair" else blocks)
        half = rows * blocks // 2
        self.rows, self.first, self.cols = rows, first, cols
        self.order, self.came, self.sums = order, came, list(sums)
        keys = list(range(blocks))
        self.away0 = [k for k in keys if k & order[0][1]]
        self.held = [k for k in keys if not k & order[0][1]]
        self.ins = [grad] + ([came] if came is not None else [])
        self.outs = [jax.ShapeDtypeStruct((rows, cols), F32)]
        self.alias = {}
        self.kinds = [name for name, _ in order[0 if came is None else 1 :]]
        if phase == "exchange":
            self.outs = [jax.ShapeDtypeStruct((2 * rows, cols), BF16)]
        elif phase == "pair":
            self.kinds = ["swap", "back"]
        else:
            self.kinds += ["swap", "back"] + self.sums
        self.scratch = [pltpu.VMEM((half, cols), BF16), pltpu.VMEM((half, cols), BF16)]
        for level in range(1, len(order)):
            self.scratch.append(pltpu.VMEM((half >> level, cols), BF16))
        self.scratch += [
            pltpu.VMEM((2 * rows, cols), BF16),
            pltpu.VMEM((1 + len(self.sums), rows, cols), F32),
            pltpu.SemaphoreType.DMA((blocks + 2,)),
            pltpu.SemaphoreType.DMA((blocks * 2 + 4,)),
            pltpu.SemaphoreType.DMA((blocks * 2 + 4,)),
        ]
        self.levels = len(order) + (1 if phase == "exchange" else 2 + len(self.sums))
        self.until = {"all": self.levels, "exchange": 1, "pair": 0}[phase]

    def chain(self, ins, outs, refs):
        self.in_refs, self.out = ins, outs[0]
        self.own, self.got = refs[0], list(refs[1 : 1 + len(self.order)])
        self.pair, self.total, self.load, self.send, self.recv = refs[1 + len(self.order) :]
        self.level, self.place, self.live = 0, 0, None
        return self

    def remote(self, kind, src, dst):
        copy = Copy(kind, src, dst, self.send.at[self.place], self.recv.at[self.place])
        self.place += 1
        copy.start()
        return copy

    def block(self, at, count=1):
        return pl.ds(at * self.rows, count * self.rows)

    def start(self):
        cols = pl.ds(self.first, self.cols)
        grad = self.in_refs[0]
        self.live, at = [], 0
        if self.phase == "pair":
            self.level = len(self.order)
            copy = pltpu.make_async_copy(grad, self.own, self.load.at[0])
            copy.start()
            self.live = [copy] + [
                self.remote(kind, grad.at[self.block(k)], self.pair.at[self.block(k)])
                for k, kind in enumerate(("swap", "back"))
            ]
            return
        for i, (k, n) in enumerate(runs(self.held)):
            copy = pltpu.make_async_copy(
                grad.at[self.block(k, n), cols], self.own.at[self.block(at, n)], self.load.at[i])
            copy.start()
            self.live.append(copy)
            at += n
        if self.came is not None:
            copy = pltpu.make_async_copy(self.in_refs[1], self.got[0], self.load.at[len(self.live)])
            copy.start()
            self.live.append(copy)
        else:
            at = 0
            for k, n in runs(self.away0):
                self.live.append(self.remote(
                    self.order[0][0], grad.at[self.block(k, n), cols],
                    self.got[0].at[self.block(at, n)]))
                at += n

    def add(self, got, places):
        def one(i, p):
            value = self.own[self.block(p), :].astype(F32) + got[self.block(i), :].astype(F32)
            self.own[self.block(i), :] = value.astype(BF16)

        for i, p in enumerate(places):
            one(i, p)

    def step(self):
        for copy in self.live:
            copy.wait()
        bits = len(self.order)
        level = self.level
        self.level += 1
        if level < bits:
            if level == 0:
                self.add(self.got[0], range(len(self.held)))
            else:
                self.add(self.got[level], self.stay)
                self.held = [self.held[p] for p in self.stay]
            if level + 1 < bits:
                name, weight = self.order[level + 1]
                self.stay = [p for p, k in enumerate(self.held) if not k & weight]
                away = [p for p, k in enumerate(self.held) if k & weight]
                self.live, at = [], 0
                for p, n in runs(away):
                    self.live.append(self.remote(
                        name, self.own.at[self.block(p, n)],
                        self.got[level + 1].at[self.block(at, n)]))
                    at += n
            elif self.phase == "exchange":
                copy = pltpu.make_async_copy(
                    self.own.at[self.block(0, 2)], self.out, self.load.at[0])
                copy.start()
                self.live = [copy]
            else:
                self.live = [
                    self.remote("swap", self.own.at[self.block(0)], self.pair.at[self.block(0)]),
                    self.remote("back", self.own.at[self.block(1)], self.pair.at[self.block(1)]),
                ]
            return
        if self.phase == "exchange":
            return
        if level == bits:
            def diagonal_sum():
                self.total[0] = (self.own[self.block(0), :].astype(F32)
                                 + self.pair[self.block(1), :].astype(F32))

            def other_sum():
                self.total[0] = (self.pair[self.block(0), :].astype(F32)
                                 + self.pair[self.block(1), :].astype(F32))

            pl.when(off_diagonal() == 0)(diagonal_sum)
            pl.when(off_diagonal() == 1)(other_sum)
        elif level <= bits + len(self.sums):
            self.total[0] = self.total[0] + self.total[level - bits]
        else:
            return
        nth = level - bits
        if nth < len(self.sums):
            self.live = [self.remote(self.sums[nth], self.total.at[0], self.total.at[nth + 1])]
        else:
            copy = pltpu.make_async_copy(self.total.at[0], self.out, self.load.at[0])
            copy.start()
            self.live = [copy]


def runs(keys):
    keys, out = sorted(keys), []
    for k in keys:
        if out and out[-1][0] + out[-1][1] == k:
            out[-1][1] += 1
        else:
            out.append([k, 1])
    return out


def pair_ride(shard, blocks):
    rows, cols = shard.shape
    out = jax.ShapeDtypeStruct((rows * blocks, cols), shard.dtype)

    def stages(ins, outs):
        near, far = outs[0].at[pl.ds(0, rows)], outs[0].at[pl.ds(rows, rows)]
        return [[("ring", ins[0], far), ("swap", ins[0], near), ("stay", ins[0], near)]]

    return Ride([shard], [out], stages, ["ring", "swap"], 3)


def spread_ride(buffer, pieces, levels, blocks):
    rows = buffer.shape[0] // blocks
    plan = []
    for level in levels:
        stage = []
        for first, cols, order in pieces:
            held = [0, 1]
            for name, weight in order[:level]:
                held = held + [k + weight for k in held]
            name, weight = order[level]
            for k, n in runs(held):
                stage.append((name, k, k + weight, n, first, cols))
        plan.append(stage)

    def stages(ins, outs):
        ref = outs[0]
        return [
            [
                (name, ref.at[pl.ds(a * rows, n * rows), pl.ds(first, cols)],
                 ref.at[pl.ds(b * rows, n * rows), pl.ds(first, cols)])
                for name, a, b, n, first, cols in stage
            ]
            for stage in plan
        ]

    kinds = [item[0] for stage in plan for item in stage]
    out = jax.ShapeDtypeStruct(buffer.shape, buffer.dtype)
    return Ride([buffer], [out], stages, kinds, sum(len(s) for s in plan), {0: 0})


def chain_ride(shard, pieces, levels, blocks):
    first = pair_ride(shard, blocks)
    rest = spread_ride(first.outs[0], pieces, levels, blocks)

    def stages(ins, outs):
        return first.stages(ins, outs) + rest.stages(ins, outs)

    count = len(first.kinds) + 1 + len(rest.kinds)
    return Ride([shard], first.outs, stages, first.kinds + rest.kinds, count)


def send_ride(value, kind, after=0):
    out = jax.ShapeDtypeStruct(value.shape, value.dtype)
    return Ride([value], [out], lambda ins, outs: [[]] * after + [[(kind, ins[0], outs[0])]],
                [kind], 1)


class Part:
    ins, outs, scratch, kinds = (), (), (), ()

    def early(self, in_refs, out_refs, refs):
        pass

    def begin(self):
        pass

    def run(self, rides):
        pass

    def settle(self):
        pass


class Rides:
    def __init__(self, chains, outs):
        self.chains, self.outs = chains, outs
        for chain in chains:
            chain.start()

    def advance(self, kind=object):
        for chain in self.chains:
            more = chain.levels - chain.level > 1 and chain.level < chain.until
            if more and isinstance(chain, kind):
                chain.step()

    def finish(self, i):
        while self.chains[i].level < self.chains[i].levels:
            self.chains[i].step()

    def end(self):
        for level in range(max([c.levels for c in self.chains], default=0)):
            for chain in self.chains:
                if chain.level == level and level < chain.levels:
                    chain.step()


def launch(name, number, parts, rides, quick=(), limit=62):
    ins = [x for p in parts for x in p.ins]
    outs = [x for p in parts for x in p.outs]
    in_arrays, out_shapes = list(ins), list(outs)
    aliases, spans = {}, []
    for ride in rides:
        for a, b in ride.alias.items():
            aliases[len(in_arrays) + a] = len(out_shapes) + b
        spans.append((len(in_arrays), len(in_arrays) + len(ride.ins),
                      len(out_shapes), len(out_shapes) + len(ride.outs)))
        in_arrays += ride.ins
        out_shapes += ride.outs
    kinds = [k for p in parts for k in p.kinds] + [k for r in rides for k in r.kinds]
    scratch = [x for p in parts for x in p.scratch]
    parts_scratch = len(scratch)
    scratch += [x for r in rides for x in r.scratch]

    def kernel(*refs):
        in_refs = refs[: len(in_arrays)]
        out_refs = refs[len(in_arrays) : len(in_arrays) + len(out_shapes)]
        rest = refs[len(in_arrays) + len(out_shapes) :]
        i, o, c = 0, 0, 0
        for p in parts:
            p.early(in_refs[i : i + len(p.ins)], out_refs[o : o + len(p.outs)],
                    rest[c : c + len(p.scratch)])
            i, o, c = i + len(p.ins), o + len(p.outs), c + len(p.scratch)
        if kinds:
            greet(kinds)
        chains, at = [], parts_scratch
        for ride, (a, b, c, d) in zip(rides, spans):
            more = len(ride.scratch)
            chains.append(ride.chain(in_refs[a:b], out_refs[c:d], rest[at : at + more]))
            at += more
        under_way = Rides(chains, [out_refs[c] for _, _, c, _ in spans])
        for p in parts:
            p.begin()
        for p in parts:
            p.run(under_way)
        for p in parts:
            p.settle()
        if quick:
            under_way.advance(Fold)
        for i in quick:
            under_way.finish(i)
        under_way.end()

    results = pl.pallas_call(
        kernel,
        out_shape=tuple(out_shapes),
        in_specs=[ANY] * len(in_arrays),
        out_specs=tuple([ANY] * len(out_shapes)),
        scratch_shapes=scratch,
        input_output_aliases=aliases,
        name=name,
        compiler_params=pltpu.CompilerParams(
            collective_id=number if kinds else None,
            has_side_effects=bool(kinds),
            vmem_limit_bytes=limit << 20,
        ),
    )(*in_arrays)
    main_outs, at = [], 0
    for p in parts:
        main_outs.append(results[at : at + len(p.outs)])
        at += len(p.outs)
    return main_outs, [results[c:d] for _, _, c, d in spans]


def normalise_value(rows, gain, shift):
    centre = jnp.mean(rows, axis=-1, keepdims=True)
    centred = rows - centre
    spread = jnp.mean(centred * centred, axis=-1, keepdims=True)
    return (centred * lax.rsqrt(spread + NORM_EPS) * gain + shift).astype(BF16)


def gelu_pair(upper):
    cdf = 0.5 * (1.0 + lax.erf(upper * (0.5**0.5)))
    density = jnp.exp(-0.5 * upper * upper) * (0.5 / jnp.pi) ** 0.5
    return (upper * cdf).astype(BF16), (cdf + upper * density).astype(BF16)


class Gather(Part):
    def __init__(self, rows, size, norm, weight, width, n, ending=None, slope=None):
        self.size, self.width, self.n = size, width, n
        self.has_rows, self.has_norm, self.has_slope = rows is not None, norm is not None, slope is not None
        self.double = ending == "gelu"
        self.filler = lambda: None
        self.ride = weight if isinstance(weight, int) else None
        self.kinds = ["c", "zl"]
        self.ins = []
        if self.has_rows:
            self.ins.append(rows)
        if self.ride is None:
            self.ins.append(weight)
        if self.has_norm:
            self.ins.append(jnp.concatenate([norm[0], norm[1]], axis=0))
        if self.has_slope:
            self.ins.append(slope)
        self.outs = [jax.ShapeDtypeStruct((4, size, width), BF16)]
        self.outs += [jax.ShapeDtypeStruct((4, size, n), BF16)] * (2 if self.double else 1)
        tall = self.double or self.has_slope
        self.scratch = [
            pltpu.VMEM((size, width) if self.has_rows else (8, 128), F32),
            pltpu.VMEM((width, n), BF16),
            pltpu.VMEM((2, width), F32),
            pltpu.VMEM((4, size, width), BF16),
            pltpu.VMEM((4, size, n), BF16),
            pltpu.VMEM((4, size, n) if tall else (1, 16, 128), BF16),
            pltpu.SemaphoreType.DMA((4,)),
            pltpu.SemaphoreType.DMA((6,)),
            pltpu.SemaphoreType.DMA((6,)),
            pltpu.SemaphoreType.DMA((3, 6)),
        ]

    def early(self, in_refs, out_refs, refs):
        self.rows, self.w, self.norms, self.x, self.y, self.second = refs[:6]
        self.load, self.send, self.recv, self.store = refs[6:]
        self.out_refs, self.over = out_refs, []
        todo, self.loads = list(in_refs), {}
        if self.has_rows:
            self.loads["rows"] = pltpu.make_async_copy(todo.pop(0), self.rows, self.load.at[0])
        if self.ride is None:
            self.loads["w"] = pltpu.make_async_copy(todo.pop(0), self.w, self.load.at[1])
        if self.has_norm:
            self.loads["norm"] = pltpu.make_async_copy(todo.pop(0), self.norms, self.load.at[2])
        if self.has_slope:
            self.loads["slope"] = pltpu.make_async_copy(todo.pop(0), self.second, self.load.at[3])
        for copy in self.loads.values():
            copy.start()

    def send_half(self, h, source):
        half = self.size // 2
        part = pl.ds(h * half, half)
        if h == 0 and self.has_norm:
            self.loads["norm"].wait()
        value = source[part, :]
        if self.has_norm:
            value = normalise_value(value, self.norms[0:1, :], self.norms[1:2, :])
        x = self.x
        x[0, part, :] = value.astype(BF16)
        self.over.append(
            Copy("zl", x.at[0, part], x.at[2, part], self.send.at[h], self.recv.at[h]))
        self.over[-1].start()
        if h == 1:
            self.beside = Copy("c", x.at[0], x.at[1], self.send.at[2], self.recv.at[2])
            self.beside.start()

    def begin(self):
        if self.has_rows:
            self.loads["rows"].wait()
            for h in range(2):
                self.send_half(h, self.rows)

    def run(self, rides):
        x, y, w, second, n = self.x, self.y, self.w, self.second, self.n
        tile, half = min(TILE, n), self.size // 2
        if self.ride is not None:
            rides.finish(self.ride)
            copy = pltpu.make_async_copy(rides.outs[self.ride], w, self.load.at[1])
            copy.start()
            copy.wait()
        else:
            self.loads["w"].wait()
        if self.has_slope:
            self.loads["slope"].wait()
        stores = []

        def multiply(b, rows, slot):
            def step(j, carry):
                cols = pl.ds(pl.multiple_of(j * tile, tile), tile)
                value = nn(x[b, rows, :], w[:, cols])
                if self.double:
                    y[b, rows, cols], second[b, rows, cols] = gelu_pair(value)
                elif self.has_slope:
                    y[b, rows, cols] = (value * second[b, rows, cols].astype(F32)).astype(BF16)
                else:
                    y[b, rows, cols] = value.astype(BF16)
                return carry

            lax.fori_loop(0, n // tile, step, 0)
            for k, ref in enumerate([x, y] + ([second] if self.double else [])):
                stores.append(pltpu.make_async_copy(
                    ref.at[b, rows], self.out_refs[k].at[b, rows], self.store.at[k, slot]))
                stores[-1].start()

        whole = pl.ds(0, self.size)

        multiply(0, whole, 0)
        self.beside.wait()
        multiply(1, whole, 1)
        self.filler()
        for h in range(2):
            part = pl.ds(h * half, half)
            self.over[h].wait()
            relay = Copy("c", x.at[2, part], x.at[3, part], self.send.at[3 + h], self.recv.at[3 + h])
            relay.start()
            multiply(2, part, 2 + h)
            relay.wait()
            multiply(3, part, 4 + h)
        for copy in stores:
            copy.wait()


class Scatter(Part):
    def __init__(self, parts, weight, base, norm, fills, hand=None):
        _, size, n = parts.shape
        width = weight.shape[0]
        half = size // 2
        rows = 4 * size
        ins = [parts.reshape(rows, n), weight] + ([base] if base is not None else [])
        if norm is not None:
            ins += list(norm)
        fill_at = len(ins)
        fill_cols = []
        for a, b, _ in fills:
            ins.append(a)
            if b is not None:
                ins.append(b)
            fill_cols.append(n if b is None else b.shape[1])
        outs = [jax.ShapeDtypeStruct((size, width), F32)]
        if norm is not None:
            outs.append(jax.ShapeDtypeStruct((2, width), F32))
        outs += [jax.ShapeDtypeStruct((width, k), BF16) for k in fill_cols]
        sends_at, copies = len(outs), 0
        for _, _, sends in fills:
            for _, rows_away, _, k in sends:
                outs.append(jax.ShapeDtypeStruct((sum(n for _, n in rows_away), k), BF16))
                copies += len(rows_away)
        scratch = [
            pltpu.VMEM((rows, n), BF16),
            pltpu.VMEM((width, n), BF16),
            pltpu.VMEM((size, width), F32),
            pltpu.VMEM((size, width), F32),
            pltpu.VMEM((2, size, width), BF16),
            pltpu.VMEM((2, size, width), BF16),
            pltpu.VMEM((size, width), BF16),
            pltpu.VMEM((size, width), BF16),
            pltpu.SemaphoreType.DMA((8,)),
            pltpu.SemaphoreType.DMA((6,)),
            pltpu.SemaphoreType.DMA((6,)),
        ]
        if norm is not None:
            scratch += [
                pltpu.VMEM((size, width), F32),
                pltpu.VMEM((1, width), F32),
                pltpu.VMEM((size, width), F32),
                pltpu.VMEM((2, width), F32),
                pltpu.SemaphoreType.DMA((4,)),
            ]
        for (a, b, _), k in zip(fills, fill_cols):
            scratch.append(pltpu.VMEM((rows, width), BF16))
            if b is not None:
                scratch.append(pltpu.VMEM((rows, k), BF16))
            scratch += [pltpu.VMEM((width, k), BF16), pltpu.SemaphoreType.DMA((3,))]
        scratch += [pltpu.SemaphoreType.DMA((max(copies, 1),))] * 2
        self.kinds = ["c", "zl"] + [name for _, _, sends in fills for name, _, _, _ in sends]
        self.sends_at = sends_at
        self.ins, self.outs, self.scratch = ins, outs, scratch
        self.facts = (size, n, width, half, base, norm, fills, fill_at, fill_cols, outs)
        self.hand = hand

    def early(self, in_refs, out_refs, refs):
        size, n, width, half, base, norm, fills, fill_at, fill_cols, outs = self.facts
        self.out_refs, self.refs = out_refs, refs
        y, w, total, far, give, came, across, over, load, send, recv = refs[:11]
        refs = list(refs[11:])
        if norm is not None:
            stream, gain, back, sums, norm_sem = refs[:5]
            refs = refs[5:]
        loads = [pltpu.make_async_copy(in_refs[1], w, load.at[0])]
        loads += [
            pltpu.make_async_copy(
                in_refs[0].at[pl.ds(b * size, size)], y.at[pl.ds(b * size, size)],
                load.at[1 + b])
            for b in range(4)
        ]
        if base is not None:
            loads.append(pltpu.make_async_copy(in_refs[2], total, load.at[5]))
        for place in (0, 4, 3, 2, 1, 5)[: len(loads)]:
            loads[place].start()
        others = []
        if norm is not None:
            at = 3 if base is not None else 2
            for i, ref in enumerate((stream, gain, back)):
                others.append(pltpu.make_async_copy(in_refs[at + i], ref, norm_sem.at[i]))
        at = fill_at
        for a, b, _ in fills:
            others.append(pltpu.make_async_copy(in_refs[at], refs[0], refs[2 if b is None else 3].at[0]))
            at += 1
            if b is not None:
                others.append(pltpu.make_async_copy(in_refs[at], refs[1], refs[3].at[1]))
                at += 1
            refs = refs[3 if b is None else 4 :]
        for copy in others:
            copy.start()
        self.loads, self.others = loads, others

    def run(self, rides):
        size, n, width, half, base, norm, fills, fill_at, fill_cols, outs = self.facts
        out_refs, refs = self.out_refs, self.refs
        y, w, total, far, give, came, across, over, load, send, recv = refs[:11]
        refs = list(refs[11:])
        if norm is not None:
            stream, gain, back, sums, norm_sem = refs[:5]
            refs = refs[5:]
        loads, others = self.loads, self.others

        def multiply(b, part, count, put):
            def step(j, carry):
                cols = pl.ds(pl.multiple_of(j * TILE, TILE), TILE)
                put(cols, nt(y[pl.ds(b * size + part, count), :], w[cols, :]))
                return carry

            lax.fori_loop(0, width // TILE, step, 0)

        for place in (0, 4, 3):
            loads[place].wait()
        sent = []
        for h in range(2):
            part = pl.ds(h * half, half)

            def put_give(cols, value, part=part):
                give[0, part, cols] = value.astype(BF16)

            def put_far(cols, value, part=part):
                far[part, cols] = value

            multiply(3, h * half, half, put_give)
            copy = Copy("c", give.at[0, part], came.at[0, part], send.at[h], recv.at[h])
            copy.start()
            multiply(2, h * half, half, put_far)
            copy.wait()
            across[part, :] = (far[part, :] + came[0, part, :].astype(F32)).astype(BF16)
            copy = Copy("zl", across.at[part], over.at[part], send.at[2 + h], recv.at[2 + h])
            copy.start()
            sent.append(copy)
        rides.advance(Fold)
        loads[2].wait()

        def put_near(cols, value):
            give[1, :, cols] = value.astype(BF16)

        multiply(1, 0, size, put_near)
        near = Copy("c", give.at[1], came.at[1], send.at[4], recv.at[4])
        near.start()
        loads[1].wait()
        if base is not None:
            loads[5].wait()

        def put_total(cols, value):
            total[:, cols] = value + (total[:, cols] if base is not None else 0.0)

        multiply(0, 0, size, put_total)
        for copy in others:
            copy.wait()
        stores, fill_refs, refs_all = [], refs, self.refs
        slot = [self.sends_at, 0]

        def fill(k, left, right, result, sem):
            count = fill_cols[k]
            wide = 768 if count % 768 == 0 else count

            def step(j, carry):
                rows_ = pl.ds(pl.multiple_of(j * 256, 256), 256)
                turned = left[:, rows_].T
                for q in range(count // wide):
                    cols = slice(q * wide, (q + 1) * wide)
                    result[rows_, cols] = nn(turned, right[:, cols]).astype(BF16)
                return carry

            lax.fori_loop(0, width // 256, step, 0)
            where = self.sends_at - len(fills) + k
            stores.append(pltpu.make_async_copy(result, out_refs[where], sem.at[2]))
            stores[-1].start()
            for name, rows_away, first, cols in fills[k][2]:
                at = 0
                for row, count in rows_away:
                    copy = Copy(name, result.at[pl.ds(row, count), pl.ds(first, cols)],
                                out_refs[slot[0]].at[pl.ds(at, count)],
                                refs_all[-2].at[slot[1]], refs_all[-1].at[slot[1]])
                    copy.start()
                    stores.append(copy)
                    at += count
                    slot[1] += 1
                slot[0] += 1

        for k, (a, b, _) in enumerate(fills):
            if b is None:
                left, result, sem = fill_refs[:3]
                right, fill_refs = y, fill_refs[3:]
            else:
                left, right, result, sem = fill_refs[:4]
                fill_refs = fill_refs[4:]
            job = functools.partial(fill, k, left, right, result, sem)
            if self.hand is not None and k == len(fills) - 1 and not fills[k][2]:
                self.hand.filler = job
            else:
                job()
        rides.advance()
        near.wait()
        total[...] += came[1].astype(F32)
        for h in range(2):
            part = pl.ds(h * half, half)
            sent[h].wait()
            total[part, :] += over[part, :].astype(F32)
            if norm is not None:
                value = total[part, :]
                rows_in = stream[part, :]
                centred = rows_in - jnp.mean(rows_in, axis=-1, keepdims=True)
                inverse = lax.rsqrt(jnp.mean(centred * centred, axis=-1, keepdims=True) + NORM_EPS)
                unit = centred * inverse
                gain_sum = jnp.sum(value * unit, axis=0, keepdims=True)
                shift_sum = jnp.sum(value, axis=0, keepdims=True)
                sums[0:1, :] = gain_sum if h == 0 else sums[0:1, :] + gain_sum
                sums[1:2, :] = shift_sum if h == 0 else sums[1:2, :] + shift_sum
                scaled = value * gain[...]
                total[part, :] = back[part, :] + inverse * (
                    scaled
                    - jnp.mean(scaled, axis=-1, keepdims=True)
                    - unit * jnp.mean(scaled * unit, axis=-1, keepdims=True)
                )
            if self.hand is not None:
                self.hand.send_half(h, total)
            copy = pltpu.make_async_copy(total.at[part], out_refs[0].at[part], load.at[6 + h])
            copy.start()
            stores.append(copy)
        if norm is not None:
            copy = pltpu.make_async_copy(sums, out_refs[1], norm_sem.at[3])
            copy.start()
            stores.append(copy)
        self.stores = stores

    def settle(self):
        for copy in self.stores:
            copy.wait()


def place_of(i):
    c, zl = lax.axis_index("c"), lax.axis_index("zl")
    dc, dz = i // 2, i % 2
    return (c + dc) % 2 + 2 * ((zl + dz) % 2)


def head_only(value, u):
    lane = lax.broadcasted_iota(jnp.int32, value.shape, 1)
    keep = (lane < HEAD_DIM) if u == 0 else (lane >= HEAD_DIM)
    return jnp.where(keep, value, jnp.zeros_like(value))


def masked(scores):
    key = lax.broadcasted_iota(jnp.int32, scores.shape, 0)
    query = lax.broadcasted_iota(jnp.int32, scores.shape, 1)
    return jnp.where(key <= query, scores, MASKED)


def softmax_parts(parts, value_rows):
    top = parts[0].max(axis=0, keepdims=True)
    for scores in parts[1:]:
        top = jnp.maximum(top, scores.max(axis=0, keepdims=True))
    total, mixed = 0.0, 0.0
    for scores, values in zip(parts, value_rows):
        expo = jnp.exp(scores - top)
        total = total + expo.sum(axis=0, keepdims=True)
        mixed = mixed + nn(values, expo.astype(BF16))
    return mixed / total, top + jnp.log(total)


def softmax_back(scores, slopes, logsum):
    probs = [jnp.exp(s - logsum) for s in scores]
    inner = 0.0
    for p, d in zip(probs, slopes):
        inner = inner + (p * d).sum(axis=0, keepdims=True)
    return [p.astype(BF16) for p in probs], [
        (p * (d - inner)).astype(BF16) for p, d in zip(probs, slopes)
    ]


class Local(Part):
    def __init__(self, ins, outs, scratch, main):
        self.ins, self.outs, self.scratch, self.main = ins, outs, scratch, main

    def early(self, in_refs, out_refs, refs):
        self.refs = (in_refs, out_refs, refs)
        self.stage = self.main(in_refs, out_refs, refs, True)

    def run(self, rides):
        self.main(*self.refs, self.stage, rides)


def attend_self(proj, scale):
    _, size, wide = proj.shape
    cols = wide // 3
    frames, heads = 4 * size, cols // HEAD_DIM
    outs = [jax.ShapeDtypeStruct((4, size, cols), BF16), jax.ShapeDtypeStruct((heads, frames), F32)]
    scratch = [
        pltpu.VMEM((4, size, wide), BF16),
        pltpu.VMEM((frames, 128), BF16),
        pltpu.VMEM((128, frames), BF16),
        pltpu.VMEM((4, size, cols), BF16),
        pltpu.VMEM((heads, frames), F32),
        pltpu.SemaphoreType.DMA((3,)),
    ]

    def main(in_refs, out_refs, refs, stage, rides=None):
        x, keys, values, out, logs, sem = refs
        if stage is True:
            copy = pltpu.make_async_copy(in_refs[0], x, sem.at[0])
            copy.start()
            return copy
        stage.wait()
        for g in range(cols // 128):
            if g:
                rides.advance()
            lanes = [pl.ds(part * cols + g * 128, 128) for part in range(3)]
            for i in range(4):
                rows = pl.ds(i * size, size)
                keys[rows, :] = x[place_of(i), :, lanes[1]]
                values[:, rows] = x[place_of(i), :, lanes[2]].T
            for i in range(4):
                query = x[place_of(i), :, lanes[0]]
                before = i * size
                done = []
                for u in range(2):
                    q = head_only(query, u)
                    mine = pl.ds(u * HEAD_DIM, HEAD_DIM)
                    parts = [masked(nt(keys[pl.ds(before, size), :], q) * scale)]
                    rows = [values[mine, pl.ds(before, size)]]
                    if i:
                        parts.append(nt(keys[pl.ds(0, before), :], q) * scale)
                        rows.append(values[mine, pl.ds(0, before)])
                    mixed, logsum = softmax_parts(parts, rows)
                    done.append(mixed)
                    logs[pl.ds(2 * g + u, 1), pl.ds(before, size)] = logsum
                joined = jnp.concatenate(done, axis=0).T
                out[place_of(i), :, pl.ds(g * 128, 128)] = joined.astype(BF16)
        copies = [pltpu.make_async_copy(out, out_refs[0], sem.at[1]),
                  pltpu.make_async_copy(logs, out_refs[1], sem.at[2])]
        for copy in copies:
            copy.start()
        for copy in copies:
            copy.wait()

    return Local([proj], outs, scratch, main)


def attend_self_back(proj, grad_joined, logsum, scale):
    _, size, wide = proj.shape
    cols = wide // 3
    frames, heads = 4 * size, cols // HEAD_DIM
    outs = [jax.ShapeDtypeStruct((4, size, wide), BF16)]
    scratch = [
        pltpu.VMEM((4, size, wide), BF16),
        pltpu.VMEM((4, size, cols), BF16),
        pltpu.VMEM((heads, frames), F32),
        pltpu.VMEM((frames, 128), BF16),
        pltpu.VMEM((128, frames), BF16),
        pltpu.VMEM((frames, 128), BF16),
        pltpu.VMEM((frames, 128), F32),
        pltpu.VMEM((frames, 128), F32),
        pltpu.VMEM((4, size, wide), BF16),
        pltpu.SemaphoreType.DMA((4,)),
    ]

    def main(in_refs, out_refs, refs, stage, rides=None):
        x, grads, logs, keys, keys_t, values, grad_k, grad_v, out, sem = refs
        if stage is True:
            copies = [
                pltpu.make_async_copy(in_refs[i], ref, sem.at[i])
                for i, ref in enumerate((x, grads, logs))
            ]
            for copy in copies:
                copy.start()
            return copies
        for copy in stage:
            copy.wait()
        for g in range(cols // 128):
            if g < 2:
                rides.advance(Fold)
            lanes = [pl.ds(part * cols + g * 128, 128) for part in range(3)]
            for i in range(4):
                rows = pl.ds(i * size, size)
                keys[rows, :] = x[place_of(i), :, lanes[1]]
                keys_t[:, rows] = x[place_of(i), :, lanes[1]].T
                values[rows, :] = x[place_of(i), :, lanes[2]]
            grad_k[...] = jnp.zeros_like(grad_k)
            grad_v[...] = jnp.zeros_like(grad_v)
            for i in range(4):
                query = x[place_of(i), :, lanes[0]]
                grad = grads[place_of(i), :, lanes[0]]
                before = i * size
                spans = [pl.ds(before, size)] + ([pl.ds(0, before)] if i else [])
                done = []
                for u in range(2):
                    q, go = head_only(query, u), head_only(grad, u)
                    mine = pl.ds(u * HEAD_DIM, HEAD_DIM)
                    scores = [nt(keys[span, :], q) * scale for span in spans]
                    scores[0] = masked(scores[0])
                    slopes = [nt(values[span, :], go) for span in spans]
                    probs, grad_scores = softmax_back(
                        scores, slopes, logs[pl.ds(2 * g + u, 1), pl.ds(before, size)])
                    grad_q = 0.0
                    for span, p, d in zip(spans, probs, grad_scores):
                        grad_v[span, :] += nn(p, go)
                        grad_k[span, :] += nn(d, q)
                        grad_q = grad_q + nn(keys_t[mine, span], d)
                    done.append(grad_q)
                grad_q = jnp.concatenate(done, axis=0).T * scale
                out[place_of(i), :, lanes[0]] = grad_q.astype(BF16)
            for i in range(4):
                rows = pl.ds(i * size, size)
                out[place_of(i), :, lanes[1]] = (grad_k[rows, :] * scale).astype(BF16)
                out[place_of(i), :, lanes[2]] = grad_v[rows, :].astype(BF16)
        copy = pltpu.make_async_copy(out, out_refs[0], sem.at[3])
        copy.start()
        copy.wait()

    return Local([proj, grad_joined, logsum], outs, scratch, main)


def attend_cross(query, text, weight, scale):
    _, size, cols = query.shape
    frames, heads = 4 * size, cols // HEAD_DIM
    states, width = text.shape
    outs = [jax.ShapeDtypeStruct((4, size, cols), BF16), jax.ShapeDtypeStruct((heads, frames), F32),
            jax.ShapeDtypeStruct((states, 2 * cols), BF16)]
    scratch = [
        pltpu.VMEM((4, size, cols), BF16),
        pltpu.VMEM((states, 2 * cols), BF16),
        pltpu.VMEM((4, size, cols), BF16),
        pltpu.VMEM((heads, frames), F32),
        pltpu.VMEM((states, width), BF16),
        pltpu.VMEM((width, 2 * cols), BF16),
        pltpu.SemaphoreType.DMA((6,)),
    ]

    def main(in_refs, out_refs, refs, stage, rides=None):
        x, kv, out, logs, states_in, w, sem = refs
        if stage is True:
            copies = [
                pltpu.make_async_copy(in_refs[i], ref, sem.at[i])
                for i, ref in enumerate((x, states_in, w))
            ]
            for copy in copies:
                copy.start()
            return copies
        for copy in stage:
            copy.wait()
        kv[...] = nn(states_in[...], w[...]).astype(BF16)
        for g in range(cols // 128):
            lanes = pl.ds(g * 128, 128)
            keys = kv[:, lanes]
            values = kv[:, pl.ds(cols + g * 128, 128)].T
            for i in range(4):
                rows = x[i, :, lanes]
                done = []
                for u in range(2):
                    scores = nt(keys, head_only(rows, u)) * scale
                    mixed, logsum = softmax_parts(
                        [scores], [values[u * HEAD_DIM : (u + 1) * HEAD_DIM, :]])
                    done.append(mixed)
                    logs[pl.ds(2 * g + u, 1), pl.ds(i * size, size)] = logsum
                out[i, :, lanes] = jnp.concatenate(done, axis=0).T.astype(BF16)
        copies = [
            pltpu.make_async_copy(ref, out_refs[i], sem.at[3 + i])
            for i, ref in enumerate((out, logs, kv))
        ]
        for copy in copies:
            copy.start()
        for copy in copies:
            copy.wait()

    return Local([query, text, weight], outs, scratch, main)


def attend_cross_back(query, pairs, grad_joined, logsum, text, weight, scale):
    _, size, cols = query.shape
    frames, heads = 4 * size, cols // HEAD_DIM
    states, width = text.shape
    outs = [jax.ShapeDtypeStruct((4, size, cols), BF16),
            jax.ShapeDtypeStruct((width, 2 * cols), BF16),
            jax.ShapeDtypeStruct((states, width), F32)]
    scratch = [
        pltpu.VMEM((4, size, cols), BF16),
        pltpu.VMEM((states, 2 * cols), BF16),
        pltpu.VMEM((4, size, cols), BF16),
        pltpu.VMEM((heads, frames), F32),
        pltpu.VMEM((states, width), BF16),
        pltpu.VMEM((width, 2 * cols), BF16),
        pltpu.VMEM((4, size, cols), BF16),
        pltpu.VMEM((states, 2 * cols), BF16),
        pltpu.VMEM((width, 2 * cols), BF16),
        pltpu.VMEM((states, width), F32),
        pltpu.SemaphoreType.DMA((9,)),
    ]

    def main(in_refs, out_refs, refs, stage, rides=None):
        x, kv, grads, logs, states_in, w, out, out_kv, out_w, out_text, sem = refs
        if stage is True:
            copies = [
                pltpu.make_async_copy(in_refs[i], ref, sem.at[i])
                for i, ref in enumerate((x, kv, grads, logs, states_in, w))
            ]
            for copy in copies:
                copy.start()
            return copies
        for copy in stage:
            copy.wait()
        for g in range(cols // 128):
            if g:
                rides.advance()
            lanes, lanes_v = pl.ds(g * 128, 128), pl.ds(cols + g * 128, 128)
            keys, values = kv[:, lanes], kv[:, lanes_v]
            keys_t = keys.T
            grad_k, grad_v = 0.0, 0.0
            for i in range(4):
                done = []
                for u in range(2):
                    q, go = head_only(x[i, :, lanes], u), head_only(grads[i, :, lanes], u)
                    scores = nt(keys, q) * scale
                    probs, grad_scores = softmax_back(
                        [scores], [nt(values, go)],
                        logs[pl.ds(2 * g + u, 1), pl.ds(i * size, size)])
                    grad_v = grad_v + nn(probs[0], go)
                    grad_k = grad_k + nn(grad_scores[0], q)
                    done.append(nn(keys_t[u * HEAD_DIM : (u + 1) * HEAD_DIM, :], grad_scores[0]))
                out[i, :, lanes] = (jnp.concatenate(done, axis=0).T * scale).astype(BF16)
            out_kv[:, lanes] = (grad_k * scale).astype(BF16)
            out_kv[:, lanes_v] = grad_v.astype(BF16)
        grad_pairs = out_kv[...]
        out_w[...] = nn(states_in[...].T, grad_pairs).astype(BF16)
        out_text[...] = nt(grad_pairs, w[...])
        copies = [
            pltpu.make_async_copy(ref, out_refs[i], sem.at[6 + i])
            for i, ref in enumerate((out, out_w, out_text))
        ]
        for copy in copies:
            copy.start()
        for copy in copies:
            copy.wait()

    return Local([query, pairs, grad_joined, logsum, text, weight], outs, scratch, main)


def flat(parts):
    return parts.reshape(-1, parts.shape[-1])


def body(bits, frames_in, text_states, ln_gain, ln_bias, w_self, w_self_out, w_cross_q,
         w_cross_kv, w_cross_out, w_up, w_down, cotangent):
    scale = float(HEAD_DIM) ** (-0.5)
    layers = w_self.shape[0]
    width = frames_in.shape[2]
    part = w_self.shape[1]
    blocks = width // part
    cols = w_self.shape[3]
    hidden = w_up.shape[2]
    me = lax.axis_index("zh")
    for place, name in enumerate(reversed(bits)):
        me = me + (lax.axis_index(name) << (place + 1))

    row = lax.broadcasted_iota(jnp.int32, (width, width), 0)
    col = lax.broadcasted_iota(jnp.int32, (width, width), 1)
    permute = ((row // part == ((col // part) ^ me)) & (row % part == col % part)).astype(BF16)
    permute = lax.optimization_barrier(permute)

    def reorder(value):
        return nn(value, permute)

    up = [(name, 2 << (len(bits) - 1 - place)) for place, name in enumerate(bits)]
    low_first = list(reversed(up))
    levels = len(bits)
    early, late = list(range(levels // 2)), list(range(levels // 2, levels))
    sizes = {"self": 3 * cols, "self_out": cols, "q": cols, "kv": 2 * cols, "out": cols,
             "up": hidden, "down": hidden, "norm": 128}

    def halves(name):
        n = sizes[name]
        if name == "up":
            return [(i * n // 4, n // 4, up if i % 2 else low_first) for i in range(4)]
        if name in ("self", "kv", "down"):
            first = (n // 2 + 127) // 128 * 128
            return [(0, first, low_first), (first, n - first, up)]
        return [(0, n, low_first if name in ("q", "norm") else up)]

    packs = {"a": "self", "o": "self_out", "q": "q", "k": "kv", "u": "out", "c": "up", "d": "down"}
    norm_rows = jnp.concatenate([ln_gain.reshape(-1, part), ln_bias.reshape(-1, part)], axis=0).T
    norm_rows = jnp.pad(norm_rows, ((0, 0), (0, sizes["norm"] - norm_rows.shape[1])))
    shards = {}
    for l in range(layers):
        shards[l, "self"] = w_self[l].reshape(part, 3 * cols)
        shards[l, "self_out"] = w_self_out[l].T
        shards[l, "q"] = w_cross_q[l]
        shards[l, "kv"] = w_cross_kv[l].reshape(part, 2 * cols)
        shards[l, "out"] = w_cross_out[l].T
        shards[l, "up"] = w_up[l]
        shards[l, "down"] = w_down[l].T
    held = {}
    counter = [0]

    def number():
        counter[0] += 1
        return counter[0] - 1

    def forward(parts, todo=(), more=()):
        rides, keys = [], []
        for word in todo:
            l, name, stage = int(word[0]), packs[word[1]], int(word[2])
            if l >= layers:
                continue
            if stage == 1:
                rides.append(pair_ride(shards[l, name], blocks))
            else:
                which = {2: early, 3: late, 4: early + late}[stage]
                rides.append(spread_ride(held[l, name], halves(name), which, blocks))
            keys.append((l, name))
        outs, extra = launch(f"step_{counter[0]}", number(), parts, rides + list(more))
        for key, value in zip(keys, extra):
            held[key] = value[0]
        return outs, [e[0] for e in extra[len(keys):]]

    def move(rides, quick=()):
        return launch(f"move_{counter[0]}", number(), [], rides, quick)[1]

    extra = move([
        chain_ride(shards[0, "self"], halves("self"), early, blocks),
        chain_ride(norm_rows, halves("norm"), early + late, blocks),
        send_ride(text_states[0], "c"),
        send_ride(frames_in[0], "swap", 1),
    ])
    held[0, "self"], norms, text_far, frames_far = [e[0] for e in extra]
    stream = reorder(jnp.where(diagonal(), frames_in[0], frames_far))
    text_own = reorder(jnp.where(diagonal(), text_states[0], text_far)).astype(BF16)
    norms = norms.astype(F32).T
    gains = norms[: 3 * layers].reshape(layers, 3, 1, width)
    shifts = norms[3 * layers : 6 * layers].reshape(layers, 3, 1, width)
    size = stream.shape[0]

    def norm_of(l, j):
        return gains[l, j], shifts[l, j]

    records = []
    (((first, proj),), _) = forward(
        [Gather(stream, size, norm_of(0, 0), 0, width, 3 * cols)], ["0a3", "0o1", "0q1", "0k1", "0u1"])
    for l in range(layers):
        n = l + 1
        saved = {"one": stream, "first": first, "proj": proj}
        (((joined, logsum),), _) = forward(
            [attend_self(proj, scale)], [f"{l}o4", f"{l}q4", f"{l}c1"])
        saved.update(joined_self=joined, logsum_self=logsum)
        hand = Gather(None, size, norm_of(l, 1), held[l, "q"], width, cols)
        (((stream,), (second, query)), _) = forward(
            [Scatter(joined, held[l, "self_out"], stream, None, [], hand), hand],
            [f"{l}k4", f"{l}u4", f"{l}c2", f"{l}d1"])
        saved.update(two=stream, second=second, query=query)

        (((joined, logsum, pairs),), _) = forward(
            [attend_cross(query, text_own, held[l, "kv"], scale)], [f"{l}d2", f"{n}k1"])
        saved.update(pairs=pairs, joined_cross=joined, logsum_cross=logsum)
        hand = Gather(None, size, norm_of(l, 2), 0, width, hidden, "gelu")
        more = [send_ride(cotangent[0], "swap")] if n == layers else []
        (((stream,), (third, active, slope)), extra) = forward(
            [Scatter(joined, held[l, "out"], stream, None, [], hand), hand],
            [f"{l}c3", f"{l}d3", f"{n}a1"], more)
        saved.update(three=stream, third=third, active=active, slope=slope)
        records.append(saved)

        if n < layers:
            hand = Gather(None, size, norm_of(n, 0), 0, width, 3 * cols)
            (((stream,), (first, proj)), _) = forward(
                [Scatter(active, held[l, "down"], stream, None, [], hand), hand],
                [f"{n}a4", f"{n}o1", f"{n}q1", f"{n}u1"])
        else:
            grad = reorder(jnp.where(diagonal(), cotangent[0], extra[0]))
            gather = Gather(grad, size, None, held[l, "down"], width, hidden, slope=slope)
            (((stream,), (full, grad_upper)), _) = forward(
                [Scatter(active, held[l, "down"], stream, None, []), gather])
    result_own = reorder(stream.astype(BF16)).astype(BF16)

    folding = []
    finished = {}
    grad_text = jnp.zeros((text_own.shape[0], width), F32)
    norm_grads = {}

    def fold_later(l, name, value, came=None):
        for i, (first, n, order) in enumerate(halves(name)):
            folding.append({"key": (l, name, first), "grad": value.astype(BF16), "first": first,
                            "cols": n, "order": list(reversed(order)),
                            "came": came[i] if came else None, "pair": None})

    def first_sends(name):
        sends = []
        for first, n, order in halves(name):
            axis, weight = order[-1]
            away = runs([k for k in range(blocks) if k & weight])
            sends.append((axis, [(k * part, count * part) for k, count in away], first, n))
        return sends

    def fold_ride(item, phase="all"):
        if phase == "pair":
            return Fold(item["pair"], 0, item["cols"], None, 4, phase=phase)
        sums = ("zl", "zh") if item["key"][1] == "norm" else ()
        return Fold(item["grad"], item["first"], item["cols"], item["order"], blocks,
                    item["came"], sums, phase)

    def first_ride(item):
        name, weight = item["order"][0]
        away = runs([k for k in range(blocks) if k & weight])
        grad, first, n = item["grad"], item["first"], item["cols"]
        out = jax.ShapeDtypeStruct((grad.shape[0] // 2, n), BF16)

        def stages(ins, outs):
            copies, at = [], 0
            for k, count in away:
                copies.append((name, ins[0].at[pl.ds(k * part, count * part), pl.ds(first, n)],
                               outs[0].at[pl.ds(at * part, count * part)]))
                at += count
            return [copies]

        return Ride([grad], [out], stages, [name] * len(away), len(away))

    def folds(parts, begin=(), exchange=(), pair=(), end=(), more=()):
        def of(names):
            return [i for i in folding if i["key"][:2] in names or i["key"] in names]

        begins, exchanges, pairs, ends = of(begin), of(exchange), of(pair), of(end)
        rides = [first_ride(i) for i in begins]
        rides += [fold_ride(i, "exchange") for i in exchanges]
        rides += [fold_ride(i, "pair") for i in pairs]
        rides += [fold_ride(i) for i in ends]
        outs, extra = launch(f"step_{counter[0]}", number(), parts, rides + list(more))
        extra = [e[0] for e in extra]
        for item in begins:
            item["came"] = extra.pop(0)
        for item in exchanges:
            item["pair"] = extra.pop(0)
        for item in pairs + ends:
            finished[item["key"]] = extra.pop(0)
            folding.remove(item)
        return outs, extra

    for l in reversed(range(layers)):
        saved = records[l]
        more = [send_ride(result_own, "swap")] if l == layers - 1 else []
        hand = Gather(None, size, None, held[l, "out"], width, cols)
        fills = [(flat(full), flat(saved["active"]), first_sends("down")),
                 (flat(saved["third"]), None, [])]
        (((grad, norm_grads[l, 2], down, up_, *came), (full, grad_joined)), extra) = folds(
            [Scatter(grad_upper, held[l, "up"], None, (saved["three"], gains[l, 2], grad), fills,
                     hand), hand], exchange=[(l + 1, "self_out"), (l + 1, "self")],
            pair=[(l + 1, "out"), (l + 1, "q"), (l + 1, "kv")], more=more)
        if more:
            result = jnp.where(diagonal(), result_own, extra[0])
        fold_later(l, "down", down, came)
        fold_later(l, "up", up_)

        (((grad_query, kv_, text_part),), _) = folds(
            [attend_cross_back(saved["query"], saved["pairs"], grad_joined,
                               saved["logsum_cross"], text_own, held[l, "kv"], scale)],
            begin=[(l, "up", 0), (l, "up", hidden // 4)], pair=[(l + 1, "self", 0)])
        grad_text = grad_text + text_part
        fold_later(l, "kv", kv_)
        more = [send_ride(grad_text.astype(BF16), "c")] if l == 0 else []
        hand = Gather(None, size, None, held[l, "self_out"], width, cols)
        fills = [(flat(full), flat(saved["joined_cross"]), first_sends("out")),
                 (flat(saved["second"]), None, first_sends("q"))]
        (((grad, norm_grads[l, 1], out_, q_, *came), (full, grad_joined)), extra) = folds(
            [Scatter(grad_query, held[l, "q"], None, (saved["two"], gains[l, 1], grad), fills,
                     hand), hand], begin=[(l, "up", hidden // 2), (l, "up", hidden // 4 * 3)],
            exchange=[(l, "down")], pair=[(l + 1, "self"), (l + 1, "self_out")], more=more)
        fold_later(l, "out", out_, came[:1])
        fold_later(l, "q", q_, came[1:])
        if more:
            grad_text = grad_text.astype(BF16).astype(F32) + extra[0].astype(F32)
            more = [send_ride(grad_text.astype(BF16), "zl")]

        (((grad_proj,),), extra) = folds(
            [attend_self_back(saved["proj"], grad_joined, saved["logsum_self"], scale)],
            begin=[(l, "kv")], exchange=[(l, "up")], pair=[(l, "down")], more=more)
        if more:
            grad_text = grad_text.astype(BF16).astype(F32) + extra[0].astype(F32)
        fills = [(flat(full), flat(saved["joined_self"]), first_sends("self_out")),
                 (flat(saved["first"]), None, first_sends("self"))]
        chain = (saved["one"], gains[l, 0], grad)
        parts = [Scatter(grad_proj, held[l, "self"], None, chain, fills)]
        if l:
            hand = Gather(None, size, None, held[l - 1, "down"], width, hidden,
                          slope=records[l - 1]["slope"])
            parts = [Scatter(grad_proj, held[l, "self"], None, chain, fills, hand), hand]
        (((grad, norm_grads[l, 0], out_, self_, *came), *after), _) = folds(
            parts, pair=[(l, "up")],
            **{"exchange" if l else "end": [(l, "out"), (l, "q"), (l, "kv")]})
        if l:
            ((full, grad_upper),) = after
        fold_later(l, "self_out", out_, came[:1])
        fold_later(l, "self", self_, came[1:])

    small = [norm_grads[l, j][k] for l in range(layers) for k in range(2) for j in range(3)]
    small = jnp.stack(small, axis=1)
    small = jnp.pad(small, ((0, 0), (0, sizes["norm"] - small.shape[1])))
    fold_later(0, "norm", small)
    frames_back = reorder(grad.astype(BF16)).astype(BF16)
    text_back = reorder(grad_text.astype(BF16)).astype(BF16)
    folds_left = [fold_ride(item) for item in folding]
    quick = [i for i, item in enumerate(folding) if item["key"][1] == "norm"]
    extra = move(
        folds_left + [send_ride(frames_back, "swap"), send_ride(text_back, "swap")], quick)
    for item, came in zip(folding, extra):
        finished[item["key"]] = came[0]
    grad_frames, text_sum = [
        jnp.where(diagonal(), mine, came[0]).astype(F32)
        for mine, came in zip((frames_back, text_back), extra[len(folds_left):])
    ]
    small = finished[0, "norm", 0][:, : 6 * layers]
    small = small.T.reshape(layers, 6, part)

    def gradient(l, name):
        pieces = [finished[l, name, first] for first, _, _ in halves(name)]
        return jnp.concatenate(pieces, axis=1) if len(pieces) > 1 else pieces[0]

    def stacked(name, shape=None, turned=False):
        members = [gradient(l, name) for l in range(layers)]
        if turned:
            members = [m.T for m in members]
        if shape is not None:
            members = [m.reshape(shape) for m in members]
        return jnp.stack(members)

    return (
        result[None],
        grad_frames[None],
        text_sum[None],
        small[:, :3],
        small[:, 3:],
        stacked("self", (part, 3, cols)),
        stacked("self_out", turned=True),
        stacked("q"),
        stacked("kv", (part, 2, cols)),
        stacked("out", turned=True),
        stacked("up"),
        stacked("down", turned=True),
    )


def solution(mesh):
    count = mesh.shape["dp"]
    bits = tuple(f"b{i}" for i in range(count.bit_length() - 2))
    dp = (*bits, "c")
    tensor = ("zh", "zl")
    inner = Mesh(mesh.devices.reshape((2,) * (len(bits) + 3)), (*dp, *tensor))
    return jax.shard_map(
        functools.partial(body, bits),
        mesh=inner,
        in_specs=(
            P(dp, tensor, None),
            P(dp, None, None),
            P(None, None, dp),
            P(None, None, dp),
            P(None, dp, None, tensor),
            P(None, tensor, dp),
            P(None, dp, tensor),
            P(None, dp, None, tensor),
            P(None, tensor, dp),
            P(None, dp, tensor),
            P(None, tensor, dp),
            P(dp, tensor, None),
        ),
        out_specs=(
            P(dp, tensor, None),
            P(dp, tensor, None),
            P(dp, None, None),
            P(None, None, dp),
            P(None, None, dp),
            P(None, dp, None, tensor),
            P(None, tensor, dp),
            P(None, dp, tensor),
            P(None, dp, None, tensor),
            P(None, tensor, dp),
            P(None, dp, tensor),
            P(None, tensor, dp),
        ),
        check_vma=False,
    )
```

```python
import functools
import jax
import jax.numpy as jnp
from jax import lax
from jax.experimental import pallas as pl
from jax.experimental.pallas import tpu as pltpu
from jax.sharding import Mesh, PartitionSpec as P

HEAD_DIM = 64
NORM_EPS = 1e-05
MASKED = -1e30
TILE = 384
F32 = jnp.float32
BF16 = jnp.bfloat16
MESH = pl.DeviceIdType.MESH
ANY = pl.BlockSpec(memory_space=pl.ANY)


def nn(a, b):
    return lax.dot_general(a, b, (((1,), (0,)), ((), ())), preferred_element_type=F32)


def nt(a, b):
    return lax.dot_general(a, b, (((1,), (1,)), ((), ())), preferred_element_type=F32)


def tn(a, b):
    return lax.dot_general(a, b, (((0,), (0,)), ((), ())), preferred_element_type=F32)


def flip(value, axis):
    return lax.ppermute(value, axis, [(0, 1), (1, 0)])


def diagonal():
    return lax.axis_index("c") == lax.axis_index("zh")


def off_diagonal():
    return lax.rem(lax.axis_index("c") + lax.axis_index("zh"), 2)


def target(kind):
    c, zh = lax.axis_index("c"), lax.axis_index("zh")
    off = off_diagonal()
    if kind == "ring":
        return {"c": lax.rem(c + off, 2), "zh": lax.rem(zh + 1 + off, 2)}
    if kind == "back":
        return {"c": lax.rem(c + 1 + off, 2), "zh": lax.rem(zh + off, 2)}
    if kind == "swap":
        return {"c": 1 - c, "zh": 1 - zh}
    return {kind: 1 - lax.axis_index(kind)}


def greeted(kinds):
    names = []
    for kind in kinds:
        pairs = {"ring": [("c",), ("zh",)], "back": [("c",), ("zh",)],
                 "swap": [("c", "zh")], "stay": []}.get(kind, [(kind,)])
        names += [p for p in pairs if p not in names]
    return names


def greet(kinds):
    barrier = pltpu.get_barrier_semaphore()
    names = greeted(kinds)
    for group in names:
        pl.semaphore_signal(
            barrier, inc=1, device_id={n: 1 - lax.axis_index(n) for n in group},
            device_id_type=MESH,
        )
    pl.semaphore_wait(barrier, len(names))


class Copy:
    def __init__(self, kind, src, dst, send, recv):
        self.kind = kind
        if kind == "stay":
            self.copy = pltpu.make_async_copy(src, dst, send)
        else:
            self.copy = pltpu.make_async_remote_copy(
                src_ref=src, dst_ref=dst, send_sem=send, recv_sem=recv,
                device_id=target(kind), device_id_type=MESH,
            )

    def guarded(self, act):
        if self.kind == "swap":
            pl.when(off_diagonal() == 1)(act)
        elif self.kind == "stay":
            pl.when(off_diagonal() == 0)(act)
        else:
            act()

    def start(self):
        self.guarded(lambda: self.copy.start())

    def wait(self):
        self.guarded(lambda: self.copy.wait())


class Ride:
    def __init__(self, ins, outs, stages, kinds, count, alias=()):
        self.ins, self.outs, self.stages = list(ins), list(outs), stages
        self.kinds, self.alias = list(kinds), dict(alias)
        self.scratch = [pltpu.SemaphoreType.DMA((count,)), pltpu.SemaphoreType.DMA((count,))]

    def chain(self, ins, outs, refs):
        return Chain(self.stages(ins, outs), *refs)


class Chain:
    def __init__(self, stages, send, recv):
        self.copies, place = [], 0
        for stage in stages:
            self.copies.append([])
            for kind, src, dst in stage:
                self.copies[-1].append(Copy(kind, src, dst, send.at[place], recv.at[place]))
                place += 1
        self.level, self.levels, self.until = 0, len(self.copies), len(self.copies)

    def start(self):
        for copy in self.copies[0]:
            copy.start()

    def step(self):
        for copy in self.copies[self.level]:
            copy.wait()
        self.level += 1
        if self.level < self.levels:
            for copy in self.copies[self.level]:
                copy.start()


class Fold(Ride):
    def __init__(self, grad, first, cols, order, blocks, came=None, sums=(), phase="all"):
        self.phase = phase
        if phase == "pair":
            order, blocks = [(None, 2)], 4
        rows = grad.shape[0] // (2 if phase == "pair" else blocks)
        half = rows * blocks // 2
        self.rows, self.first, self.cols = rows, first, cols
        self.order, self.came, self.sums = order, came, list(sums)
        keys = list(range(blocks))
        self.away0 = [k for k in keys if k & order[0][1]]
        self.held = [k for k in keys if not k & order[0][1]]
        self.ins = [grad] + ([came] if came is not None else [])
        self.outs = [jax.ShapeDtypeStruct((rows, cols), F32)]
        self.alias = {}
        self.kinds = [name for name, _ in order[0 if came is None else 1 :]]
        if phase == "exchange":
            self.outs = [jax.ShapeDtypeStruct((2 * rows, cols), BF16)]
        elif phase == "pair":
            self.kinds = ["swap", "back"]
        else:
            self.kinds += ["swap", "back"] + self.sums
        self.scratch = [pltpu.VMEM((half, cols), BF16), pltpu.VMEM((half, cols), BF16)]
        for level in range(1, len(order)):
            self.scratch.append(pltpu.VMEM((half >> level, cols), BF16))
        self.scratch += [
            pltpu.VMEM((2 * rows, cols), BF16),
            pltpu.VMEM((1 + len(self.sums), rows, cols), F32),
            pltpu.SemaphoreType.DMA((blocks + 2,)),
            pltpu.SemaphoreType.DMA((blocks * 2 + 4,)),
            pltpu.SemaphoreType.DMA((blocks * 2 + 4,)),
        ]
        self.levels = len(order) + (1 if phase == "exchange" else 2 + len(self.sums))
        self.until = {"all": self.levels, "exchange": 1, "pair": 0}[phase]

    def chain(self, ins, outs, refs):
        self.in_refs, self.out = ins, outs[0]
        self.own, self.got = refs[0], list(refs[1 : 1 + len(self.order)])
        self.pair, self.total, self.load, self.send, self.recv = refs[1 + len(self.order) :]
        self.level, self.place, self.live = 0, 0, None
        return self

    def remote(self, kind, src, dst):
        copy = Copy(kind, src, dst, self.send.at[self.place], self.recv.at[self.place])
        self.place += 1
        copy.start()
        return copy

    def block(self, at, count=1):
        return pl.ds(at * self.rows, count * self.rows)

    def start(self):
        cols = pl.ds(self.first, self.cols)
        grad = self.in_refs[0]
        self.live, at = [], 0
        if self.phase == "pair":
            self.level = len(self.order)
            copy = pltpu.make_async_copy(grad, self.own, self.load.at[0])
            copy.start()
            self.live = [copy] + [
                self.remote(kind, grad.at[self.block(k)], self.pair.at[self.block(k)])
                for k, kind in enumerate(("swap", "back"))
            ]
            return
        for i, (k, n) in enumerate(runs(self.held)):
            copy = pltpu.make_async_copy(
                grad.at[self.block(k, n), cols], self.own.at[self.block(at, n)], self.load.at[i])
            copy.start()
            self.live.append(copy)
            at += n
        if self.came is not None:
            copy = pltpu.make_async_copy(self.in_refs[1], self.got[0], self.load.at[len(self.live)])
            copy.start()
            self.live.append(copy)
        else:
            at = 0
            for k, n in runs(self.away0):
                self.live.append(self.remote(
                    self.order[0][0], grad.at[self.block(k, n), cols],
                    self.got[0].at[self.block(at, n)]))
                at += n

    def add(self, got, places):
        def one(i, p):
            value = self.own[self.block(p), :].astype(F32) + got[self.block(i), :].astype(F32)
            self.own[self.block(i), :] = value.astype(BF16)

        for i, p in enumerate(places):
            one(i, p)

    def step(self):
        for copy in self.live:
            copy.wait()
        bits = len(self.order)
        level = self.level
        self.level += 1
        if level < bits:
            if level == 0:
                self.add(self.got[0], range(len(self.held)))
            else:
                self.add(self.got[level], self.stay)
                self.held = [self.held[p] for p in self.stay]
            if level + 1 < bits:
                name, weight = self.order[level + 1]
                self.stay = [p for p, k in enumerate(self.held) if not k & weight]
                away = [p for p, k in enumerate(self.held) if k & weight]
                self.live, at = [], 0
                for p, n in runs(away):
                    self.live.append(self.remote(
                        name, self.own.at[self.block(p, n)],
                        self.got[level + 1].at[self.block(at, n)]))
                    at += n
            elif self.phase == "exchange":
                copy = pltpu.make_async_copy(
                    self.own.at[self.block(0, 2)], self.out, self.load.at[0])
                copy.start()
                self.live = [copy]
            else:
                self.live = [
                    self.remote("swap", self.own.at[self.block(0)], self.pair.at[self.block(0)]),
                    self.remote("back", self.own.at[self.block(1)], self.pair.at[self.block(1)]),
                ]
            return
        if self.phase == "exchange":
            return
        if level == bits:
            def diagonal_sum():
                self.total[0] = (self.own[self.block(0), :].astype(F32)
                                 + self.pair[self.block(1), :].astype(F32))

            def other_sum():
                self.total[0] = (self.pair[self.block(0), :].astype(F32)
                                 + self.pair[self.block(1), :].astype(F32))

            pl.when(off_diagonal() == 0)(diagonal_sum)
            pl.when(off_diagonal() == 1)(other_sum)
        elif level <= bits + len(self.sums):
            self.total[0] = self.total[0] + self.total[level - bits]
        else:
            return
        nth = level - bits
        if nth < len(self.sums):
            self.live = [self.remote(self.sums[nth], self.total.at[0], self.total.at[nth + 1])]
        else:
            copy = pltpu.make_async_copy(self.total.at[0], self.out, self.load.at[0])
            copy.start()
            self.live = [copy]


def runs(keys):
    keys, out = sorted(keys), []
    for k in keys:
        if out and out[-1][0] + out[-1][1] == k:
            out[-1][1] += 1
        else:
            out.append([k, 1])
    return out


def pair_ride(shard, blocks):
    rows, cols = shard.shape
    out = jax.ShapeDtypeStruct((rows * blocks, cols), shard.dtype)

    def stages(ins, outs):
        near, far = outs[0].at[pl.ds(0, rows)], outs[0].at[pl.ds(rows, rows)]
        return [[("ring", ins[0], far), ("swap", ins[0], near), ("stay", ins[0], near)]]

    return Ride([shard], [out], stages, ["ring", "swap"], 3)


def spread_ride(buffer, pieces, levels, blocks):
    rows = buffer.shape[0] // blocks
    plan = []
    for level in levels:
        stage = []
        for first, cols, order in pieces:
            held = [0, 1]
            for name, weight in order[:level]:
                held = held + [k + weight for k in held]
            name, weight = order[level]
            for k, n in runs(held):
                stage.append((name, k, k + weight, n, first, cols))
        plan.append(stage)

    def stages(ins, outs):
        ref = outs[0]
        return [
            [
                (name, ref.at[pl.ds(a * rows, n * rows), pl.ds(first, cols)],
                 ref.at[pl.ds(b * rows, n * rows), pl.ds(first, cols)])
                for name, a, b, n, first, cols in stage
            ]
            for stage in plan
        ]

    kinds = [item[0] for stage in plan for item in stage]
    out = jax.ShapeDtypeStruct(buffer.shape, buffer.dtype)
    return Ride([buffer], [out], stages, kinds, sum(len(s) for s in plan), {0: 0})


def chain_ride(shard, pieces, levels, blocks):
    first = pair_ride(shard, blocks)
    rest = spread_ride(first.outs[0], pieces, levels, blocks)

    def stages(ins, outs):
        return first.stages(ins, outs) + rest.stages(ins, outs)

    count = len(first.kinds) + 1 + len(rest.kinds)
    return Ride([shard], first.outs, stages, first.kinds + rest.kinds, count)


def send_ride(value, kind, after=0):
    out = jax.ShapeDtypeStruct(value.shape, value.dtype)
    return Ride([value], [out], lambda ins, outs: [[]] * after + [[(kind, ins[0], outs[0])]],
                [kind], 1)


class Part:
    ins, outs, scratch, kinds = (), (), (), ()

    def early(self, in_refs, out_refs, refs):
        pass

    def begin(self):
        pass

    def run(self, rides):
        pass

    def settle(self):
        pass


class Rides:
    def __init__(self, chains, outs):
        self.chains, self.outs = chains, outs
        for chain in chains:
            chain.start()

    def advance(self, kind=object):
        for chain in self.chains:
            more = chain.levels - chain.level > 1 and chain.level < chain.until
            if more and isinstance(chain, kind):
                chain.step()

    def finish(self, i):
        while self.chains[i].level < self.chains[i].levels:
            self.chains[i].step()

    def end(self):
        for level in range(max([c.levels for c in self.chains], default=0)):
            for chain in self.chains:
                if chain.level == level and level < chain.levels:
                    chain.step()


def launch(name, number, parts, rides, quick=(), limit=62):
    ins = [x for p in parts for x in p.ins]
    outs = [x for p in parts for x in p.outs]
    in_arrays, out_shapes = list(ins), list(outs)
    aliases, spans = {}, []
    for ride in rides:
        for a, b in ride.alias.items():
            aliases[len(in_arrays) + a] = len(out_shapes) + b
        spans.append((len(in_arrays), len(in_arrays) + len(ride.ins),
                      len(out_shapes), len(out_shapes) + len(ride.outs)))
        in_arrays += ride.ins
        out_shapes += ride.outs
    kinds = [k for p in parts for k in p.kinds] + [k for r in rides for k in r.kinds]
    scratch = [x for p in parts for x in p.scratch]
    parts_scratch = len(scratch)
    scratch += [x for r in rides for x in r.scratch]

    def kernel(*refs):
        in_refs = refs[: len(in_arrays)]
        out_refs = refs[len(in_arrays) : len(in_arrays) + len(out_shapes)]
        rest = refs[len(in_arrays) + len(out_shapes) :]
        i, o, c = 0, 0, 0
        for p in parts:
            p.early(in_refs[i : i + len(p.ins)], out_refs[o : o + len(p.outs)],
                    rest[c : c + len(p.scratch)])
            i, o, c = i + len(p.ins), o + len(p.outs), c + len(p.scratch)
        if kinds:
            greet(kinds)
        chains, at = [], parts_scratch
        for ride, (a, b, c, d) in zip(rides, spans):
            more = len(ride.scratch)
            chains.append(ride.chain(in_refs[a:b], out_refs[c:d], rest[at : at + more]))
            at += more
        under_way = Rides(chains, [out_refs[c] for _, _, c, _ in spans])
        for p in parts:
            p.begin()
        for p in parts:
            p.run(under_way)
        for p in parts:
            p.settle()
        if quick:
            under_way.advance(Fold)
        for i in quick:
            under_way.finish(i)
        under_way.end()

    results = pl.pallas_call(
        kernel,
        out_shape=tuple(out_shapes),
        in_specs=[ANY] * len(in_arrays),
        out_specs=tuple([ANY] * len(out_shapes)),
        scratch_shapes=scratch,
        input_output_aliases=aliases,
        name=name,
        compiler_params=pltpu.CompilerParams(
            collective_id=number if kinds else None,
            has_side_effects=bool(kinds),
            vmem_limit_bytes=limit << 20,
        ),
    )(*in_arrays)
    main_outs, at = [], 0
    for p in parts:
        main_outs.append(results[at : at + len(p.outs)])
        at += len(p.outs)
    return main_outs, [results[c:d] for _, _, c, d in spans]


def normalise_value(rows, gain, shift):
    centre = jnp.mean(rows, axis=-1, keepdims=True)
    centred = rows - centre
    spread = jnp.mean(centred * centred, axis=-1, keepdims=True)
    return (centred * lax.rsqrt(spread + NORM_EPS) * gain + shift).astype(BF16)


def gelu_pair(upper):
    cdf = 0.5 * (1.0 + lax.erf(upper * (0.5**0.5)))
    density = jnp.exp(-0.5 * upper * upper) * (0.5 / jnp.pi) ** 0.5
    return (upper * cdf).astype(BF16), (cdf + upper * density).astype(BF16)


class Gather(Part):
    def __init__(self, rows, size, norm, weight, width, n, ending=None, slope=None):
        self.size, self.width, self.n = size, width, n
        self.has_rows, self.has_norm, self.has_slope = rows is not None, norm is not None, slope is not None
        self.double = ending == "gelu"
        self.filler = lambda: None
        self.ride = weight if isinstance(weight, int) else None
        self.kinds = ["c", "zl"]
        self.ins = []
        if self.has_rows:
            self.ins.append(rows)
        if self.ride is None:
            self.ins.append(weight)
        if self.has_norm:
            self.ins.append(jnp.concatenate([norm[0], norm[1]], axis=0))
        if self.has_slope:
            self.ins.append(slope)
        self.outs = [jax.ShapeDtypeStruct((4, size, width), BF16)]
        self.outs += [jax.ShapeDtypeStruct((4, size, n), BF16)] * (2 if self.double else 1)
        tall = self.double or self.has_slope
        self.scratch = [
            pltpu.VMEM((size, width) if self.has_rows else (8, 128), F32),
            pltpu.VMEM((width, n), BF16),
            pltpu.VMEM((2, width), F32),
            pltpu.VMEM((4, size, width), BF16),
            pltpu.VMEM((4, size, n), BF16),
            pltpu.VMEM((4, size, n) if tall else (1, 16, 128), BF16),
            pltpu.SemaphoreType.DMA((4,)),
            pltpu.SemaphoreType.DMA((6,)),
            pltpu.SemaphoreType.DMA((6,)),
            pltpu.SemaphoreType.DMA((3, 6)),
        ]

    def early(self, in_refs, out_refs, refs):
        self.rows, self.w, self.norms, self.x, self.y, self.second = refs[:6]
        self.load, self.send, self.recv, self.store = refs[6:]
        self.out_refs, self.over, self.rest = out_refs, [], None
        todo, self.loads = list(in_refs), {}
        if self.has_rows:
            self.loads["rows"] = pltpu.make_async_copy(todo.pop(0), self.rows, self.load.at[0])
        if self.ride is None:
            self.loads["w"] = pltpu.make_async_copy(todo.pop(0), self.w, self.load.at[1])
        if self.has_norm:
            self.loads["norm"] = pltpu.make_async_copy(todo.pop(0), self.norms, self.load.at[2])
        if self.has_slope:
            self.loads["slope"] = pltpu.make_async_copy(todo.pop(0), self.second, self.load.at[3])
        for copy in self.loads.values():
            copy.start()

    def send_half(self, h, source):
        half = self.size // 2
        part = pl.ds(h * half, half)
        if h == 0 and self.has_norm:
            self.loads["norm"].wait()
        value = source[part, :]
        if self.has_norm:
            value = normalise_value(value, self.norms[0:1, :], self.norms[1:2, :])
        x = self.x
        x[0, part, :] = value.astype(BF16)
        self.over.append(
            Copy("zl", x.at[0, part], x.at[2, part], self.send.at[h], self.recv.at[h]))
        self.over[-1].start()
        if h == 1:
            self.beside = Copy("c", x.at[0], x.at[1], self.send.at[2], self.recv.at[2])
            self.beside.start()

    def begin(self):
        if self.has_rows:
            self.loads["rows"].wait()
            for h in range(2):
                self.send_half(h, self.rows)

    def near(self, rides):
        x, y, w, second, n = self.x, self.y, self.w, self.second, self.n
        tile, half = min(TILE, n), self.size // 2
        if self.ride is not None:
            rides.finish(self.ride)
            copy = pltpu.make_async_copy(rides.outs[self.ride], w, self.load.at[1])
            copy.start()
            copy.wait()
        else:
            self.loads["w"].wait()
        if self.has_slope:
            self.loads["slope"].wait()
        stores = []

        def multiply(b, rows, slot):
            def step(j, carry):
                cols = pl.ds(pl.multiple_of(j * tile, tile), tile)
                value = nn(x[b, rows, :], w[:, cols])
                if self.double:
                    y[b, rows, cols], second[b, rows, cols] = gelu_pair(value)
                elif self.has_slope:
                    y[b, rows, cols] = (value * second[b, rows, cols].astype(F32)).astype(BF16)
                else:
                    y[b, rows, cols] = value.astype(BF16)
                return carry

            lax.fori_loop(0, n // tile, step, 0)
            for k, ref in enumerate([x, y] + ([second] if self.double else [])):
                stores.append(pltpu.make_async_copy(
                    ref.at[b, rows], self.out_refs[k].at[b, rows], self.store.at[k, slot]))
                stores[-1].start()

        whole = pl.ds(0, self.size)

        multiply(0, whole, 0)
        self.beside.wait()
        multiply(1, whole, 1)
        self.rest = multiply, stores

    def run(self, rides):
        if self.rest is None:
            self.near(rides)
        multiply, stores = self.rest
        x, half = self.x, self.size // 2
        self.filler()
        for h in range(2):
            part = pl.ds(h * half, half)
            self.over[h].wait()
            relay = Copy("c", x.at[2, part], x.at[3, part], self.send.at[3 + h], self.recv.at[3 + h])
            relay.start()
            multiply(2, part, 2 + h)
            relay.wait()
            multiply(3, part, 4 + h)
        for copy in stores:
            copy.wait()


class Scatter(Part):
    def __init__(self, parts, weight, base, norm, fills, hand=None):
        _, size, n = parts.shape
        width = weight.shape[0]
        half = size // 2
        rows = 4 * size
        ins = [parts.reshape(rows, n), weight] + ([base] if base is not None else [])
        if norm is not None:
            ins += list(norm)
        fill_at = len(ins)
        fill_cols = []
        for a, b, _ in fills:
            ins.append(a)
            if b is not None:
                ins.append(b)
            fill_cols.append(n if b is None else b.shape[1])
        outs = [jax.ShapeDtypeStruct((size, width), F32)]
        if norm is not None:
            outs.append(jax.ShapeDtypeStruct((2, width), F32))
        outs += [jax.ShapeDtypeStruct((width, k), BF16) for k in fill_cols]
        sends_at, copies = len(outs), 0
        for _, _, sends in fills:
            for _, rows_away, _, k in sends:
                outs.append(jax.ShapeDtypeStruct((sum(n for _, n in rows_away), k), BF16))
                copies += len(rows_away)
        scratch = [
            pltpu.VMEM((rows, n), BF16),
            pltpu.VMEM((width, n), BF16),
            pltpu.VMEM((size, width), F32),
            pltpu.VMEM((size, width), F32),
            pltpu.VMEM((2, size, width), BF16),
            pltpu.VMEM((2, size, width), BF16),
            pltpu.VMEM((size, width), BF16),
            pltpu.VMEM((size, width), BF16),
            pltpu.SemaphoreType.DMA((8,)),
            pltpu.SemaphoreType.DMA((6,)),
            pltpu.SemaphoreType.DMA((6,)),
        ]
        if norm is not None:
            scratch += [
                pltpu.VMEM((size, width), F32),
                pltpu.VMEM((1, width), F32),
                pltpu.VMEM((size, width), F32),
                pltpu.VMEM((2, width), F32),
                pltpu.SemaphoreType.DMA((4,)),
            ]
        for (a, b, _), k in zip(fills, fill_cols):
            scratch.append(pltpu.VMEM((rows, width), BF16))
            if b is not None:
                scratch.append(pltpu.VMEM((rows, k), BF16))
            scratch += [pltpu.VMEM((width, k), BF16), pltpu.SemaphoreType.DMA((3,))]
        scratch += [pltpu.SemaphoreType.DMA((max(copies, 1),))] * 2
        self.kinds = ["c", "zl"] + [name for _, _, sends in fills for name, _, _, _ in sends]
        self.sends_at = sends_at
        self.middle = lambda rides: None
        self.ins, self.outs, self.scratch = ins, outs, scratch
        self.facts = (size, n, width, half, base, norm, fills, fill_at, fill_cols, outs)
        self.hand = hand

    def early(self, in_refs, out_refs, refs):
        size, n, width, half, base, norm, fills, fill_at, fill_cols, outs = self.facts
        self.out_refs, self.refs = out_refs, refs
        y, w, total, far, give, came, across, over, load, send, recv = refs[:11]
        refs = list(refs[11:])
        if norm is not None:
            stream, gain, back, sums, norm_sem = refs[:5]
            refs = refs[5:]
        loads = [pltpu.make_async_copy(in_refs[1], w, load.at[0])]
        loads += [
            pltpu.make_async_copy(
                in_refs[0].at[pl.ds(b * size, size)], y.at[pl.ds(b * size, size)],
                load.at[1 + b])
            for b in range(4)
        ]
        if base is not None:
            loads.append(pltpu.make_async_copy(in_refs[2], total, load.at[5]))
        for place in (0, 4, 3, 2, 1, 5)[: len(loads)]:
            loads[place].start()
        others = []
        if norm is not None:
            at = 3 if base is not None else 2
            for i, ref in enumerate((stream, gain, back)):
                others.append(pltpu.make_async_copy(in_refs[at + i], ref, norm_sem.at[i]))
        at = fill_at
        for a, b, _ in fills:
            others.append(pltpu.make_async_copy(in_refs[at], refs[0], refs[2 if b is None else 3].at[0]))
            at += 1
            if b is not None:
                others.append(pltpu.make_async_copy(in_refs[at], refs[1], refs[3].at[1]))
                at += 1
            refs = refs[3 if b is None else 4 :]
        for copy in others:
            copy.start()
        self.loads, self.others = loads, others

    def run(self, rides):
        size, n, width, half, base, norm, fills, fill_at, fill_cols, outs = self.facts
        out_refs, refs = self.out_refs, self.refs
        y, w, total, far, give, came, across, over, load, send, recv = refs[:11]
        refs = list(refs[11:])
        if norm is not None:
            stream, gain, back, sums, norm_sem = refs[:5]
            refs = refs[5:]
        loads, others = self.loads, self.others

        def multiply(b, part, count, put):
            def step(j, carry):
                cols = pl.ds(pl.multiple_of(j * TILE, TILE), TILE)
                put(cols, nt(y[pl.ds(b * size + part, count), :], w[cols, :]))
                return carry

            lax.fori_loop(0, width // TILE, step, 0)

        for place in (0, 4, 3):
            loads[place].wait()
        sent = []
        for h in range(2):
            part = pl.ds(h * half, half)

            def put_give(cols, value, part=part):
                give[0, part, cols] = value.astype(BF16)

            def put_far(cols, value, part=part):
                far[part, cols] = value

            multiply(3, h * half, half, put_give)
            copy = Copy("c", give.at[0, part], came.at[0, part], send.at[h], recv.at[h])
            copy.start()
            multiply(2, h * half, half, put_far)
            copy.wait()
            across[part, :] = (far[part, :] + came[0, part, :].astype(F32)).astype(BF16)
            copy = Copy("zl", across.at[part], over.at[part], send.at[2 + h], recv.at[2 + h])
            copy.start()
            sent.append(copy)
        rides.advance(Fold)
        loads[2].wait()

        def put_near(cols, value):
            give[1, :, cols] = value.astype(BF16)

        multiply(1, 0, size, put_near)
        near = Copy("c", give.at[1], came.at[1], send.at[4], recv.at[4])
        near.start()
        loads[1].wait()
        if base is not None:
            loads[5].wait()

        def put_total(cols, value):
            total[:, cols] = value + (total[:, cols] if base is not None else 0.0)

        multiply(0, 0, size, put_total)
        for copy in others:
            copy.wait()
        stores, fill_refs, refs_all = [], refs, self.refs
        slot = [self.sends_at, 0]

        def fill(k, left, right, result, sem):
            count = fill_cols[k]
            wide = 768 if count % 768 == 0 else count

            def step(j, carry):
                rows_ = pl.ds(pl.multiple_of(j * 256, 256), 256)
                turned = left[:, rows_].T
                for q in range(count // wide):
                    cols = slice(q * wide, (q + 1) * wide)
                    result[rows_, cols] = nn(turned, right[:, cols]).astype(BF16)
                return carry

            lax.fori_loop(0, width // 256, step, 0)
            where = self.sends_at - len(fills) + k
            stores.append(pltpu.make_async_copy(result, out_refs[where], sem.at[2]))
            stores[-1].start()
            for name, rows_away, first, cols in fills[k][2]:
                at = 0
                for row, count in rows_away:
                    copy = Copy(name, result.at[pl.ds(row, count), pl.ds(first, cols)],
                                out_refs[slot[0]].at[pl.ds(at, count)],
                                refs_all[-2].at[slot[1]], refs_all[-1].at[slot[1]])
                    copy.start()
                    stores.append(copy)
                    at += count
                    slot[1] += 1
                slot[0] += 1

        for k, (a, b, _) in enumerate(fills):
            if b is None:
                left, result, sem = fill_refs[:3]
                right, fill_refs = y, fill_refs[3:]
            else:
                left, right, result, sem = fill_refs[:4]
                fill_refs = fill_refs[4:]
            job = functools.partial(fill, k, left, right, result, sem)
            if self.hand is not None and k == len(fills) - 1 and not fills[k][2]:
                self.hand.filler = job
            else:
                job()
        self.middle(rides)
        rides.advance()
        near.wait()
        total[...] += came[1].astype(F32)
        for h in range(2):
            part = pl.ds(h * half, half)
            sent[h].wait()
            total[part, :] += over[part, :].astype(F32)
            if norm is not None:
                value = total[part, :]
                rows_in = stream[part, :]
                centred = rows_in - jnp.mean(rows_in, axis=-1, keepdims=True)
                inverse = lax.rsqrt(jnp.mean(centred * centred, axis=-1, keepdims=True) + NORM_EPS)
                unit = centred * inverse
                gain_sum = jnp.sum(value * unit, axis=0, keepdims=True)
                shift_sum = jnp.sum(value, axis=0, keepdims=True)
                sums[0:1, :] = gain_sum if h == 0 else sums[0:1, :] + gain_sum
                sums[1:2, :] = shift_sum if h == 0 else sums[1:2, :] + shift_sum
                scaled = value * gain[...]
                total[part, :] = back[part, :] + inverse * (
                    scaled
                    - jnp.mean(scaled, axis=-1, keepdims=True)
                    - unit * jnp.mean(scaled * unit, axis=-1, keepdims=True)
                )
            if self.hand is not None:
                self.hand.send_half(h, total)
            copy = pltpu.make_async_copy(total.at[part], out_refs[0].at[part], load.at[6 + h])
            copy.start()
            stores.append(copy)
        if norm is not None:
            copy = pltpu.make_async_copy(sums, out_refs[1], norm_sem.at[3])
            copy.start()
            stores.append(copy)
        self.stores = stores

    def settle(self):
        for copy in self.stores:
            copy.wait()


def place_of(i):
    c, zl = lax.axis_index("c"), lax.axis_index("zl")
    dc, dz = i // 2, i % 2
    return (c + dc) % 2 + 2 * ((zl + dz) % 2)


def head_only(value, u):
    lane = lax.broadcasted_iota(jnp.int32, value.shape, 1)
    keep = (lane < HEAD_DIM) if u == 0 else (lane >= HEAD_DIM)
    return jnp.where(keep, value, jnp.zeros_like(value))


def masked(scores):
    key = lax.broadcasted_iota(jnp.int32, scores.shape, 0)
    query = lax.broadcasted_iota(jnp.int32, scores.shape, 1)
    return jnp.where(key <= query, scores, MASKED)


def softmax_parts(parts, value_rows):
    top = parts[0].max(axis=0, keepdims=True)
    for scores in parts[1:]:
        top = jnp.maximum(top, scores.max(axis=0, keepdims=True))
    total, mixed = 0.0, 0.0
    for scores, values in zip(parts, value_rows):
        expo = jnp.exp(scores - top)
        total = total + expo.sum(axis=0, keepdims=True)
        mixed = mixed + nn(values, expo.astype(BF16))
    return mixed / total, top + jnp.log(total)


def softmax_back(scores, slopes, logsum):
    probs = [jnp.exp(s - logsum) for s in scores]
    inner = 0.0
    for p, d in zip(probs, slopes):
        inner = inner + (p * d).sum(axis=0, keepdims=True)
    return [p.astype(BF16) for p in probs], [
        (p * (d - inner)).astype(BF16) for p, d in zip(probs, slopes)
    ]


class Local(Part):
    def __init__(self, ins, outs, scratch, main):
        self.ins, self.outs, self.scratch, self.main = ins, outs, scratch, main

    def early(self, in_refs, out_refs, refs):
        self.refs = (in_refs, out_refs, refs)
        self.stage = self.main(in_refs, out_refs, refs, True)

    def run(self, rides):
        self.main(*self.refs, self.stage, rides)


def attend_self(proj, scale):
    _, size, wide = proj.shape
    cols = wide // 3
    frames, heads = 4 * size, cols // HEAD_DIM
    outs = [jax.ShapeDtypeStruct((4, size, cols), BF16), jax.ShapeDtypeStruct((heads, frames), F32)]
    scratch = [
        pltpu.VMEM((4, size, wide), BF16),
        pltpu.VMEM((frames, 128), BF16),
        pltpu.VMEM((128, frames), BF16),
        pltpu.VMEM((4, size, cols), BF16),
        pltpu.VMEM((heads, frames), F32),
        pltpu.SemaphoreType.DMA((3,)),
    ]

    def main(in_refs, out_refs, refs, stage, rides=None):
        x, keys, values, out, logs, sem = refs
        if stage is True:
            copy = pltpu.make_async_copy(in_refs[0], x, sem.at[0])
            copy.start()
            return copy
        stage.wait()
        for g in range(cols // 128):
            if g:
                rides.advance()
            lanes = [pl.ds(part * cols + g * 128, 128) for part in range(3)]
            for i in range(4):
                rows = pl.ds(i * size, size)
                keys[rows, :] = x[place_of(i), :, lanes[1]]
                values[:, rows] = x[place_of(i), :, lanes[2]].T
            for i in range(4):
                query = x[place_of(i), :, lanes[0]]
                before = i * size
                done = []
                for u in range(2):
                    q = head_only(query, u)
                    mine = pl.ds(u * HEAD_DIM, HEAD_DIM)
                    parts = [masked(nt(keys[pl.ds(before, size), :], q) * scale)]
                    rows = [values[mine, pl.ds(before, size)]]
                    if i:
                        parts.append(nt(keys[pl.ds(0, before), :], q) * scale)
                        rows.append(values[mine, pl.ds(0, before)])
                    mixed, logsum = softmax_parts(parts, rows)
                    done.append(mixed)
                    logs[pl.ds(2 * g + u, 1), pl.ds(before, size)] = logsum
                joined = jnp.concatenate(done, axis=0).T
                out[place_of(i), :, pl.ds(g * 128, 128)] = joined.astype(BF16)
        copies = [pltpu.make_async_copy(out, out_refs[0], sem.at[1]),
                  pltpu.make_async_copy(logs, out_refs[1], sem.at[2])]
        for copy in copies:
            copy.start()
        for copy in copies:
            copy.wait()

    return Local([proj], outs, scratch, main)


def attend_self_back(proj, grad_joined, logsum, scale):
    _, size, wide = proj.shape
    cols = wide // 3
    frames, heads = 4 * size, cols // HEAD_DIM
    outs = [jax.ShapeDtypeStruct((4, size, wide), BF16)]
    scratch = [
        pltpu.VMEM((4, size, wide), BF16),
        pltpu.VMEM((4, size, cols), BF16),
        pltpu.VMEM((heads, frames), F32),
        pltpu.VMEM((frames, 128), BF16),
        pltpu.VMEM((128, frames), BF16),
        pltpu.VMEM((frames, 128), BF16),
        pltpu.VMEM((frames, 128), F32),
        pltpu.VMEM((frames, 128), F32),
        pltpu.VMEM((4, size, wide), BF16),
        pltpu.SemaphoreType.DMA((4,)),
    ]

    def main(in_refs, out_refs, refs, stage, rides=None):
        x, grads, logs, keys, keys_t, values, grad_k, grad_v, out, sem = refs
        if stage is True:
            copies = [
                pltpu.make_async_copy(in_refs[i], ref, sem.at[i])
                for i, ref in enumerate((x, grads, logs))
            ]
            for copy in copies:
                copy.start()
            return copies
        for copy in stage:
            copy.wait()
        for g in range(cols // 128):
            if g < 2:
                rides.advance(Fold)
            lanes = [pl.ds(part * cols + g * 128, 128) for part in range(3)]
            for i in range(4):
                rows = pl.ds(i * size, size)
                keys[rows, :] = x[place_of(i), :, lanes[1]]
                keys_t[:, rows] = x[place_of(i), :, lanes[1]].T
                values[rows, :] = x[place_of(i), :, lanes[2]]
            grad_k[...] = jnp.zeros_like(grad_k)
            grad_v[...] = jnp.zeros_like(grad_v)
            for i in range(4):
                query = x[place_of(i), :, lanes[0]]
                grad = grads[place_of(i), :, lanes[0]]
                before = i * size
                spans = [pl.ds(before, size)] + ([pl.ds(0, before)] if i else [])
                done = []
                for u in range(2):
                    q, go = head_only(query, u), head_only(grad, u)
                    mine = pl.ds(u * HEAD_DIM, HEAD_DIM)
                    scores = [nt(keys[span, :], q) * scale for span in spans]
                    scores[0] = masked(scores[0])
                    slopes = [nt(values[span, :], go) for span in spans]
                    probs, grad_scores = softmax_back(
                        scores, slopes, logs[pl.ds(2 * g + u, 1), pl.ds(before, size)])
                    grad_q = 0.0
                    for span, p, d in zip(spans, probs, grad_scores):
                        grad_v[span, :] += nn(p, go)
                        grad_k[span, :] += nn(d, q)
                        grad_q = grad_q + nn(keys_t[mine, span], d)
                    done.append(grad_q)
                grad_q = jnp.concatenate(done, axis=0).T * scale
                out[place_of(i), :, lanes[0]] = grad_q.astype(BF16)
            for i in range(4):
                rows = pl.ds(i * size, size)
                out[place_of(i), :, lanes[1]] = (grad_k[rows, :] * scale).astype(BF16)
                out[place_of(i), :, lanes[2]] = grad_v[rows, :].astype(BF16)
        copy = pltpu.make_async_copy(out, out_refs[0], sem.at[3])
        copy.start()
        copy.wait()

    return Local([proj, grad_joined, logsum], outs, scratch, main)


def attend_cross(query, text, weight, scale):
    _, size, cols = query.shape
    frames, heads = 4 * size, cols // HEAD_DIM
    states, width = text.shape
    outs = [jax.ShapeDtypeStruct((4, size, cols), BF16), jax.ShapeDtypeStruct((heads, frames), F32),
            jax.ShapeDtypeStruct((states, 2 * cols), BF16)]
    scratch = [
        pltpu.VMEM((4, size, cols), BF16),
        pltpu.VMEM((states, 2 * cols), BF16),
        pltpu.VMEM((4, size, cols), BF16),
        pltpu.VMEM((heads, frames), F32),
        pltpu.VMEM((states, width), BF16),
        pltpu.VMEM((width, 2 * cols), BF16),
        pltpu.SemaphoreType.DMA((6,)),
    ]

    def main(in_refs, out_refs, refs, stage, rides=None):
        x, kv, out, logs, states_in, w, sem = refs
        if stage is True:
            copies = [
                pltpu.make_async_copy(in_refs[i], ref, sem.at[i])
                for i, ref in enumerate((x, states_in, w))
            ]
            for copy in copies:
                copy.start()
            return copies
        for copy in stage:
            copy.wait()
        kv[...] = nn(states_in[...], w[...]).astype(BF16)
        for g in range(cols // 128):
            lanes = pl.ds(g * 128, 128)
            keys = kv[:, lanes]
            values = kv[:, pl.ds(cols + g * 128, 128)].T
            for i in range(4):
                rows = x[i, :, lanes]
                done = []
                for u in range(2):
                    scores = nt(keys, head_only(rows, u)) * scale
                    mixed, logsum = softmax_parts(
                        [scores], [values[u * HEAD_DIM : (u + 1) * HEAD_DIM, :]])
                    done.append(mixed)
                    logs[pl.ds(2 * g + u, 1), pl.ds(i * size, size)] = logsum
                out[i, :, lanes] = jnp.concatenate(done, axis=0).T.astype(BF16)
        copies = [
            pltpu.make_async_copy(ref, out_refs[i], sem.at[3 + i])
            for i, ref in enumerate((out, logs, kv))
        ]
        for copy in copies:
            copy.start()
        for copy in copies:
            copy.wait()

    return Local([query, text, weight], outs, scratch, main)


def attend_cross_back(query, pairs, grad_joined, logsum, text, weight, scale):
    _, size, cols = query.shape
    frames, heads = 4 * size, cols // HEAD_DIM
    states, width = text.shape
    outs = [jax.ShapeDtypeStruct((4, size, cols), BF16),
            jax.ShapeDtypeStruct((width, 2 * cols), BF16),
            jax.ShapeDtypeStruct((states, width), F32)]
    scratch = [
        pltpu.VMEM((4, size, cols), BF16),
        pltpu.VMEM((states, 2 * cols), BF16),
        pltpu.VMEM((4, size, cols), BF16),
        pltpu.VMEM((heads, frames), F32),
        pltpu.VMEM((states, width), BF16),
        pltpu.VMEM((width, 2 * cols), BF16),
        pltpu.VMEM((4, size, cols), BF16),
        pltpu.VMEM((states, 2 * cols), BF16),
        pltpu.VMEM((width, 2 * cols), BF16),
        pltpu.VMEM((states, width), F32),
        pltpu.SemaphoreType.DMA((9,)),
    ]

    def main(in_refs, out_refs, refs, stage, rides=None):
        x, kv, grads, logs, states_in, w, out, out_kv, out_w, out_text, sem = refs
        if stage is True:
            copies = [
                pltpu.make_async_copy(in_refs[i], ref, sem.at[i])
                for i, ref in enumerate((x, kv, grads, logs, states_in, w))
            ]
            for copy in copies:
                copy.start()
            return copies
        for copy in stage:
            copy.wait()
        for g in range(cols // 128):
            if g:
                rides.advance()
            lanes, lanes_v = pl.ds(g * 128, 128), pl.ds(cols + g * 128, 128)
            keys, values = kv[:, lanes], kv[:, lanes_v]
            keys_t = keys.T
            grad_k, grad_v = 0.0, 0.0
            for i in range(4):
                done = []
                for u in range(2):
                    q, go = head_only(x[i, :, lanes], u), head_only(grads[i, :, lanes], u)
                    scores = nt(keys, q) * scale
                    probs, grad_scores = softmax_back(
                        [scores], [nt(values, go)],
                        logs[pl.ds(2 * g + u, 1), pl.ds(i * size, size)])
                    grad_v = grad_v + nn(probs[0], go)
                    grad_k = grad_k + nn(grad_scores[0], q)
                    done.append(nn(keys_t[u * HEAD_DIM : (u + 1) * HEAD_DIM, :], grad_scores[0]))
                out[i, :, lanes] = (jnp.concatenate(done, axis=0).T * scale).astype(BF16)
            out_kv[:, lanes] = (grad_k * scale).astype(BF16)
            out_kv[:, lanes_v] = grad_v.astype(BF16)
        grad_pairs = out_kv[...]
        out_w[...] = nn(states_in[...].T, grad_pairs).astype(BF16)
        out_text[...] = nt(grad_pairs, w[...])
        copies = [
            pltpu.make_async_copy(ref, out_refs[i], sem.at[6 + i])
            for i, ref in enumerate((out, out_w, out_text))
        ]
        for copy in copies:
            copy.start()
        for copy in copies:
            copy.wait()

    return Local([query, pairs, grad_joined, logsum, text, weight], outs, scratch, main)


def flat(parts):
    return parts.reshape(-1, parts.shape[-1])


def body(bits, frames_in, text_states, ln_gain, ln_bias, w_self, w_self_out, w_cross_q,
         w_cross_kv, w_cross_out, w_up, w_down, cotangent):
    scale = float(HEAD_DIM) ** (-0.5)
    layers = w_self.shape[0]
    width = frames_in.shape[2]
    part = w_self.shape[1]
    blocks = width // part
    cols = w_self.shape[3]
    hidden = w_up.shape[2]
    me = lax.axis_index("zh")
    for place, name in enumerate(reversed(bits)):
        me = me + (lax.axis_index(name) << (place + 1))

    row = lax.broadcasted_iota(jnp.int32, (width, width), 0)
    col = lax.broadcasted_iota(jnp.int32, (width, width), 1)
    permute = ((row // part == ((col // part) ^ me)) & (row % part == col % part)).astype(BF16)
    permute = lax.optimization_barrier(permute)

    def reorder(value):
        return nn(value, permute)

    up = [(name, 2 << (len(bits) - 1 - place)) for place, name in enumerate(bits)]
    low_first = list(reversed(up))
    levels = len(bits)
    early, late = list(range(levels // 2)), list(range(levels // 2, levels))
    sizes = {"self": 3 * cols, "self_out": cols, "q": cols, "kv": 2 * cols, "out": cols,
             "up": hidden, "down": hidden, "norm": 128}

    def halves(name):
        n = sizes[name]
        if name == "up":
            return [(i * n // 4, n // 4, up if i % 2 else low_first) for i in range(4)]
        if name in ("self", "kv", "down"):
            first = (n // 2 + 127) // 128 * 128
            return [(0, first, low_first), (first, n - first, up)]
        return [(0, n, low_first if name in ("q", "norm") else up)]

    packs = {"a": "self", "o": "self_out", "q": "q", "k": "kv", "u": "out", "c": "up", "d": "down"}
    norm_rows = jnp.concatenate([ln_gain.reshape(-1, part), ln_bias.reshape(-1, part)], axis=0).T
    norm_rows = jnp.pad(norm_rows, ((0, 0), (0, sizes["norm"] - norm_rows.shape[1])))
    shards = {}
    for l in range(layers):
        shards[l, "self"] = w_self[l].reshape(part, 3 * cols)
        shards[l, "self_out"] = w_self_out[l].T
        shards[l, "q"] = w_cross_q[l]
        shards[l, "kv"] = w_cross_kv[l].reshape(part, 2 * cols)
        shards[l, "out"] = w_cross_out[l].T
        shards[l, "up"] = w_up[l]
        shards[l, "down"] = w_down[l].T
    held = {}
    counter = [0]

    def number():
        counter[0] += 1
        return counter[0] - 1

    def forward(parts, todo=(), more=()):
        rides, keys = [], []
        for word in todo:
            l, name, stage = int(word[0]), packs[word[1]], int(word[2])
            if l >= layers:
                continue
            if stage == 1:
                rides.append(pair_ride(shards[l, name], blocks))
            else:
                which = {2: early, 3: late, 4: early + late}[stage]
                rides.append(spread_ride(held[l, name], halves(name), which, blocks))
            keys.append((l, name))
        outs, extra = launch(f"step_{counter[0]}", number(), parts, rides + list(more))
        for key, value in zip(keys, extra):
            held[key] = value[0]
        return outs, [e[0] for e in extra[len(keys):]]

    def move(rides, quick=()):
        return launch(f"move_{counter[0]}", number(), [], rides, quick)[1]

    extra = move([
        chain_ride(shards[0, "self"], halves("self"), early, blocks),
        chain_ride(norm_rows, halves("norm"), early + late, blocks),
        send_ride(text_states[0], "c"),
        send_ride(frames_in[0], "swap", 1),
    ])
    held[0, "self"], norms, text_far, frames_far = [e[0] for e in extra]
    stream = reorder(jnp.where(diagonal(), frames_in[0], frames_far))
    text_own = reorder(jnp.where(diagonal(), text_states[0], text_far)).astype(BF16)
    norms = norms.astype(F32).T
    gains = norms[: 3 * layers].reshape(layers, 3, 1, width)
    shifts = norms[3 * layers : 6 * layers].reshape(layers, 3, 1, width)
    size = stream.shape[0]

    def norm_of(l, j):
        return gains[l, j], shifts[l, j]

    records = []
    (((first, proj),), _) = forward(
        [Gather(stream, size, norm_of(0, 0), 0, width, 3 * cols)], ["0a3", "0o1", "0q1", "0k1", "0u1"])
    for l in range(layers):
        n = l + 1
        saved = {"one": stream, "first": first, "proj": proj}
        (((joined, logsum),), _) = forward(
            [attend_self(proj, scale)], [f"{l}o4", f"{l}q4", f"{l}c1"])
        saved.update(joined_self=joined, logsum_self=logsum)
        hand = Gather(None, size, norm_of(l, 1), held[l, "q"], width, cols)
        (((stream,), (second, query)), _) = forward(
            [Scatter(joined, held[l, "self_out"], stream, None, [], hand), hand],
            [f"{l}k4", f"{l}u4", f"{l}c2", f"{l}d1"])
        saved.update(two=stream, second=second, query=query)

        (((joined, logsum, pairs),), _) = forward(
            [attend_cross(query, text_own, held[l, "kv"], scale)], [f"{l}d2", f"{n}k1"])
        saved.update(pairs=pairs, joined_cross=joined, logsum_cross=logsum)
        hand = Gather(None, size, norm_of(l, 2), 0, width, hidden, "gelu")
        more = [send_ride(cotangent[0], "swap")] if n == layers else []
        (((stream,), (third, active, slope)), extra) = forward(
            [Scatter(joined, held[l, "out"], stream, None, [], hand), hand],
            [f"{l}c3", f"{l}d3", f"{n}a1"], more)
        saved.update(three=stream, third=third, active=active, slope=slope)
        records.append(saved)

        if n < layers:
            hand = Gather(None, size, norm_of(n, 0), 0, width, 3 * cols)
            (((stream,), (first, proj)), _) = forward(
                [Scatter(active, held[l, "down"], stream, None, [], hand), hand],
                [f"{n}a4", f"{n}o1", f"{n}q1", f"{n}u1"])
        else:
            grad = reorder(jnp.where(diagonal(), cotangent[0], extra[0]))
            gather = Gather(grad, size, None, held[l, "down"], width, hidden, slope=slope)
            scatter = Scatter(active, held[l, "down"], stream, None, [])
            scatter.middle = gather.near
            (((stream,), (full, grad_upper)), _) = forward([scatter, gather])
    result_own = reorder(stream.astype(BF16)).astype(BF16)

    folding = []
    finished = {}
    grad_text = jnp.zeros((text_own.shape[0], width), F32)
    norm_grads = {}

    def fold_later(l, name, value, came=None):
        for i, (first, n, order) in enumerate(halves(name)):
            folding.append({"key": (l, name, first), "grad": value.astype(BF16), "first": first,
                            "cols": n, "order": list(reversed(order)),
                            "came": came[i] if came else None, "pair": None})

    def first_sends(name):
        sends = []
        for first, n, order in halves(name):
            axis, weight = order[-1]
            away = runs([k for k in range(blocks) if k & weight])
            sends.append((axis, [(k * part, count * part) for k, count in away], first, n))
        return sends

    def fold_ride(item, phase="all"):
        if phase == "pair":
            return Fold(item["pair"], 0, item["cols"], None, 4, phase=phase)
        sums = ("zl", "zh") if item["key"][1] == "norm" else ()
        return Fold(item["grad"], item["first"], item["cols"], item["order"], blocks,
                    item["came"], sums, phase)

    def first_ride(item):
        name, weight = item["order"][0]
        away = runs([k for k in range(blocks) if k & weight])
        grad, first, n = item["grad"], item["first"], item["cols"]
        out = jax.ShapeDtypeStruct((grad.shape[0] // 2, n), BF16)

        def stages(ins, outs):
            copies, at = [], 0
            for k, count in away:
                copies.append((name, ins[0].at[pl.ds(k * part, count * part), pl.ds(first, n)],
                               outs[0].at[pl.ds(at * part, count * part)]))
                at += count
            return [copies]

        return Ride([grad], [out], stages, [name] * len(away), len(away))

    def folds(parts, begin=(), exchange=(), pair=(), end=(), more=()):
        def of(names):
            return [i for i in folding if i["key"][:2] in names or i["key"] in names]

        begins, exchanges, pairs, ends = of(begin), of(exchange), of(pair), of(end)
        rides = [first_ride(i) for i in begins]
        rides += [fold_ride(i, "exchange") for i in exchanges]
        rides += [fold_ride(i, "pair") for i in pairs]
        rides += [fold_ride(i) for i in ends]
        outs, extra = launch(f"step_{counter[0]}", number(), parts, rides + list(more))
        extra = [e[0] for e in extra]
        for item in begins:
            item["came"] = extra.pop(0)
        for item in exchanges:
            item["pair"] = extra.pop(0)
        for item in pairs + ends:
            finished[item["key"]] = extra.pop(0)
            folding.remove(item)
        return outs, extra

    for l in reversed(range(layers)):
        saved = records[l]
        more = [send_ride(result_own, "swap")] if l == layers - 1 else []
        hand = Gather(None, size, None, held[l, "out"], width, cols)
        fills = [(flat(full), flat(saved["active"]), first_sends("down")),
                 (flat(saved["third"]), None, [])]
        (((grad, norm_grads[l, 2], down, up_, *came), (full, grad_joined)), extra) = folds(
            [Scatter(grad_upper, held[l, "up"], None, (saved["three"], gains[l, 2], grad), fills,
                     hand), hand], exchange=[(l + 1, "self_out"), (l + 1, "self")],
            pair=[(l + 1, "out"), (l + 1, "q"), (l + 1, "kv")], more=more)
        if more:
            result = jnp.where(diagonal(), result_own, extra[0])
        fold_later(l, "down", down, came)
        fold_later(l, "up", up_)

        (((grad_query, kv_, text_part),), _) = folds(
            [attend_cross_back(saved["query"], saved["pairs"], grad_joined,
                               saved["logsum_cross"], text_own, held[l, "kv"], scale)],
            begin=[(l, "up", 0), (l, "up", hidden // 4)], pair=[(l + 1, "self", 0)])
        grad_text = grad_text + text_part
        fold_later(l, "kv", kv_)
        more = [send_ride(grad_text.astype(BF16), "c")] if l == 0 else []
        hand = Gather(None, size, None, held[l, "self_out"], width, cols)
        fills = [(flat(full), flat(saved["joined_cross"]), first_sends("out")),
                 (flat(saved["second"]), None, first_sends("q"))]
        (((grad, norm_grads[l, 1], out_, q_, *came), (full, grad_joined)), extra) = folds(
            [Scatter(grad_query, held[l, "q"], None, (saved["two"], gains[l, 1], grad), fills,
                     hand), hand], begin=[(l, "up", hidden // 2), (l, "up", hidden // 4 * 3)],
            exchange=[(l, "down")], pair=[(l + 1, "self"), (l + 1, "self_out")], more=more)
        fold_later(l, "out", out_, came[:1])
        fold_later(l, "q", q_, came[1:])
        if more:
            grad_text = grad_text.astype(BF16).astype(F32) + extra[0].astype(F32)
            more = [send_ride(grad_text.astype(BF16), "zl")]

        (((grad_proj,),), extra) = folds(
            [attend_self_back(saved["proj"], grad_joined, saved["logsum_self"], scale)],
            begin=[(l, "kv")], exchange=[(l, "up")], pair=[(l, "down")], more=more)
        if more:
            grad_text = grad_text.astype(BF16).astype(F32) + extra[0].astype(F32)
        fills = [(flat(full), flat(saved["joined_self"]), first_sends("self_out")),
                 (flat(saved["first"]), None, first_sends("self"))]
        chain = (saved["one"], gains[l, 0], grad)
        parts = [Scatter(grad_proj, held[l, "self"], None, chain, fills)]
        if l:
            hand = Gather(None, size, None, held[l - 1, "down"], width, hidden,
                          slope=records[l - 1]["slope"])
            parts = [Scatter(grad_proj, held[l, "self"], None, chain, fills, hand), hand]
        (((grad, norm_grads[l, 0], out_, self_, *came), *after), _) = folds(
            parts, pair=[(l, "up")],
            **{"exchange" if l else "end": [(l, "out"), (l, "q"), (l, "kv")]})
        if l:
            ((full, grad_upper),) = after
        fold_later(l, "self_out", out_, came[:1])
        fold_later(l, "self", self_, came[1:])

    small = [norm_grads[l, j][k] for l in range(layers) for k in range(2) for j in range(3)]
    small = jnp.stack(small, axis=1)
    small = jnp.pad(small, ((0, 0), (0, sizes["norm"] - small.shape[1])))
    fold_later(0, "norm", small)
    frames_back = reorder(grad.astype(BF16)).astype(BF16)
    text_back = reorder(grad_text.astype(BF16)).astype(BF16)
    folds_left = [fold_ride(item) for item in folding]
    quick = [i for i, item in enumerate(folding) if item["key"][1] == "norm"]
    extra = move(
        folds_left + [send_ride(frames_back, "swap"), send_ride(text_back, "swap")], quick)
    for item, came in zip(folding, extra):
        finished[item["key"]] = came[0]
    grad_frames, text_sum = [
        jnp.where(diagonal(), mine, came[0]).astype(F32)
        for mine, came in zip((frames_back, text_back), extra[len(folds_left):])
    ]
    small = finished[0, "norm", 0][:, : 6 * layers]
    small = small.T.reshape(layers, 6, part)

    def gradient(l, name):
        pieces = [finished[l, name, first] for first, _, _ in halves(name)]
        return jnp.concatenate(pieces, axis=1) if len(pieces) > 1 else pieces[0]

    def stacked(name, shape=None, turned=False):
        members = [gradient(l, name) for l in range(layers)]
        if turned:
            members = [m.T for m in members]
        if shape is not None:
            members = [m.reshape(shape) for m in members]
        return jnp.stack(members)

    return (
        result[None],
        grad_frames[None],
        text_sum[None],
        small[:, :3],
        small[:, 3:],
        stacked("self", (part, 3, cols)),
        stacked("self_out", turned=True),
        stacked("q"),
        stacked("kv", (part, 2, cols)),
        stacked("out", turned=True),
        stacked("up"),
        stacked("down", turned=True),
    )


def solution(mesh):
    count = mesh.shape["dp"]
    bits = tuple(f"b{i}" for i in range(count.bit_length() - 2))
    dp = (*bits, "c")
    tensor = ("zh", "zl")
    inner = Mesh(mesh.devices.reshape((2,) * (len(bits) + 3)), (*dp, *tensor))
    return jax.shard_map(
        functools.partial(body, bits),
        mesh=inner,
        in_specs=(
            P(dp, tensor, None),
            P(dp, None, None),
            P(None, None, dp),
            P(None, None, dp),
            P(None, dp, None, tensor),
            P(None, tensor, dp),
            P(None, dp, tensor),
            P(None, dp, None, tensor),
            P(None, tensor, dp),
            P(None, dp, tensor),
            P(None, tensor, dp),
            P(dp, tensor, None),
        ),
        out_specs=(
            P(dp, tensor, None),
            P(dp, tensor, None),
            P(dp, None, None),
            P(None, None, dp),
            P(None, None, dp),
            P(None, dp, None, tensor),
            P(None, tensor, dp),
            P(None, dp, tensor),
            P(None, dp, None, tensor),
            P(None, tensor, dp),
            P(None, dp, tensor),
            P(None, tensor, dp),
        ),
        check_vma=False,
    )
```
